32 devices in a mesh: groups: 2 (over x), dp: 4 (over y, core), tensor: 4 (over z).
Axes of the slice: x: 2, y: 2, z: 4, core: 2. Of those that a mesh axis runs over, the one named last changes fastest.
Arguments:
- tokens_in: bfloat16 [8192, 8192], P(('groups', 'dp'), 'tensor'), parts along dimension 0, may hold values from -6 to 6
- grad_out: bfloat16 [8192, 1024], P(('groups', 'dp'), 'tensor'), parts along dimension 0, may hold values from -3 to 3
- value_weight: bfloat16 [8192, 1024], P('tensor'), may hold values from -0.1875 to 0.1875
- token_adapter: int32 [8192], P(('groups', 'dp')), parts along dimension 0, may hold values from 0 to 512, as said below
- adapter_home: int32 [1024], P('groups'), parts along dimension 0, may hold values from 0 to 511, as said below
- cold_down: bfloat16 [960, 16, 8192], P(('groups', 'dp'), None, 'tensor'), parts along dimension 0, may hold values from -0.119628906 to 0.119628906
- cold_up: bfloat16 [960, 16, 1024], P(('groups', 'dp'), None, 'tensor'), parts along dimension 0, may hold values from -0.1875 to 0.1875
- hot_down: bfloat16 [64, 16, 8192], P('groups', None, 'tensor'), parts along dimension 0, may hold values from -0.119628906 to 0.119628906
- hot_up: bfloat16 [64, 16, 1024], P('groups', None, 'tensor'), parts along dimension 0, may hold values from -0.1875 to 0.1875
Outputs:
- input_gradient: bfloat16 [8192, 8192], P(('groups', 'dp'), 'tensor'), parts along dimension 0
- cold_down_grad: float32 [960, 16, 8192], P(('groups', 'dp'), None, 'tensor'), parts along dimension 0
- cold_up_grad: float32 [960, 16, 1024], P(('groups', 'dp'), None, 'tensor'), parts along dimension 0
- hot_down_grad: float32 [64, 16, 8192], P(('groups', 'dp'), None, 'tensor'), parts along dimension 0
- hot_up_grad: float32 [64, 16, 1024], P(('groups', 'dp'), None, 'tensor'), parts along dimension 0
The draws below stay inside these ranges and needn't reach their ends.
There are 2 independent parts, one for each index of `groups`. The reference program is written for one: setup_inputs(seed, part) draws one part's arguments, and reference() takes and returns one part's arrays. A program takes and returns all parts, laid end to end along the dimension named above; an argument that names none is the same for every part. Nothing has to cross between parts.
Inputs may be any that keep to these rules, and one draw needn't show every extreme that they name: `token_adapter`: A row r of adapter_home below 480 is a cold adapter owned by index r // 120 of dp; a row 480 + h is a hot adapter whose home is index h // 8. Among the 1024 tokens of one index of dp, at most 128 have cold adapters owned by any one index, and at most 128 have hot adapters homed on any one index; both bounds are reached on every index of dp, and on some index toward which every index of dp sends 128. `adapter_home`: a permutation of the rows 0 to 511.
All inputs are finite; a program needn't handle non-finite values.
Results may differ from the reference program's by a relative error of at most 0.0031.
Values may be sent and summed in bfloat16 or wider, within the bound.
No kernel may reach another device: no remote copies, remote signals or barrier semaphores. Data moves between devices by JAX's collectives and lax.ppermute only.
A program may use at most 128 MiB of HBM per device.

```python
import jax
import jax.numpy as jnp
from jax import lax

D = 8192
KV = 1024
RANK = 16
ADAPTERS = 512
HOT = 32
TOK_DEV = 1024
TOKENS = 4096
CAP = 128
COLD = 480
COLD_DEV = 120
HOT_DEV = 8
N_DP = 4


def draw_order(key):
    return jax.random.permutation(key, ADAPTERS).astype(jnp.int32)


def draw_adapter_home(key, part):
    adapter_order = draw_order(key)
    return jnp.zeros((ADAPTERS,), jnp.int32).at[adapter_order].set(jnp.arange(ADAPTERS, dtype=jnp.int32))


def quota(raw_key, weight_key, full_key, common_key):
    owner_weight = jax.random.randint(weight_key, (N_DP,), 1, 5)
    raw_count = jax.random.randint(raw_key, (N_DP, N_DP), 1, CAP + 1)
    slot_count = jnp.minimum(CAP, raw_count * owner_weight[None, :] // 2)
    full_dest = jax.random.randint(full_key, (N_DP, 1), 0, N_DP)
    common_dest = jax.random.randint(common_key, (), 0, N_DP)
    destination = jnp.arange(N_DP)[None, :]
    return jnp.where((destination == full_dest) | (destination == common_dest), CAP, slot_count)


def draw_token_adapter(key, part):
    adapter_order = draw_order(key)
    key = jax.random.fold_in(key, 7)
    subkeys = jax.random.split(key, 11)
    cold_count = quota(subkeys[0], subkeys[1], subkeys[2], subkeys[3])
    hot_count = quota(subkeys[4], subkeys[5], subkeys[6], subkeys[7])
    slot_index = jnp.arange(CAP)[None, None, :]
    destination = jnp.arange(N_DP)[None, :, None]
    cold_pick = jax.random.randint(subkeys[8], (N_DP, N_DP, CAP), 0, COLD_DEV)
    hot_pick = jax.random.randint(subkeys[9], (N_DP, N_DP, CAP), 0, HOT_DEV)
    cold_ids = jnp.where(slot_index < cold_count[:, :, None], adapter_order[destination * COLD_DEV + cold_pick], ADAPTERS)
    hot_ids = jnp.where(slot_index < hot_count[:, :, None], adapter_order[COLD + destination * HOT_DEV + hot_pick], ADAPTERS)
    candidates = jnp.concatenate([cold_ids.reshape(N_DP, -1), hot_ids.reshape(N_DP, -1)], axis=1)
    scores = jax.random.randint(subkeys[10], (N_DP, TOK_DEV), 0, 1 << 20) * TOK_DEV + jnp.arange(TOK_DEV)[None, :]
    shuffle = jnp.argsort(scores, axis=1)
    return jnp.take_along_axis(candidates, shuffle, axis=1).reshape(-1).astype(jnp.int32)


def steps_of(own_key, extent, pieces, least, largest):
    def one(dim, shards_of):
        heights = jax.random.uniform(jax.random.fold_in(jax.random.fold_in(own_key, 6), dim), (shards_of,), jnp.float32, least / len(pieces), largest / len(pieces))
        return jnp.repeat(jnp.exp(heights), extent[dim] // shards_of).reshape((-1,) + (1,) * (len(extent) - dim - 1))

    gain = one(*pieces[0])
    for cut in pieces[1:]:
        gain = gain * one(*cut)
    return gain


def gaussian(rng, dims, spread, reach, pieces=(), held_as=jnp.bfloat16):
    result = spread * jax.random.normal(rng, dims, jnp.float32)
    if pieces:
        result = result * steps_of(rng, dims, pieces, -0.22, 0.18)
    return jnp.clip(result, -reach, reach).astype(held_as)


def setup_inputs(seed: int = 0, part: int = 0) -> dict:
    splits = jax.random.split(jax.random.key(seed), 10)
    part_splits = jax.random.split(jax.random.fold_in(splits[9], part), 10)
    tokens_in = gaussian(part_splits[0], (TOKENS, D), 1.0, 6.0, ((0, 4), (1, 4)))
    grad_out = gaussian(part_splits[1], (TOKENS, KV), 0.5, 3.0, ((0, 4), (1, 4)))
    value_weight = gaussian(splits[2], (D, KV), KV ** -0.5, 0.1875, ((0, 4),))
    token_adapter = draw_token_adapter(jax.random.fold_in(jax.random.fold_in(splits[9], part), 71), part)
    adapter_home = draw_adapter_home(jax.random.fold_in(jax.random.fold_in(splits[9], part), 71), part)
    cold_down = gaussian(part_splits[5], (COLD, RANK, D), 0.02, 0.119628906, ((0, 4), (2, 4)))
    cold_up = gaussian(part_splits[6], (COLD, RANK, KV), KV ** -0.5, 0.1875, ((0, 4), (2, 4)))
    hot_down = gaussian(part_splits[7], (HOT, RANK, D), 0.02, 0.119628906, ((2, 4),))
    hot_up = gaussian(part_splits[8], (HOT, RANK, KV), KV ** -0.5, 0.1875, ((2, 4),))
    return dict(tokens_in=tokens_in, grad_out=grad_out, value_weight=value_weight, token_adapter=token_adapter, adapter_home=adapter_home, cold_down=cold_down, cold_up=cold_up, hot_down=hot_down, hot_up=hot_up)


ADAPTER_SCALE = 2.0


def reference(tokens_in, grad_out, value_weight, token_adapter, adapter_home, cold_down, cold_up, hot_down, hot_up):
    down_table = jnp.concatenate([cold_down, hot_down, jnp.zeros((1, RANK, D), cold_down.dtype)], axis=0)
    up_table = jnp.concatenate([cold_up, hot_up, jnp.zeros((1, RANK, KV), cold_up.dtype)], axis=0)
    has_adapter = token_adapter < ADAPTERS
    safe_ids = jnp.minimum(token_adapter, ADAPTERS - 1).astype(jnp.int32)
    table_rows = jnp.where(has_adapter, adapter_home[safe_ids], ADAPTERS).astype(jnp.int32)
    block_size = 512 if TOKENS % 512 == 0 else TOKENS
    block_count = TOKENS // block_size

    def advance(totals, block_index):
        down_weight_gradient, up_weight_gradient = totals
        start = (block_index * block_size).astype(jnp.int32)
        block_x = lax.dynamic_slice_in_dim(tokens_in, start, block_size, 0)
        block_dy = lax.dynamic_slice_in_dim(grad_out, start, block_size, 0)
        block_rows = lax.dynamic_slice_in_dim(table_rows, start, block_size, 0)
        frozen_base_product = jnp.dot(block_dy, value_weight.T, preferred_element_type=jnp.float32)
        down_weight_rows = jnp.take(down_table, block_rows, axis=0).astype(jnp.float32)
        up_weight_rows = jnp.take(up_table, block_rows, axis=0).astype(jnp.float32)
        gathered_input = block_x.astype(jnp.float32)
        gathered_output_gradient = block_dy.astype(jnp.float32)
        lowrank_input = jnp.einsum('api,ai->ap', down_weight_rows, gathered_input)
        lowrank_output = jnp.einsum('lvg,lg->lv', up_weight_rows, gathered_output_gradient)
        scaled_input = (ADAPTER_SCALE * lowrank_input).astype(jnp.bfloat16)
        scaled_output = (ADAPTER_SCALE * lowrank_output).astype(jnp.bfloat16)
        lowrank_delta = jnp.einsum('uk,ukp->up', scaled_output.astype(jnp.float32), down_weight_rows).astype(jnp.bfloat16)
        output_block_part = (frozen_base_product + lowrank_delta.astype(jnp.float32)).astype(jnp.bfloat16)
        terms_down = scaled_output.astype(jnp.float32)[:, :, None] * gathered_input[:, None, :]
        terms_up = scaled_input.astype(jnp.float32)[:, :, None] * gathered_output_gradient[:, None, :]
        down_weight_gradient = down_weight_gradient + jax.ops.segment_sum(terms_down, block_rows, num_segments=ADAPTERS + 1)
        up_weight_gradient = up_weight_gradient + jax.ops.segment_sum(terms_up, block_rows, num_segments=ADAPTERS + 1)
        return (down_weight_gradient, up_weight_gradient), output_block_part

    start_totals = (jnp.zeros((ADAPTERS + 1, RANK, D), jnp.float32), jnp.zeros((ADAPTERS + 1, RANK, KV), jnp.float32))
    (down_weight_gradient, up_weight_gradient), outputs = lax.scan(advance, start_totals, jnp.arange(block_count, dtype=jnp.int32))
    input_gradient = outputs.reshape(TOKENS, D)
    return input_gradient, down_weight_gradient[:COLD], up_weight_gradient[:COLD], down_weight_gradient[COLD:ADAPTERS], up_weight_gradient[COLD:ADAPTERS]
```

```python
import functools

import jax
import jax.numpy as jnp
from jax import lax
from jax.experimental import pallas as pl
from jax.experimental.pallas import tpu as pltpu
from jax.sharding import PartitionSpec as P

ADAPTER_SCALE = 2.0
VMEM_LIMIT = 48 * 1024 * 1024
BF16 = jnp.bfloat16
F32 = jnp.float32
I32 = jnp.int32
NN = (((1,), (0,)), ((), ()))
NT = (((1,), (1,)), ((), ()))


def mm(a, b, dims=NN):
    return lax.dot_general(a, b, dims, preferred_element_type=F32)


def sds(shape, dtype):
    return jax.ShapeDtypeStruct(shape, dtype)


def whole(shape):
    return pl.BlockSpec(shape, lambda *_: (0,) * len(shape))


def params():
    return pltpu.CompilerParams(vmem_limit_bytes=VMEM_LIMIT)


def cost(flops, moved):
    return pl.CostEstimate(flops=int(flops), bytes_accessed=int(moved), transcendentals=0)


def divide(total, parts):
    return total // parts if total % parts == 0 else total


def column(row_8):
    return jnp.transpose(row_8)[:, 0:1]


def spread_columns(scaled_t, id_col, adapters):
    rank = scaled_t.shape[0]
    count = scaled_t.shape[1]
    scaled = jnp.transpose(scaled_t).astype(BF16)
    width = adapters * rank
    lane = lax.broadcasted_iota(I32, (rank, width), 1)
    sub = lax.broadcasted_iota(I32, (rank, width), 0)
    tile = jnp.where(lax.rem(lane, rank) == sub, 1.0, 0.0).astype(BF16)
    tiled = mm(scaled, tile)
    own = lax.div(lax.broadcasted_iota(I32, (count, width), 1), rank)
    return jnp.where(own == id_col, tiled, 0.0).astype(BF16)


def spread_rows(out_ref, scaled_t, id_row, first, adapters):
    rank = scaled_t.shape[0]
    for a in range(adapters):
        out_ref[a * rank : (a + 1) * rank, :] = jnp.where(
            id_row == first + a, scaled_t, 0.0
        ).astype(BF16)


def fold(product, id_row, first, adapters, rank):
    total = jnp.zeros((rank, product.shape[1]), F32)
    for a in range(adapters):
        total += jnp.where(id_row == first + a, product[a * rank : (a + 1) * rank, :], 0.0)
    return total


def scaled(total):
    return (ADAPTER_SCALE * total).astype(BF16).astype(F32)


def pack_kernel(peers, cap, cold_here, hot_here, me_ref, adapter_ref, home_ref, x_ref, dy_ref, *rest):
    sx_refs = rest[:peers]
    sd_refs = rest[peers : 2 * peers]
    rows_ref = rest[2 * peers]
    pick_ref = rest[2 * peers + 1]
    adapters = home_ref.shape[1]
    tokens = adapter_ref.shape[1]
    slots = peers * cap

    @pl.when(pl.program_id(0) == 0)
    def _():
        me = me_ref[0]
        adapter = adapter_ref[...]
        home = home_ref[...]
        sub8 = lax.broadcasted_iota(I32, (8, adapters), 0)
        digits = jnp.where(
            sub8 == 0, lax.shift_right_logical(home, 5), jnp.where(sub8 == 1, home & 31, 0)
        ).astype(F32).astype(BF16)
        onehot = jnp.where(
            lax.broadcasted_iota(I32, (adapters, tokens), 0) == adapter, 1.0, 0.0
        ).astype(BF16)
        found = mm(digits, onehot).astype(I32)
        row = found[0:1, :] * 32 + found[1:2, :]
        has = adapter < adapters
        cold_total = cold_here * peers
        cold = has & (row < cold_total)
        hot = has & (row >= cold_total)
        dest = jnp.zeros_like(row)
        hot_row = row - cold_total
        hot_dest = jnp.zeros_like(row)
        for p in range(1, peers):
            dest += jnp.where(row >= p * cold_here, 1, 0)
            hot_dest += jnp.where(hot_row >= p * hot_here, 1, 0)
        dest = jnp.minimum(dest, peers - 1)
        local = row - dest * cold_here
        turn = dest ^ me
        height = max(8, peers)
        hits = jnp.where(
            (lax.broadcasted_iota(I32, (height, tokens), 0) == turn) & cold, 1, 0
        )
        running = hits
        lane = lax.broadcasted_iota(I32, (height, tokens), 1)
        step = 1
        while step < tokens:
            running += jnp.where(lane >= step, pltpu.roll(running, step, 1), 0)
            step *= 2
        within = jnp.sum(hits * (running - 1), axis=0, keepdims=True)
        position = jnp.where(cold, turn * cap + within, slots)
        hot_nat = jnp.where(hot, hot_row, hot_here * peers)
        hot_turn = jnp.where(
            hot,
            (hot_dest ^ me) * hot_here + hot_row - hot_dest * hot_here,
            hot_here * peers,
        )
        sub = lax.broadcasted_iota(I32, (8, tokens), 0)
        rows_ref[...] = jnp.where(
            sub == 0, hot_nat, jnp.where(sub == 1, hot_turn, jnp.where(sub == 2, position, 0))
        )
        pick_ref[...] = jnp.where(
            lax.broadcasted_iota(I32, (slots, tokens), 0) == position, 1.0, 0.0
        ).astype(BF16)
        packed = mm(pick_ref[...], dy_ref[...]).astype(BF16)
        ids = mm(
            jnp.broadcast_to(local.astype(F32), (16, tokens)).astype(BF16), pick_ref[...], NT
        )
        for k in range(peers):
            sd_refs[k][0:cap, :] = packed[k * cap : (k + 1) * cap, :]
            sd_refs[k][cap : cap + 16, :] = jnp.zeros((16, sd_refs[k].shape[1]), BF16)
            sd_refs[k][cap : cap + 16, 0:cap] = ids[:, k * cap : (k + 1) * cap].astype(BF16)

    packed_x = mm(pick_ref[...], x_ref[...]).astype(BF16)
    for k in range(peers):
        sx_refs[k][...] = packed_x[k * cap : (k + 1) * cap, :]


def pack(me, token_adapter, adapter_home, x, dy, peers, cap, cold_here, hot_here):
    tokens, width = x.shape
    kv = dy.shape[1]
    slots = peers * cap
    block = divide(width, 4)
    outs = pl.pallas_call(
        functools.partial(pack_kernel, peers, cap, cold_here, hot_here),
        grid=(width // block,),
        in_specs=[
            pl.BlockSpec(memory_space=pltpu.SMEM),
            whole((1, tokens)),
            whole((1, adapter_home.shape[0])),
            pl.BlockSpec((tokens, block), lambda j: (0, j)),
            whole((tokens, kv)),
        ],
        out_specs=[pl.BlockSpec((cap, block), lambda j: (0, j))] * peers
        + [whole((cap + 16, kv))] * peers
        + [whole((8, tokens))],
        out_shape=[sds((cap, width), BF16)] * peers
        + [sds((cap + 16, kv), BF16)] * peers
        + [sds((8, tokens), I32)],
        scratch_shapes=[pltpu.VMEM((slots, tokens), BF16)],
        compiler_params=params(),
        cost_estimate=cost(2 * slots * tokens * width, 2 * tokens * width + 2 * slots * width),
        name="pack",
    )(me, token_adapter.reshape(1, -1), adapter_home.reshape(1, -1), x, dy)
    return outs[:peers], outs[peers : 2 * peers], outs[2 * peers]


def hot_products_kernel(hot, rank, rows_ref, x_ref, hd_ref, dy_ref, hu_ref, out_ref, acc_ref):
    j = pl.program_id(0)
    part = mm(hd_ref[...], x_ref[...], NT)

    @pl.when(j == 0)
    def _():
        acc_ref[...] = part
        out_ref[0:rank, :] = fold(mm(hu_ref[...], dy_ref[...], NT), rows_ref[0:1, :], 0, hot, rank)

    @pl.when(j > 0)
    def _():
        acc_ref[...] += part

    @pl.when(j == pl.num_programs(0) - 1)
    def _():
        out_ref[rank : 2 * rank, :] = fold(acc_ref, rows_ref[0:1, :], 0, hot, rank)


def hot_products(rows, x, hot_down, dy, hot_up, rank):
    tokens, width = x.shape
    flat = hot_down.shape[0]
    kv = dy.shape[1]
    block = divide(width, 4)
    return pl.pallas_call(
        functools.partial(hot_products_kernel, flat // rank, rank),
        grid=(width // block,),
        in_specs=[
            whole((8, tokens)),
            pl.BlockSpec((tokens, block), lambda j: (0, j)),
            pl.BlockSpec((flat, block), lambda j: (0, j)),
            whole((tokens, kv)),
            whole((flat, kv)),
        ],
        out_specs=whole((2 * rank, tokens)),
        out_shape=sds((2 * rank, tokens), F32),
        scratch_shapes=[pltpu.VMEM((flat, tokens), F32)],
        compiler_params=params(),
        cost_estimate=cost(2 * flat * tokens * (width + kv), 2 * (tokens + flat) * width),
        name="hot_products",
    )(rows, x, hot_down, dy, hot_up)


def cold_out_kernel(peers, cap, adapters, rank, hot_ref, up_ref, *rest):
    rd_refs = rest[:peers]
    pay_ref, ids_ref, dys_ref = rest[peers:]
    slots = peers * cap
    ids = []
    for k in range(peers):
        dys_ref[k * cap : (k + 1) * cap, :] = rd_refs[k][0:cap, :]
        ids.append(rd_refs[k][cap : cap + 16, 0:cap].astype(F32)[0:8])
    ids_8 = jnp.concatenate(ids, axis=1)
    ids_ref[...] = ids_8
    id_row = ids_8[0:1, :]
    group = divide(adapters, 8)
    total = jnp.zeros((rank, slots), F32)
    for c in range(adapters // group):
        part = mm(up_ref[c * group * rank : (c + 1) * group * rank, :], dys_ref[...], NT)
        total += fold(part, id_row, float(c * group), group, rank)
    pay_ref[0 : 2 * rank, :] = hot_ref[...]
    half = rank // 2
    pay_ref[2 * rank : 2 * rank + half, 0:slots] = total[0:half]
    pay_ref[2 * rank : 2 * rank + half, slots : 2 * slots] = total[half:rank]


def cold_out(hot_part, cold_up, rd, cap, rank):
    peers = len(rd)
    flat, kv = cold_up.shape
    slots = peers * cap
    tokens = hot_part.shape[1]
    return pl.pallas_call(
        functools.partial(cold_out_kernel, peers, cap, flat // rank, rank),
        out_shape=[sds((2 * rank + rank // 2, tokens), F32), sds((8, slots), F32)],
        scratch_shapes=[pltpu.VMEM((slots, kv), BF16)],
        compiler_params=params(),
        cost_estimate=cost(2 * flat * slots * kv, 2 * (flat + slots) * kv),
        name="cold_out",
    )(hot_part, cold_up, *rd)


def cold_total_out(pay_refs, rank, slots):
    half = rank // 2
    rows = slice(2 * rank, 2 * rank + half)
    total = sum((r[rows, :] for r in pay_refs[1:]), pay_refs[0][rows, :])
    return scaled(jnp.concatenate([total[:, 0:slots], total[:, slots : 2 * slots]], axis=0))


def hot_grads_kernel(peers, parts, rank, hot, rows_ref, x_ref, dy_ref, *rest):
    pay_refs = rest[:parts]
    keep_ref, send_ref, wide_ref = rest[parts:]
    j = pl.program_id(0)
    width = x_ref.shape[1]
    block = hot // peers * rank

    def put(product, column):
        for k in range(peers):
            piece = product[k * block : (k + 1) * block, :]
            at = pl.ds((k // 2) * block, block)
            if k % 2 == 0:
                keep_ref[at, column] = piece
            else:
                send_ref[at, column] = piece.astype(BF16)

    def total(first):
        return scaled(
            sum((r[first : first + rank, :] for r in pay_refs[1:]), pay_refs[0][first : first + rank, :])
        )

    @pl.when(j == 0)
    def _():
        turn = rows_ref[1:2, :]
        spread_rows(wide_ref, total(rank), turn, 0, hot)
        kv = dy_ref.shape[1]
        put(mm(wide_ref[...], dy_ref[...]), pl.ds(keep_ref.shape[1] - kv, kv))
        spread_rows(wide_ref, total(0), turn, 0, hot)

    put(mm(wide_ref[...], x_ref[...]), pl.ds(pl.multiple_of(j * width, width), width))


def hot_grads(rows, x, dy, pays, rank, hot, peers):
    tokens, width = x.shape
    kv = dy.shape[1]
    flat = hot * rank
    block = divide(width, 4)
    half = flat // 2
    return pl.pallas_call(
        functools.partial(hot_grads_kernel, peers, len(pays), rank, hot),
        grid=(width // block,),
        in_specs=[
            whole((8, tokens)),
            pl.BlockSpec((tokens, block), lambda j: (0, j)),
            whole((tokens, kv)),
        ]
        + [whole(pays[0].shape)] * len(pays),
        out_specs=[whole((half, width + kv))] * 2,
        out_shape=[sds((half, width + kv), F32), sds((half, width + kv), BF16)],
        scratch_shapes=[pltpu.VMEM((flat, tokens), BF16)],
        compiler_params=params(),
        cost_estimate=cost(2 * flat * tokens * (width + kv), 2 * tokens * width + 6 * half * width),
        name="hot_grads",
    )(rows, x, dy, *pays)


def cold_delta_kernel(parts, cap, rank, slots, first, count, ids_ref, down_ref, *rest):
    pay_refs = rest[:parts]
    out_refs = rest[parts : parts + count]
    wide_ref = rest[parts + count]
    adapters = down_ref.shape[0] // rank

    @pl.when(pl.program_id(0) == 0)
    def _():
        lo, hi = first * cap, (first + count) * cap
        total = cold_total_out(pay_refs, rank, slots)[:, lo:hi]
        id_col = column(ids_ref[...][:, lo:hi]).astype(I32)
        wide_ref[...] = spread_columns(total, id_col, adapters)

    delta = mm(wide_ref[...], down_ref[...]).astype(BF16)
    for k in range(count):
        out_refs[k][...] = delta[k * cap : (k + 1) * cap, :]


def cold_delta(ids, cold_down, pays, cap, rank, first, count):
    flat, width = cold_down.shape
    slots = ids.shape[1]
    block = divide(width, 4)
    return pl.pallas_call(
        functools.partial(cold_delta_kernel, len(pays), cap, rank, slots, first, count),
        grid=(width // block,),
        in_specs=[whole((8, slots)), pl.BlockSpec((flat, block), lambda j: (0, j))]
        + [whole(pays[0].shape)] * len(pays),
        out_specs=[pl.BlockSpec((cap, block), lambda j: (0, j))] * count,
        out_shape=[sds((cap, width), BF16)] * count,
        scratch_shapes=[pltpu.VMEM((count * cap, flat), BF16)],
        compiler_params=params(),
        cost_estimate=cost(2 * flat * count * cap * width, 2 * flat * width + 2 * count * cap * width),
        name="cold_delta",
    )(ids, cold_down, *pays)


def cold_in_kernel(peers, cap, rank, ids_ref, down_ref, *rest):
    rx_refs = rest[:peers]
    out_ref, xs_ref = rest[peers:]
    i = pl.program_id(0)
    group = down_ref.shape[0] // rank

    @pl.when(i == 0)
    def _():
        for k in range(peers):
            xs_ref[k * cap : (k + 1) * cap, :] = rx_refs[k][...]
        out_ref[...] = jnp.zeros_like(out_ref)

    part = mm(down_ref[...], xs_ref[...], NT)
    shifted = ids_ref[0:1, :].astype(I32) - i * group
    out_ref[...] += fold(part, shifted, 0, group, rank)


def cold_in(ids, cold_down, rx, cap, rank):
    peers = len(rx)
    flat, width = cold_down.shape
    slots = ids.shape[1]
    group = divide(flat // rank, 4) * rank
    return pl.pallas_call(
        functools.partial(cold_in_kernel, peers, cap, rank),
        grid=(flat // group,),
        in_specs=[whole((8, slots)), pl.BlockSpec((group, width), lambda i: (i, 0))]
        + [whole((cap, width))] * peers,
        out_specs=whole((rank, slots)),
        out_shape=sds((rank, slots), F32),
        scratch_shapes=[pltpu.VMEM((slots, width), BF16)],
        compiler_params=params(),
        cost_estimate=cost(2 * flat * slots * width, 2 * (flat + slots) * width),
        name="cold_in",
    )(ids, cold_down, *rx)


def cold_down_grad_kernel(parts, peers, cap, rank, ids_ref, *rest):
    pay_refs = rest[:parts]
    rx_refs = rest[parts : parts + peers]
    out_ref, xs_ref, so_ref, wide_ref = rest[parts + peers :]
    i = pl.program_id(0)
    group = out_ref.shape[0] // rank

    @pl.when(i == 0)
    def _():
        for k in range(peers):
            xs_ref[k * cap : (k + 1) * cap, :] = rx_refs[k][...]
        so_ref[...] = cold_total_out(pay_refs, rank, peers * cap)

    shifted = ids_ref[0:1, :].astype(I32) - i * group
    spread_rows(wide_ref, so_ref[...], shifted, 0, group)
    out_ref[...] = mm(wide_ref[...], xs_ref[...])


def cold_down_gradient(ids, pays, rx, cap, rank, adapters):
    peers = len(rx)
    width = rx[0].shape[1]
    slots = ids.shape[1]
    flat = adapters * rank
    group = divide(adapters, 4) * rank
    return pl.pallas_call(
        functools.partial(cold_down_grad_kernel, len(pays), peers, cap, rank),
        grid=(flat // group,),
        in_specs=[whole((8, slots))]
        + [whole(pays[0].shape)] * len(pays)
        + [whole((cap, width))] * peers,
        out_specs=pl.BlockSpec((group, width), lambda i: (i, 0)),
        out_shape=sds((flat, width), F32),
        scratch_shapes=[
            pltpu.VMEM((slots, width), BF16),
            pltpu.VMEM((rank, slots), F32),
            pltpu.VMEM((group, slots), BF16),
        ],
        compiler_params=params(),
        cost_estimate=cost(2 * flat * slots * width, 4 * flat * width + 2 * slots * width),
        name="cold_down_grad",
    )(ids, *pays, *rx)


def cold_up_grad_kernel(parts, peers, cap, rank, ids_ref, *rest):
    in_refs = rest[:parts]
    rd_refs = rest[parts : parts + peers]
    out_ref, dys_ref, si_ref, wide_ref = rest[parts + peers :]
    i = pl.program_id(0)
    group = out_ref.shape[0] // rank

    @pl.when(i == 0)
    def _():
        for k in range(peers):
            dys_ref[k * cap : (k + 1) * cap, :] = rd_refs[k][0:cap, :]
        si_ref[...] = scaled(sum((r[...] for r in in_refs[1:]), in_refs[0][...]))

    shifted = ids_ref[0:1, :].astype(I32) - i * group
    spread_rows(wide_ref, si_ref[...], shifted, 0, group)
    out_ref[...] = mm(wide_ref[...], dys_ref[...])


def cold_up_gradient(ids, ins, rd, cap, rank, adapters):
    peers = len(rd)
    kv = rd[0].shape[1]
    slots = ids.shape[1]
    flat = adapters * rank
    group = divide(adapters, 2) * rank
    return pl.pallas_call(
        functools.partial(cold_up_grad_kernel, len(ins), peers, cap, rank),
        grid=(flat // group,),
        in_specs=[whole((8, slots))]
        + [whole((rank, slots))] * len(ins)
        + [whole((cap + 16, kv))] * peers,
        out_specs=pl.BlockSpec((group, kv), lambda i: (i, 0)),
        out_shape=sds((flat, kv), F32),
        scratch_shapes=[
            pltpu.VMEM((slots, kv), BF16),
            pltpu.VMEM((rank, slots), F32),
            pltpu.VMEM((group, slots), BF16),
        ],
        compiler_params=params(),
        cost_estimate=cost(2 * flat * slots * kv, 4 * flat * kv + 2 * slots * kv),
        name="cold_up_grad",
    )(ids, *ins, *rd)


def position_matrix(rows_ref, first, count):
    tokens = rows_ref.shape[1]
    as_float = jnp.broadcast_to(rows_ref[2:3, :], (8, tokens)).astype(F32)
    pos = column(as_float).astype(I32) - first
    return jnp.where(lax.broadcasted_iota(I32, (tokens, count), 1) == pos, 1.0, 0.0).astype(BF16)


def base_kernel(parts, near, cap, rank, t_ref, rows_ref, w_ref, hd_ref, *rest):
    dy_refs = rest[:parts]
    pay_refs = rest[parts : 2 * parts]
    near_refs = rest[2 * parts : 2 * parts + near]
    out_ref, wide_ref, place_ref, near_ref = rest[2 * parts + near :]
    t = t_ref[0]
    kv = dy_refs[0].shape[1]
    tokens = rows_ref.shape[1]

    @pl.when(pl.program_id(0) == 0)
    def _():
        total = scaled(sum((r[0:rank, :] for r in pay_refs[1:]), pay_refs[0][0:rank, :]))
        as_float = jnp.broadcast_to(rows_ref[0:1, :], (8, tokens)).astype(F32)
        id_col = column(as_float).astype(I32)
        wide_ref[...] = spread_columns(total, id_col, hd_ref.shape[0] // rank)
        place_ref[...] = position_matrix(rows_ref, 0, near * cap)

    total = mm(wide_ref[...], hd_ref[...]).astype(BF16).astype(F32)
    for k in range(near):
        near_ref[k * cap : (k + 1) * cap, :] = near_refs[k][...]
    total += mm(place_ref[...], near_ref[...])
    for k in range(parts):
        at = pl.ds(pl.multiple_of((t ^ k) * kv, kv), kv)
        total += mm(dy_refs[k][...], w_ref[:, at], NT)
    out_ref[...] = total


def base(t, rows, weight, hot_down, dys, pays, nears, cap, rank):
    width, kv_all = weight.shape
    tokens, kv = dys[0].shape
    flat = hot_down.shape[0]
    block = divide(width, 4)
    near = len(nears)
    return pl.pallas_call(
        functools.partial(base_kernel, len(dys), near, cap, rank),
        grid=(width // block,),
        in_specs=[
            pl.BlockSpec(memory_space=pltpu.SMEM),
            whole((8, tokens)),
            pl.BlockSpec((block, kv_all), lambda j: (j, 0)),
            pl.BlockSpec((flat, block), lambda j: (0, j)),
        ]
        + [whole((tokens, kv))] * len(dys)
        + [whole(pays[0].shape)] * len(pays)
        + [pl.BlockSpec((cap, block), lambda j: (0, j))] * near,
        out_specs=pl.BlockSpec((tokens, block), lambda j: (0, j)),
        out_shape=sds((tokens, width), F32),
        scratch_shapes=[
            pltpu.VMEM((tokens, flat), BF16),
            pltpu.VMEM((tokens, near * cap), BF16),
            pltpu.VMEM((near * cap, block), BF16),
        ],
        compiler_params=params(),
        cost_estimate=cost(
            2 * tokens * width * (kv_all + flat + near * cap),
            2 * width * kv_all + 4 * tokens * width + 2 * flat * width,
        ),
        name="base",
    )(t, rows, weight, hot_down, *dys, *pays, *nears)


def final_kernel(first, cap, rows_ref, base_ref, *rest):
    far = len(rest) - 3
    far_refs = rest[:far]
    out_ref, place_ref, far_ref = rest[far:]

    @pl.when(pl.program_id(0) == 0)
    def _():
        place_ref[...] = position_matrix(rows_ref, first * cap, far * cap)

    for k in range(far):
        far_ref[k * cap : (k + 1) * cap, :] = far_refs[k][...]
    out_ref[...] = (base_ref[...] + mm(place_ref[...], far_ref[...])).astype(BF16)


def final(rows, base_sum, fars, first, cap):
    tokens, width = base_sum.shape
    block = divide(width, 8)
    far = len(fars)
    return pl.pallas_call(
        functools.partial(final_kernel, first, cap),
        grid=(width // block,),
        in_specs=[whole((8, tokens)), pl.BlockSpec((tokens, block), lambda j: (0, j))]
        + [pl.BlockSpec((cap, block), lambda j: (0, j))] * far,
        out_specs=pl.BlockSpec((tokens, block), lambda j: (0, j)),
        out_shape=sds((tokens, width), BF16),
        scratch_shapes=[
            pltpu.VMEM((tokens, far * cap), BF16),
            pltpu.VMEM((far * cap, block), BF16),
        ],
        compiler_params=params(),
        cost_estimate=cost(2 * tokens * width * far * cap, 6 * tokens * width),
        name="final",
    )(rows, base_sum, *fars)


def swap(value, axis, k):
    count = lax.axis_size(axis)
    return lax.ppermute(value, axis, [(i, i ^ k) for i in range(count)])


def shards(
    tokens_in,
    grad_out,
    value_weight,
    token_adapter,
    adapter_home,
    cold_down,
    cold_up,
    hot_down,
    hot_up,
):
    peers = lax.axis_size("dp")
    parts = lax.axis_size("tensor")
    tokens, width = tokens_in.shape
    kv = grad_out.shape[1]
    cap = tokens // (2 * peers)
    cold_here, rank, _ = cold_down.shape
    hot = hot_down.shape[0]
    hot_here = hot // peers
    near = 2
    flat_cold_down = cold_down.reshape(cold_here * rank, width)
    flat_cold_up = cold_up.reshape(cold_here * rank, kv)
    flat_hot_down = hot_down.reshape(hot * rank, width)
    flat_hot_up = hot_up.reshape(hot * rank, kv)
    me = lax.axis_index("dp").astype(I32).reshape(1)
    t = lax.axis_index("tensor").astype(I32).reshape(1)

    sx, sd, rows = pack(
        me, token_adapter, adapter_home, tokens_in, grad_out, peers, cap, cold_here, hot_here
    )
    rd = [sd[0]] + [swap(sd[k], "dp", k) for k in range(1, peers)]
    rx = [sx[0]] + [swap(sx[k], "dp", k) for k in range(1, peers)]
    dys = [grad_out] + [swap(grad_out, "tensor", k) for k in range(1, parts)]

    hot_part = hot_products(rows, tokens_in, flat_hot_down, grad_out, flat_hot_up, rank)
    pay, ids = cold_out(hot_part, flat_cold_up, rd, cap, rank)
    pays = [pay] + [swap(pay, "tensor", k) for k in range(1, parts)]

    keep, send = hot_grads(rows, tokens_in, grad_out, pays, rank, hot, peers)
    mate = swap(send, "dp", 1)
    far_delta = cold_delta(ids, flat_cold_down, pays, cap, rank, near, peers - near)
    far_back = [swap(far_delta[k - near], "dp", k) for k in range(near, peers)]
    near_delta = cold_delta(ids, flat_cold_down, pays, cap, rank, 0, near)
    near_back = [near_delta[0]] + [swap(near_delta[k], "dp", k) for k in range(1, near)]

    rows_home = hot_here * rank
    hot_sum = keep[:rows_home] + mate[:rows_home].astype(F32)
    for c in range(1, peers // 2):
        at = slice(c * rows_home, (c + 1) * rows_home)
        away = (keep[at] + mate[at].astype(F32)).astype(BF16)
        hot_sum = hot_sum + swap(away, "dp", 2 * c).astype(F32)
    hot_down_grad = hot_sum[:, :width].reshape(hot_here, rank, width)
    hot_up_grad = hot_sum[:, width:].reshape(hot_here, rank, kv)

    in_part = cold_in(ids, flat_cold_down, rx, cap, rank)
    ins = [in_part] + [swap(in_part, "tensor", k) for k in range(1, parts)]
    cold_down_grad = cold_down_gradient(ids, pays, rx, cap, rank, cold_here)
    cold_up_grad = cold_up_gradient(ids, ins, rd, cap, rank, cold_here)

    base_sum = base(t, rows, value_weight, flat_hot_down, dys, pays, near_back, cap, rank)
    input_gradient = final(rows, base_sum, far_back, near, cap)
    return (
        input_gradient,
        cold_down_grad.reshape(cold_here, rank, width),
        cold_up_grad.reshape(cold_here, rank, kv),
        hot_down_grad,
        hot_up_grad,
    )


def solution(mesh):
    in_specs = (
        P(("groups", "dp"), "tensor"),
        P(("groups", "dp"), "tensor"),
        P("tensor", None),
        P(("groups", "dp")),
        P("groups"),
        P(("groups", "dp"), None, "tensor"),
        P(("groups", "dp"), None, "tensor"),
        P("groups", None, "tensor"),
        P("groups", None, "tensor"),
    )
    out_specs = (
        P(("groups", "dp"), "tensor"),
        P(("groups", "dp"), None, "tensor"),
        P(("groups", "dp"), None, "tensor"),
        P(("groups", "dp"), None, "tensor"),
        P(("groups", "dp"), None, "tensor"),
    )
    return jax.shard_map(shards, mesh=mesh, in_specs=in_specs, out_specs=out_specs, check_vma=False)
```

```python
import functools

import jax
import jax.numpy as jnp
from jax import lax
from jax.experimental import pallas as pl
from jax.experimental.pallas import tpu as pltpu
from jax.sharding import PartitionSpec as P

ADAPTER_SCALE = 2.0
VMEM_LIMIT = 16 * 1024 * 1024
COST_SCALE = 0.3
BF16 = jnp.bfloat16
F32 = jnp.float32
I32 = jnp.int32
NN = (((1,), (0,)), ((), ()))
NT = (((1,), (1,)), ((), ()))


def mm(a, b, dims=NN):
    return lax.dot_general(a, b, dims, preferred_element_type=F32)


def sds(shape, dtype):
    return jax.ShapeDtypeStruct(shape, dtype)


def whole(shape):
    return pl.BlockSpec(shape, lambda *_: (0,) * len(shape))


def vmem(count):
    return [pl.BlockSpec(memory_space=pltpu.VMEM)] * count


def smem():
    return pl.BlockSpec(memory_space=pltpu.SMEM)


def hbm(count):
    return [pl.BlockSpec(memory_space=pltpu.HBM)] * count


def anywhere(count):
    return [pl.BlockSpec(memory_space=pl.ANY)] * count


def params():
    return pltpu.CompilerParams(vmem_limit_bytes=VMEM_LIMIT)


def cost(flops, moved):
    return pl.CostEstimate(
        flops=int(COST_SCALE * flops), bytes_accessed=int(COST_SCALE * moved), transcendentals=0
    )


def join(refs, into, rows):
    for k, ref in enumerate(refs):
        into[k * rows : (k + 1) * rows, :] = ref[0:rows, 0 : into.shape[1]]


def join_last(refs, into, rows):
    for k, ref in enumerate(refs):
        into[k * rows : (k + 1) * rows, :] = ref[0:rows, ref.shape[1] - into.shape[1] :]


TOKEN = (8, 128)


def call(body, name, after, args, in_specs, out_shape, flops, moved, out_specs=None, scratch=(), grid=None):
    taken, given = len(args), len(out_shape)
    chained = [] if after is None else [after]

    def kernel(*refs):
        outs = refs[taken + len(chained) :]
        body(*refs[:taken], *outs[:given], *outs[given + 1 :])
        outs[given][...] = jnp.zeros(TOKEN, F32)

    more = {} if grid is None else {"grid": grid}
    results = pl.pallas_call(
        kernel,
        in_specs=list(in_specs) + anywhere(len(chained)),
        out_specs=list(out_specs or vmem(given)) + (vmem(1) if grid is None else [whole(TOKEN)]),
        out_shape=list(out_shape) + [sds(TOKEN, F32)],
        scratch_shapes=list(scratch),
        compiler_params=params(),
        cost_estimate=cost(flops, moved),
        name=name,
        **more,
    )(*args, *chained)
    return results[:given], results[given]


def divide(total, parts):
    return total // parts if total % parts == 0 else total


def pieces_of(total, parts=4):
    step = divide(total, parts)
    return [slice(k * step, (k + 1) * step) for k in range(total // step)]


def column(row_8):
    return jnp.transpose(row_8)[:, 0:1]


def spread_columns(scaled_t, id_col, adapters):
    rank = scaled_t.shape[0]
    count = scaled_t.shape[1]
    scaled = jnp.transpose(scaled_t).astype(BF16)
    width = adapters * rank
    lane = lax.broadcasted_iota(I32, (rank, width), 1)
    sub = lax.broadcasted_iota(I32, (rank, width), 0)
    tile = jnp.where(lax.rem(lane, rank) == sub, 1.0, 0.0).astype(BF16)
    tiled = mm(scaled, tile)
    own = lax.div(lax.broadcasted_iota(I32, (count, width), 1), rank)
    return jnp.where(own == id_col, tiled, 0.0).astype(BF16)


def spread_rows(out_ref, scaled_t, id_row, first, adapters):
    rank = scaled_t.shape[0]
    for a in range(adapters):
        out_ref[a * rank : (a + 1) * rank, :] = jnp.where(
            id_row == first + a, scaled_t, 0.0
        ).astype(BF16)


def fold(product, id_row, first, adapters, rank):
    total = jnp.zeros((rank, product.shape[1]), F32)
    for a in range(adapters):
        total += jnp.where(id_row == first + a, product[a * rank : (a + 1) * rank, :], 0.0)
    return total


def scaled(total):
    return (ADAPTER_SCALE * total).astype(BF16).astype(F32)


def route_kernel(peers, cap, cold_here, hot_here, me_ref, adapter_in, home_in, dy_in, x_ref, *rest):
    sd_refs = rest[:peers]
    rows_ref, pick_ref, held_ref, adapter_ref, home_ref, dy_ref, sems = rest[peers:]
    pairs = ((adapter_in, adapter_ref), (home_in, home_ref), (dy_in, dy_ref), (x_ref, held_ref))
    loads = [pltpu.make_async_copy(a, b, sems.at[n]) for n, (a, b) in enumerate(pairs)]
    for load in loads:
        load.start()
    adapters = home_ref.shape[1]
    tokens = adapter_ref.shape[1]
    slots = peers * cap
    loads[0].wait()
    loads[1].wait()
    me = me_ref[0]
    adapter = adapter_ref[...]
    home = home_ref[...]
    sub8 = lax.broadcasted_iota(I32, (8, adapters), 0)
    digits = jnp.where(
        sub8 == 0, lax.shift_right_logical(home, 5), jnp.where(sub8 == 1, home & 31, 0)
    ).astype(F32).astype(BF16)
    onehot = jnp.where(
        lax.broadcasted_iota(I32, (adapters, tokens), 0) == adapter, 1.0, 0.0
    ).astype(BF16)
    found = mm(digits, onehot).astype(I32)
    row = found[0:1, :] * 32 + found[1:2, :]
    has = adapter < adapters
    cold_total = cold_here * peers
    cold = has & (row < cold_total)
    hot = has & (row >= cold_total)
    dest = jnp.zeros_like(row)
    hot_row = row - cold_total
    hot_dest = jnp.zeros_like(row)
    for p in range(1, peers):
        dest += jnp.where(row >= p * cold_here, 1, 0)
        hot_dest += jnp.where(hot_row >= p * hot_here, 1, 0)
    dest = jnp.minimum(dest, peers - 1)
    local = row - dest * cold_here
    turn = dest ^ me
    height = max(8, peers)
    hits = jnp.where((lax.broadcasted_iota(I32, (height, tokens), 0) == turn) & cold, 1, 0)
    running = hits
    lane = lax.broadcasted_iota(I32, (height, tokens), 1)
    step = 1
    while step < tokens:
        running += jnp.where(lane >= step, pltpu.roll(running, step, 1), 0)
        step *= 2
    within = jnp.sum(hits * (running - 1), axis=0, keepdims=True)
    position = jnp.where(cold, turn * cap + within, slots)
    hot_nat = jnp.where(hot, hot_row, hot_here * peers)
    hot_turn = jnp.where(
        hot,
        (hot_dest ^ me) * hot_here + hot_row - hot_dest * hot_here,
        hot_here * peers,
    )
    sub = lax.broadcasted_iota(I32, (8, tokens), 0)
    rows_ref[...] = jnp.where(
        sub == 0, hot_nat, jnp.where(sub == 1, hot_turn, jnp.where(sub == 2, position, 0))
    )
    pick_ref[...] = jnp.where(
        lax.broadcasted_iota(I32, (slots, tokens), 0) == position, 1.0, 0.0
    ).astype(BF16)
    loads[2].wait()
    packed = mm(pick_ref[...], dy_ref[...]).astype(BF16)
    ids = mm(jnp.broadcast_to(local.astype(F32), (16, tokens)).astype(BF16), pick_ref[...], NT)
    for k in range(peers):
        sd_refs[k][0:cap, :] = packed[k * cap : (k + 1) * cap, :]
        sd_refs[k][cap : cap + 16, :] = jnp.zeros((16, sd_refs[k].shape[1]), BF16)
        sd_refs[k][cap : cap + 16, 0:cap] = ids[:, k * cap : (k + 1) * cap].astype(BF16)
    loads[3].wait()


def route(me, token_adapter, adapter_home, dy, x, peers, cap, cold_here, hot_here):
    tokens, kv = dy.shape
    slots = peers * cap
    outs, token = call(
        functools.partial(route_kernel, peers, cap, cold_here, hot_here),
        "route",
        None,
        (me, token_adapter.reshape(1, -1), adapter_home.reshape(1, -1), dy, x),
        [smem()] + hbm(4),
        [sds((cap + 16, kv), BF16)] * peers
        + [sds((8, tokens), I32), sds((slots, tokens), BF16), sds(x.shape, BF16)],
        2 * slots * tokens * kv,
        2 * tokens * kv,
        scratch=[
            pltpu.VMEM((1, tokens), I32),
            pltpu.VMEM((1, adapter_home.shape[0]), I32),
            pltpu.VMEM((tokens, kv), BF16),
            pltpu.SemaphoreType.DMA((4,)),
        ],
    )
    return outs[:peers], *outs[peers:], token


def pack_kernel(peers, cap, pick_ref, x_ref, *out_refs):
    for at in pieces_of(x_ref.shape[1]):
        packed = mm(pick_ref[...], x_ref[:, at]).astype(BF16)
        for k in range(peers):
            out_refs[k][:, at] = packed[k * cap : (k + 1) * cap, :]


def pack(pick, x, peers, cap, after):
    tokens, width = x.shape
    slots = peers * cap
    return call(
        functools.partial(pack_kernel, peers, cap),
        "pack",
        after,
        (pick, x),
        vmem(2),
        [sds((cap, width), BF16)] * peers,
        2 * slots * tokens * width,
        2 * tokens * width + 2 * slots * width,
    )


def hot_products_kernel(rank, rows_ref, x_ref, hd_ref, dy_ref, hu_ref, out_ref):
    hot = hd_ref.shape[0] // rank
    tokens = x_ref.shape[0]
    half = divide(tokens, 2)
    for c in range(tokens // half):
        at = slice(c * half, (c + 1) * half)
        row = rows_ref[0:1, at]
        out_ref[0:rank, at] = fold(mm(hu_ref[...], dy_ref[at, :], NT), row, 0, hot, rank)
        out_ref[rank : 2 * rank, at] = fold(mm(hd_ref[...], x_ref[at, :], NT), row, 0, hot, rank)


def hot_products(rows, x, hot_down, dy, hot_up, rank, after):
    tokens, width = x.shape
    flat = hot_down.shape[0]
    kv = dy.shape[1]
    return call(
        functools.partial(hot_products_kernel, rank),
        "hot_products",
        after,
        (rows, x, hot_down, dy, hot_up),
        vmem(5),
        [sds((2 * rank, tokens), F32)],
        2 * flat * tokens * (width + kv),
        2 * (tokens + flat) * width,
    )


def cold_out_kernel(peers, cap, rank, hot_ref, up_ref, *rest):
    rd_refs = rest[:peers]
    pay_ref, ids_ref, dys_ref = rest[peers:]
    adapters = up_ref.shape[0] // rank
    slots = peers * cap
    join_last(rd_refs, dys_ref, cap)
    kv = up_ref.shape[1]
    ids = [
        r[cap : cap + 16, r.shape[1] - kv : r.shape[1] - kv + cap].astype(F32)[0:8]
        for r in rd_refs
    ]
    ids_8 = jnp.concatenate(ids, axis=1)
    ids_ref[...] = ids_8
    id_row = ids_8[0:1, :]
    group = divide(adapters, 8)
    total = jnp.zeros((rank, slots), F32)
    for c in range(adapters // group):
        part = mm(up_ref[c * group * rank : (c + 1) * group * rank, :], dys_ref[...], NT)
        total += fold(part, id_row, float(c * group), group, rank)
    half = rank // 2
    folded = jnp.concatenate([total[0:half], total[half:rank]], axis=1)
    piece = pay_ref.shape[2]
    for q in range(pay_ref.shape[0]):
        at = slice(q * piece, (q + 1) * piece)
        pay_ref[q, 0 : 2 * rank, :] = hot_ref[:, at]
        pay_ref[q, 2 * rank : 2 * rank + half, :] = folded[:, at]


def cold_out(hot_part, cold_up, rd, cap, rank, parts, after):
    peers = len(rd)
    flat, kv = cold_up.shape
    slots = peers * cap
    tokens = hot_part.shape[1]
    return call(
        functools.partial(cold_out_kernel, peers, cap, rank),
        "cold_out",
        after,
        (hot_part, cold_up, *rd),
        vmem(2 + peers),
        [sds((parts, 2 * rank + rank // 2, tokens // parts), F32), sds((8, slots), F32)],
        2 * flat * slots * kv,
        2 * (flat + slots) * kv,
        scratch=[pltpu.VMEM((slots, kv), BF16)],
    )


def sum_pieces_kernel(*refs):
    out_ref = refs[-1]
    total = refs[0][0]
    for ref in refs[1:-1]:
        total += ref[0]
    filled, width = out_ref.shape[1:]
    total = (ADAPTER_SCALE * total).astype(BF16).astype(F32)
    rest = jnp.zeros((filled - total.shape[0], width), F32)
    out_ref[0] = jnp.concatenate([total, rest], axis=0).astype(BF16)


def sum_pieces(pays, after):
    _, height, width = pays[0].shape
    filled = -(-height // 16) * 16
    return call(
        sum_pieces_kernel,
        "sum_pieces",
        after,
        tuple(pays),
        vmem(len(pays)),
        [sds((1, filled, width), BF16)],
        len(pays) * pays[0].size,
        4 * len(pays) * pays[0].size,
    )


def gathered(got_ref, first, last):
    return jnp.concatenate(
        [got_ref[q, first:last, :].astype(F32) for q in range(got_ref.shape[0])], axis=1
    )


def hot_out_of(got_ref, rank):
    return gathered(got_ref, 0, rank)


def hot_in_of(got_ref, rank):
    return gathered(got_ref, rank, 2 * rank)


def cold_out_of(got_ref, rank, slots):
    half = rank // 2
    folded = gathered(got_ref, 2 * rank, got_ref.shape[1])[0:half]
    return jnp.concatenate([folded[:, 0:slots], folded[:, slots : 2 * slots]], axis=0)


def hot_grads_kernel(peers, rank, hot, rows_ref, x_ref, dy_ref, got_ref, keep_ref, send_ref, wide_ref):
    width = x_ref.shape[1]
    kv = dy_ref.shape[1]
    block = hot // peers * rank

    def put(product, column):
        for k in range(peers):
            piece = product[k * block : (k + 1) * block, :]
            at = slice((k // 2) * block, (k // 2 + 1) * block)
            if k % 2 == 0:
                keep_ref[at, column] = piece
            else:
                send_ref[at, column] = piece.astype(BF16)

    turn = rows_ref[1:2, :]
    spread_rows(wide_ref, hot_in_of(got_ref, rank), turn, 0, hot)
    put(mm(wide_ref[...], dy_ref[...]), slice(width, width + kv))
    spread_rows(wide_ref, hot_out_of(got_ref, rank), turn, 0, hot)
    step = divide(width, 4)
    for j in range(width // step):
        at = slice(j * step, (j + 1) * step)
        put(mm(wide_ref[...], x_ref[:, at]), at)


def hot_grads(rows, x, dy, got, rank, hot, peers, after):
    tokens, width = x.shape
    kv = dy.shape[1]
    flat = hot * rank
    half = flat // 2
    return call(
        functools.partial(hot_grads_kernel, peers, rank, hot),
        "hot_grads",
        after,
        (rows, x, dy, got),
        vmem(4),
        [sds((half, width + kv), F32), sds((half, width + kv), BF16)],
        2 * flat * tokens * (width + kv),
        2 * tokens * width + 6 * half * width,
        scratch=[pltpu.VMEM((flat, tokens), BF16)],
    )


def hot_away_kernel(keep_ref, mate_ref, *out_refs):
    height = out_refs[0].shape[0]
    for c, ref in enumerate(out_refs):
        at = slice((c + 1) * height, (c + 2) * height)
        ref[...] = (keep_ref[at, :] + mate_ref[at, :].astype(F32)).astype(BF16)


def hot_away(keep, mate, height, count, after):
    return call(
        hot_away_kernel,
        "hot_away",
        after,
        (keep, mate),
        vmem(2),
        [sds((height, keep.shape[1]), BF16)] * count,
        keep.size,
        8 * keep.size,
    )


def hot_final_kernel(keep_ref, mate_ref, *rest):
    down_ref, up_ref = rest[-2:]
    height, width = down_ref.shape
    total = keep_ref[0:height, :] + mate_ref[0:height, :].astype(F32)
    for ref in rest[:-2]:
        total += ref[...].astype(F32)
    down_ref[...] = total[:, 0:width]
    up_ref[...] = total[:, width:]


def hot_final(keep, mate, fars, width, height, after):
    return call(
        hot_final_kernel,
        "hot_final",
        after,
        (keep, mate, *fars),
        vmem(2 + len(fars)),
        [sds((height, width), F32), sds((height, keep.shape[1] - width), F32)],
        keep.size,
        4 * keep.size,
    )


def cold_delta_kernel(cap, rank, first, count, ids_ref, down_ref, got_ref, *rest):
    out_refs = rest[:count]
    wide_ref = rest[count]
    flat, width = down_ref.shape
    lo, hi = first * cap, (first + count) * cap
    total = cold_out_of(got_ref, rank, ids_ref.shape[1])[:, lo:hi]
    id_col = column(ids_ref[:, lo:hi]).astype(I32)
    wide_ref[...] = spread_columns(total, id_col, flat // rank)
    step = divide(width, 4)
    for j in range(width // step):
        at = slice(j * step, (j + 1) * step)
        delta = mm(wide_ref[...], down_ref[:, at]).astype(BF16)
        for k in range(count):
            out_refs[k][:, at] = delta[k * cap : (k + 1) * cap, :]


def cold_delta(ids, cold_down, got, cap, rank, first, count, after):
    flat, width = cold_down.shape
    return call(
        functools.partial(cold_delta_kernel, cap, rank, first, count),
        "cold_delta",
        after,
        (ids, cold_down, got),
        vmem(3),
        [sds((cap, width), BF16)] * count,
        2 * flat * count * cap * width,
        2 * flat * width + 2 * count * cap * width,
        scratch=[pltpu.VMEM((count * cap, flat), BF16)],
    )


def cold_in_kernel(peers, cap, rank, ids_ref, down_ref, *rest):
    rx_refs = rest[:peers]
    out_ref, xs_ref = rest[peers:]
    adapters = down_ref.shape[0] // rank
    join(rx_refs, xs_ref, cap)
    id_row = ids_ref[0:1, :]
    group = divide(adapters, 2)
    total = jnp.zeros(out_ref.shape[1:], F32)
    for c in range(adapters // group):
        part = mm(down_ref[c * group * rank : (c + 1) * group * rank, :], xs_ref[...], NT)
        total += fold(part, id_row, float(c * group), group, rank)
    for q in range(out_ref.shape[0]):
        out_ref[q] = total


def cold_in(ids, cold_down, rx, cap, rank, parts, after):
    peers = len(rx)
    flat, width = cold_down.shape
    slots = ids.shape[1]
    return call(
        functools.partial(cold_in_kernel, peers, cap, rank),
        "cold_in",
        after,
        (ids, cold_down, *rx),
        vmem(2 + peers),
        [sds((parts, rank, slots), F32), sds((slots, width), BF16)],
        2 * flat * slots * width,
        2 * (flat + slots) * width,
    )


def cold_down_grad_kernel(rank, ids_ref, xs_ref, got_ref, out_ref, so_ref, wide_ref):
    i = pl.program_id(0)
    group = out_ref.shape[0] // rank

    @pl.when(i == 0)
    def _():
        so_ref[...] = cold_out_of(got_ref, rank, ids_ref.shape[1])

    shifted = ids_ref[0:1, :].astype(I32) - i * group
    spread_rows(wide_ref, so_ref[...], shifted, 0, group)
    out_ref[...] = mm(wide_ref[...], xs_ref[...])


def cold_down_gradient(ids, got, xs, rank, adapters, after):
    slots, width = xs.shape
    flat = adapters * rank
    group = divide(adapters, 4) * rank
    return call(
        functools.partial(cold_down_grad_kernel, rank),
        "cold_down_grad",
        after,
        (ids, xs, got),
        [whole((8, slots)), whole((slots, width)), whole(got.shape)],
        [sds((flat, width), F32)],
        2 * flat * slots * width,
        4 * flat * width + 2 * slots * width,
        out_specs=[pl.BlockSpec((group, width), lambda i: (i, 0))],
        scratch=[pltpu.VMEM((rank, slots), F32), pltpu.VMEM((group, slots), BF16)],
        grid=(flat // group,),
    )


def cold_up_grad_kernel(parts, peers, cap, rank, ids_ref, *rest):
    in_refs = rest[:parts]
    rd_refs = rest[parts : parts + peers]
    out_ref, dys_ref, si_ref, wide_ref = rest[parts + peers :]
    i = pl.program_id(0)
    group = out_ref.shape[0] // rank

    @pl.when(i == 0)
    def _():
        join_last(rd_refs, dys_ref, cap)
        si_ref[...] = scaled(sum((r[0] for r in in_refs[1:]), in_refs[0][0]))

    shifted = ids_ref[0:1, :].astype(I32) - i * group
    spread_rows(wide_ref, si_ref[...], shifted, 0, group)
    out_ref[...] = mm(wide_ref[...], dys_ref[...])


def cold_up_gradient(ids, ins, rd, cap, rank, adapters, after):
    peers = len(rd)
    kv = rd[0].shape[1]
    slots = ids.shape[1]
    flat = adapters * rank
    group = divide(adapters, 2) * rank
    return call(
        functools.partial(cold_up_grad_kernel, len(ins), peers, cap, rank),
        "cold_up_grad",
        after,
        (ids, *ins, *rd),
        [whole((8, slots))] + [whole(v.shape) for v in ins] + [whole(r.shape) for r in rd],
        [sds((flat, kv), F32)],
        2 * flat * slots * kv,
        4 * flat * kv + 2 * slots * kv,
        out_specs=[pl.BlockSpec((group, kv), lambda i: (i, 0))],
        scratch=[
            pltpu.VMEM((slots, kv), BF16),
            pltpu.VMEM((rank, slots), F32),
            pltpu.VMEM((group, slots), BF16),
        ],
        grid=(flat // group,),
    )


def position_matrix(rows_ref, first, count):
    tokens = rows_ref.shape[1]
    as_float = jnp.broadcast_to(rows_ref[2:3, :], (8, tokens)).astype(F32)
    pos = column(as_float).astype(I32) - first
    return jnp.where(lax.broadcasted_iota(I32, (tokens, count), 1) == pos, 1.0, 0.0).astype(BF16)


def local_terms_kernel(near, cap, rank, rows_ref, hd_ref, got_ref, *rest):
    near_refs = rest[:near]
    out_ref, left_ref, right_ref = rest[near:]
    flat, width = hd_ref.shape
    tokens = rows_ref.shape[1]
    total = hot_out_of(got_ref, rank)
    as_float = jnp.broadcast_to(rows_ref[0:1, :], (8, tokens)).astype(F32)
    id_col = column(as_float).astype(I32)
    left_ref[:, 0:flat] = spread_columns(total, id_col, flat // rank)
    left_ref[:, flat : flat + near * cap] = position_matrix(rows_ref, 0, near * cap)
    step = divide(width, 4)
    for j in range(width // step):
        at = slice(j * step, (j + 1) * step)
        right_ref[0:flat, :] = hd_ref[:, at]
        for k in range(near):
            right_ref[flat + k * cap : flat + (k + 1) * cap, :] = near_refs[k][:, at]
        out_ref[:, at] = mm(left_ref[...], right_ref[...]).astype(BF16)


def local_terms(rows, hot_down, got, nears, cap, rank, after):
    flat, width = hot_down.shape
    tokens = rows.shape[1]
    near = len(nears)
    depth = flat + near * cap
    return call(
        functools.partial(local_terms_kernel, near, cap, rank),
        "local_terms",
        after,
        (rows, hot_down, got, *nears),
        vmem(3 + near),
        [sds((tokens, width), BF16)],
        2 * tokens * width * depth,
        2 * width * (tokens + depth),
        scratch=[
            pltpu.VMEM((tokens, depth), BF16),
            pltpu.VMEM((depth, divide(width, 4)), BF16),
        ],
    )


def base_kernel(w_ref, local_ref, dy_ref, out_ref):
    width = w_ref.shape[0]
    step = divide(width, 4)
    for j in range(width // step):
        at = slice(j * step, (j + 1) * step)
        out_ref[:, at] = mm(dy_ref[...], w_ref[at, :], NT) + local_ref[:, at].astype(F32)


def base(weight, local, dy, after):
    width, kv_all = weight.shape
    tokens = local.shape[0]
    return call(
        base_kernel,
        "base",
        after,
        (weight, local, dy),
        vmem(3),
        [sds((tokens, width), F32)],
        2 * tokens * width * kv_all,
        2 * width * kv_all + 6 * tokens * width,
    )


def final_kernel(first, cap, far, rows_ref, base_ref, *rest):
    far_refs = rest[:far]
    out_ref, place_ref, far_ref, held_ref, sems = rest[far:]
    tokens, width = base_ref.shape
    join(far_refs, far_ref, cap)
    place_ref[...] = position_matrix(rows_ref, first * cap, far * cap)
    step = divide(tokens, 4)
    count = tokens // step
    copies = []
    for i in range(count):
        at = slice(i * step, (i + 1) * step)
        if i >= 2:
            copies[i - 2].wait()
        held_ref[i % 2] = (base_ref[at, :] + mm(place_ref[at, :], far_ref[...])).astype(BF16)
        copy = pltpu.make_async_copy(
            held_ref.at[i % 2], out_ref.at[pl.ds(i * step, step)], sems.at[i % 2]
        )
        copy.start()
        copies.append(copy)
    for copy in copies[-2:]:
        copy.wait()


def final(rows, base_sum, fars, first, cap, after):
    tokens, width = base_sum.shape
    far = len(fars)
    return call(
        functools.partial(final_kernel, first, cap, far),
        "final",
        after,
        (rows, base_sum, *fars),
        vmem(2 + far),
        [sds((tokens, width), BF16)],
        2 * tokens * width * far * cap,
        6 * tokens * width,
        out_specs=anywhere(1),
        scratch=[
            pltpu.VMEM((tokens, far * cap), BF16),
            pltpu.VMEM((far * cap, width), BF16),
            pltpu.VMEM((2, divide(tokens, 4), width), BF16),
            pltpu.SemaphoreType.DMA((2,)),
        ],
    )


def swap(value, axis, k):
    count = lax.axis_size(axis)
    return lax.ppermute(value, axis, [(i, i ^ k) for i in range(count)])


def over_tensor(part, parts):
    return [part] + [swap(part, "tensor", k) for k in range(1, parts)]


def shards(
    tokens_in,
    grad_out,
    value_weight,
    token_adapter,
    adapter_home,
    cold_down,
    cold_up,
    hot_down,
    hot_up,
):
    peers = lax.axis_size("dp")
    parts = lax.axis_size("tensor")
    tokens, width = tokens_in.shape
    kv = grad_out.shape[1]
    cap = tokens // (2 * peers)
    cold_here, rank, _ = cold_down.shape
    hot = hot_down.shape[0]
    hot_here = hot // peers
    near = 2
    flat_cold_down = cold_down.reshape(cold_here * rank, width)
    flat_cold_up = cold_up.reshape(cold_here * rank, kv)
    flat_hot_down = hot_down.reshape(hot * rank, width)
    flat_hot_up = hot_up.reshape(hot * rank, kv)
    me = lax.axis_index("dp").astype(I32).reshape(1)

    dy_all = lax.all_gather(grad_out, "tensor", axis=1, tiled=True)
    sd, rows, pick, x, token = route(
        me, token_adapter, adapter_home, grad_out, tokens_in, peers, cap, cold_here, hot_here
    )
    rd = [sd[0]] + [swap(sd[k], "dp", k) for k in range(1, peers)]
    (hot_part,), token = hot_products(
        rows, x, flat_hot_down, grad_out, flat_hot_up, rank, token
    )
    (pay, ids), token = cold_out(hot_part, flat_cold_up, rd, cap, rank, 1, token)
    sx, token = pack(pick, x, peers, cap, token)
    rx = [sx[0]] + [swap(sx[k], "dp", k) for k in range(1, peers)]
    (got,), token = sum_pieces(over_tensor(pay, parts), token)

    (in_part, xs), token = cold_in(ids, flat_cold_down, rx, cap, rank, 1, token)
    ins = over_tensor(in_part, parts)
    (keep, send), token = hot_grads(rows, x, grad_out, got, rank, hot, peers, token)
    mate = swap(send, "dp", 1)
    near_delta, token = cold_delta(ids, flat_cold_down, got, cap, rank, 0, near, token)
    near_back = [near_delta[0]] + [swap(near_delta[k], "dp", k) for k in range(1, near)]
    height = hot_here * rank
    aways, token = hot_away(keep, mate, height, peers // 2 - 1, token)
    aways = [swap(aways[c - 1], "dp", 2 * c) for c in range(1, peers // 2)]
    far_delta, token = cold_delta(ids, flat_cold_down, got, cap, rank, near, peers - near, token)
    far_back = [swap(far_delta[k - near], "dp", k) for k in range(near, peers)]
    (local,), token = local_terms(rows, flat_hot_down, got, near_back, cap, rank, token)

    (cold_down_grad,), token = cold_down_gradient(ids, got, xs, rank, cold_here, token)
    (cold_up_grad,), token = cold_up_gradient(ids, ins, rd, cap, rank, cold_here, token)

    (base_sum,), token = base(value_weight, local, dy_all, token)
    (hot_down_grad, hot_up_grad), token = hot_final(keep, mate, aways, width, height, token)
    (input_gradient,), token = final(rows, base_sum, far_back, near, cap, token)
    return (
        input_gradient,
        cold_down_grad.reshape(cold_here, rank, width),
        cold_up_grad.reshape(cold_here, rank, kv),
        hot_down_grad.reshape(hot_here, rank, width),
        hot_up_grad.reshape(hot_here, rank, kv),
    )


def solution(mesh):
    in_specs = (
        P(("groups", "dp"), "tensor"),
        P(("groups", "dp"), "tensor"),
        P("tensor", None),
        P(("groups", "dp")),
        P("groups"),
        P(("groups", "dp"), None, "tensor"),
        P(("groups", "dp"), None, "tensor"),
        P("groups", None, "tensor"),
        P("groups", None, "tensor"),
    )
    out_specs = (
        P(("groups", "dp"), "tensor"),
        P(("groups", "dp"), None, "tensor"),
        P(("groups", "dp"), None, "tensor"),
        P(("groups", "dp"), None, "tensor"),
        P(("groups", "dp"), None, "tensor"),
    )
    return jax.shard_map(shards, mesh=mesh, in_specs=in_specs, out_specs=out_specs, check_vma=False)
```

```python
import functools

import jax
import jax.numpy as jnp
from jax import lax
from jax.experimental import pallas as pl
from jax.experimental.pallas import tpu as pltpu
from jax.sharding import PartitionSpec as P

ADAPTER_SCALE = 2.0
VMEM_LIMIT = 16 * 1024 * 1024
COST_SCALE = 0.3
ROUTE_MOVED = 400
BF16 = jnp.bfloat16
F32 = jnp.float32
I32 = jnp.int32
NN = (((1,), (0,)), ((), ()))
NT = (((1,), (1,)), ((), ()))


def mm(a, b, dims=NN):
    return lax.dot_general(a, b, dims, preferred_element_type=F32)


def sds(shape, dtype):
    return jax.ShapeDtypeStruct(shape, dtype)


def whole(shape):
    return pl.BlockSpec(shape, lambda *_: (0,) * len(shape))


def vmem(count):
    return [pl.BlockSpec(memory_space=pltpu.VMEM)] * count


def smem():
    return pl.BlockSpec(memory_space=pltpu.SMEM)


def hbm(count):
    return [pl.BlockSpec(memory_space=pltpu.HBM)] * count


def anywhere(count):
    return [pl.BlockSpec(memory_space=pl.ANY)] * count


def params():
    return pltpu.CompilerParams(vmem_limit_bytes=VMEM_LIMIT)


def cost(flops, moved):
    return pl.CostEstimate(
        flops=int(COST_SCALE * flops), bytes_accessed=int(COST_SCALE * moved), transcendentals=0
    )


def join(refs, into, rows):
    for k, ref in enumerate(refs):
        into[k * rows : (k + 1) * rows, :] = ref[0:rows, 0 : into.shape[1]]


def join_last(refs, into, rows):
    for k, ref in enumerate(refs):
        into[k * rows : (k + 1) * rows, :] = ref[0:rows, ref.shape[1] - into.shape[1] :]


TOKEN = (8, 128)


def call(body, name, after, args, in_specs, out_shape, flops, moved, out_specs=None, scratch=(), grid=None):
    taken, given = len(args), len(out_shape)
    chained = [] if after is None else [after]

    def kernel(*refs):
        outs = refs[taken + len(chained) :]
        body(*refs[:taken], *outs[:given], *outs[given + 1 :])
        outs[given][...] = jnp.zeros(TOKEN, F32)

    more = {} if grid is None else {"grid": grid}
    results = pl.pallas_call(
        kernel,
        in_specs=list(in_specs) + anywhere(len(chained)),
        out_specs=list(out_specs or vmem(given)) + (vmem(1) if grid is None else [whole(TOKEN)]),
        out_shape=list(out_shape) + [sds(TOKEN, F32)],
        scratch_shapes=list(scratch),
        compiler_params=params(),
        cost_estimate=cost(flops, moved),
        name=name,
        **more,
    )(*args, *chained)
    return results[:given], results[given]


def divide(total, parts):
    return total // parts if total % parts == 0 else total


def pieces_of(total, parts=4):
    step = divide(total, parts)
    return [slice(k * step, (k + 1) * step) for k in range(total // step)]


def column(row_8):
    return jnp.transpose(row_8)[:, 0:1]


def spread_columns(scaled_t, id_col, adapters):
    rank = scaled_t.shape[0]
    count = scaled_t.shape[1]
    scaled = jnp.transpose(scaled_t).astype(BF16)
    width = adapters * rank
    lane = lax.broadcasted_iota(I32, (rank, width), 1)
    sub = lax.broadcasted_iota(I32, (rank, width), 0)
    tile = jnp.where(lax.rem(lane, rank) == sub, 1.0, 0.0).astype(BF16)
    tiled = mm(scaled, tile)
    own = lax.div(lax.broadcasted_iota(I32, (count, width), 1), rank)
    return jnp.where(own == id_col, tiled, 0.0).astype(BF16)


def spread_rows(out_ref, scaled_t, id_row, first, adapters):
    rank = scaled_t.shape[0]
    for a in range(adapters):
        out_ref[a * rank : (a + 1) * rank, :] = jnp.where(
            id_row == first + a, scaled_t, 0.0
        ).astype(BF16)


def fold(product, id_row, first, adapters, rank):
    total = jnp.zeros((rank, product.shape[1]), F32)
    for a in range(adapters):
        total += jnp.where(id_row == first + a, product[a * rank : (a + 1) * rank, :], 0.0)
    return total


def scaled(total):
    return (ADAPTER_SCALE * total).astype(BF16).astype(F32)


def route_kernel(peers, cap, cold_here, hot_here, me_ref, adapter_in, home_in, dy_in, *rest):
    sd_refs = rest[:peers]
    rows_ref, pick_ref, adapter_ref, home_ref, dy_ref, sems = rest[peers:]
    pairs = ((adapter_in, adapter_ref), (home_in, home_ref), (dy_in, dy_ref))
    loads = [pltpu.make_async_copy(a, b, sems.at[n]) for n, (a, b) in enumerate(pairs)]
    for load in loads:
        load.start()
    adapters = home_ref.shape[1]
    tokens = adapter_ref.shape[1]
    slots = peers * cap
    loads[0].wait()
    loads[1].wait()
    me = me_ref[0]
    adapter = adapter_ref[...]
    home = home_ref[...]
    sub8 = lax.broadcasted_iota(I32, (8, adapters), 0)
    digits = jnp.where(
        sub8 == 0, lax.shift_right_logical(home, 5), jnp.where(sub8 == 1, home & 31, 0)
    ).astype(F32).astype(BF16)
    onehot = jnp.where(
        lax.broadcasted_iota(I32, (adapters, tokens), 0) == adapter, 1.0, 0.0
    ).astype(BF16)
    found = mm(digits, onehot).astype(I32)
    row = found[0:1, :] * 32 + found[1:2, :]
    has = adapter < adapters
    cold_total = cold_here * peers
    cold = has & (row < cold_total)
    hot = has & (row >= cold_total)
    dest = jnp.zeros_like(row)
    hot_row = row - cold_total
    hot_dest = jnp.zeros_like(row)
    for p in range(1, peers):
        dest += jnp.where(row >= p * cold_here, 1, 0)
        hot_dest += jnp.where(hot_row >= p * hot_here, 1, 0)
    dest = jnp.minimum(dest, peers - 1)
    local = row - dest * cold_here
    turn = dest ^ me
    height = max(8, peers)
    hits = jnp.where((lax.broadcasted_iota(I32, (height, tokens), 0) == turn) & cold, 1, 0)
    running = hits
    lane = lax.broadcasted_iota(I32, (height, tokens), 1)
    step = 1
    while step < tokens:
        running += jnp.where(lane >= step, pltpu.roll(running, step, 1), 0)
        step *= 2
    within = jnp.sum(hits * (running - 1), axis=0, keepdims=True)
    position = jnp.where(cold, turn * cap + within, slots)
    hot_nat = jnp.where(hot, hot_row, hot_here * peers)
    hot_turn = jnp.where(
        hot,
        (hot_dest ^ me) * hot_here + hot_row - hot_dest * hot_here,
        hot_here * peers,
    )
    sub = lax.broadcasted_iota(I32, (8, tokens), 0)
    rows_ref[...] = jnp.where(
        sub == 0, hot_nat, jnp.where(sub == 1, hot_turn, jnp.where(sub == 2, position, 0))
    )
    pick_ref[...] = jnp.where(
        lax.broadcasted_iota(I32, (slots, tokens), 0) == position, 1.0, 0.0
    ).astype(BF16)
    loads[2].wait()
    packed = mm(pick_ref[...], dy_ref[...]).astype(BF16)
    ids = mm(jnp.broadcast_to(local.astype(F32), (16, tokens)).astype(BF16), pick_ref[...], NT)
    for k in range(peers):
        sd_refs[k][0:cap, :] = packed[k * cap : (k + 1) * cap, :]
        sd_refs[k][cap : cap + 16, :] = jnp.zeros((16, sd_refs[k].shape[1]), BF16)
        sd_refs[k][cap : cap + 16, 0:cap] = ids[:, k * cap : (k + 1) * cap].astype(BF16)


def route(me, token_adapter, adapter_home, dy, peers, cap, cold_here, hot_here):
    tokens, kv = dy.shape
    slots = peers * cap
    outs, token = call(
        functools.partial(route_kernel, peers, cap, cold_here, hot_here),
        "route",
        None,
        (me, token_adapter.reshape(1, -1), adapter_home.reshape(1, -1), dy),
        [smem()] + hbm(3),
        [sds((cap + 16, kv), BF16)] * peers
        + [sds((8, tokens), I32), sds((slots, tokens), BF16)],
        2 * slots * tokens * kv,
        ROUTE_MOVED * tokens * kv,
        scratch=[
            pltpu.VMEM((1, tokens), I32),
            pltpu.VMEM((1, adapter_home.shape[0]), I32),
            pltpu.VMEM((tokens, kv), BF16),
            pltpu.SemaphoreType.DMA((3,)),
        ],
    )
    return outs[:peers], *outs[peers:], token


def pack_kernel(first, cap, pick_ref, x_ref, *out_refs):
    rows = slice(first * cap, (first + len(out_refs)) * cap)
    for at in pieces_of(x_ref.shape[1]):
        packed = mm(pick_ref[rows, :], x_ref[:, at]).astype(BF16)
        for k, ref in enumerate(out_refs):
            ref[:, at] = packed[k * cap : (k + 1) * cap, :]


def pack(pick, x, cap, first, count, after):
    tokens, width = x.shape
    return call(
        functools.partial(pack_kernel, first, cap),
        "pack",
        after,
        (pick, x),
        vmem(2),
        [sds((cap, width), BF16)] * count,
        2 * count * cap * tokens * width,
        2 * (tokens + count * cap) * width,
    )


def hot_products_kernel(rank, rows_ref, x_ref, hd_ref, dy_ref, hu_ref, out_ref):
    hot = hd_ref.shape[0] // rank
    tokens = x_ref.shape[0]
    half = divide(tokens, 2)
    for c in range(tokens // half):
        at = slice(c * half, (c + 1) * half)
        row = rows_ref[0:1, at]
        out_ref[0:rank, at] = fold(mm(hu_ref[...], dy_ref[at, :], NT), row, 0, hot, rank)
        out_ref[rank : 2 * rank, at] = fold(mm(hd_ref[...], x_ref[at, :], NT), row, 0, hot, rank)


def hot_products(rows, x, hot_down, dy, hot_up, rank, after):
    tokens, width = x.shape
    flat = hot_down.shape[0]
    kv = dy.shape[1]
    return call(
        functools.partial(hot_products_kernel, rank),
        "hot_products",
        after,
        (rows, x, hot_down, dy, hot_up),
        vmem(5),
        [sds((2 * rank, tokens), F32)],
        2 * flat * tokens * (width + kv),
        2 * (tokens + flat) * width,
    )


def cold_out_kernel(peers, cap, rank, hot_ref, up_ref, _, *rest):
    rd_refs = rest[:peers]
    pay_ref, ids_ref, dys_ref = rest[peers:]
    adapters = up_ref.shape[0] // rank
    slots = peers * cap
    join_last(rd_refs, dys_ref, cap)
    kv = up_ref.shape[1]
    ids = [
        r[cap : cap + 16, r.shape[1] - kv : r.shape[1] - kv + cap].astype(F32)[0:8]
        for r in rd_refs
    ]
    ids_8 = jnp.concatenate(ids, axis=1)
    ids_ref[...] = ids_8
    id_row = ids_8[0:1, :]
    group = divide(adapters, 8)
    total = jnp.zeros((rank, slots), F32)
    for c in range(adapters // group):
        part = mm(up_ref[c * group * rank : (c + 1) * group * rank, :], dys_ref[...], NT)
        total += fold(part, id_row, float(c * group), group, rank)
    half = rank // 2
    folded = jnp.concatenate([total[0:half], total[half:rank]], axis=1)
    piece = pay_ref.shape[2]
    for q in range(pay_ref.shape[0]):
        at = slice(q * piece, (q + 1) * piece)
        pay_ref[q, 0 : 2 * rank, :] = hot_ref[:, at]
        pay_ref[q, 2 * rank : 2 * rank + half, :] = folded[:, at]


def cold_out(hot_part, cold_up, before, rd, cap, rank, parts, after):
    peers = len(rd)
    flat, kv = cold_up.shape
    slots = peers * cap
    tokens = hot_part.shape[1]
    return call(
        functools.partial(cold_out_kernel, peers, cap, rank),
        "cold_out",
        after,
        (hot_part, cold_up, before, *rd),
        vmem(2) + anywhere(1) + vmem(peers),
        [sds((parts, 2 * rank + rank // 2, tokens // parts), F32), sds((8, slots), F32), sds((slots, kv), BF16)],
        2 * flat * slots * kv,
        2 * (flat + slots) * kv,
    )


def sum_pieces_kernel(parts, dy_ref, next_ref, *refs):
    pay_refs = refs[:parts]
    out_ref, *pair_refs = refs[parts:]
    total = pay_refs[0][0]
    for ref in pay_refs[1:]:
        total += ref[0]
    filled, width = out_ref.shape[1:]
    total = (ADAPTER_SCALE * total).astype(BF16).astype(F32)
    rest = jnp.zeros((filled - total.shape[0], width), F32)
    out_ref[0] = jnp.concatenate([total, rest], axis=0).astype(BF16)
    kv = dy_ref.shape[1]
    first = 0
    for ref in pair_refs:
        at = slice(first, first + ref.shape[0])
        first += ref.shape[0]
        ref[:, 0:kv] = dy_ref[at, :]
        ref[:, kv:] = next_ref[at, :]


def sum_pieces(pays, dy, dy_next, cuts, after):
    _, height, width = pays[0].shape
    filled = -(-height // 16) * 16
    return call(
        functools.partial(sum_pieces_kernel, len(pays)),
        "sum_pieces",
        after,
        (dy, dy_next, *pays),
        vmem(2 + len(pays)),
        [sds((1, filled, width), BF16)] + [sds((rows, 2 * dy.shape[1]), BF16) for rows in cuts],
        len(pays) * pays[0].size,
        4 * len(pays) * pays[0].size,
    )


def gathered(got_ref, first, last):
    return jnp.concatenate(
        [got_ref[q, first:last, :].astype(F32) for q in range(got_ref.shape[0])], axis=1
    )


def hot_out_of(got_ref, rank):
    return gathered(got_ref, 0, rank)


def hot_in_of(got_ref, rank):
    return gathered(got_ref, rank, 2 * rank)


def cold_out_of(got_ref, rank, slots):
    half = rank // 2
    folded = gathered(got_ref, 2 * rank, got_ref.shape[1])[0:half]
    return jnp.concatenate([folded[:, 0:slots], folded[:, slots : 2 * slots]], axis=0)


def hot_grads_kernel(peers, rank, hot, rows_ref, x_ref, dy_ref, got_ref, _, keep_ref, *rest):
    send_refs, wide_ref = rest[:-1], rest[-1]
    width = x_ref.shape[1]
    kv = dy_ref.shape[1]
    block = hot // peers * rank

    def put(product, column):
        for k in range(peers):
            piece = product[k * block : (k + 1) * block, :]
            at = slice((k // 2) * block, (k // 2 + 1) * block)
            if k % 2 == 0:
                keep_ref[at, column] = piece
            else:
                send_refs[k // 2][:, column] = piece.astype(BF16)

    turn = rows_ref[1:2, :]
    spread_rows(wide_ref, hot_in_of(got_ref, rank), turn, 0, hot)
    put(mm(wide_ref[...], dy_ref[...]), slice(width, width + kv))
    spread_rows(wide_ref, hot_out_of(got_ref, rank), turn, 0, hot)
    step = divide(width, 4)
    for j in range(width // step):
        at = slice(j * step, (j + 1) * step)
        put(mm(wide_ref[...], x_ref[:, at]), at)


def hot_grads(rows, x, dy, got, before, rank, hot, peers, after):
    tokens, width = x.shape
    kv = dy.shape[1]
    flat = hot * rank
    half = flat // 2
    return call(
        functools.partial(hot_grads_kernel, peers, rank, hot),
        "hot_grads",
        after,
        (rows, x, dy, got, before),
        vmem(4) + anywhere(1),
        [sds((half, width + kv), F32)]
        + [sds((flat // peers, width + kv), BF16)] * (peers // 2),
        2 * flat * tokens * (width + kv),
        2 * tokens * width + 6 * half * width,
        scratch=[pltpu.VMEM((flat, tokens), BF16)],
    )


def hot_away_kernel(count, keep_ref, *rest):
    for c in range(count):
        mate_ref, out_ref = rest[c], rest[count + c]
        height = out_ref.shape[0]
        at = slice((c + 1) * height, (c + 2) * height)
        out_ref[...] = (keep_ref[at, :] + mate_ref[...].astype(F32)).astype(BF16)


def hot_away(keep, mates, after):
    count = len(mates)
    return call(
        functools.partial(hot_away_kernel, count),
        "hot_away",
        after,
        (keep, *mates),
        vmem(1 + count),
        [sds(mates[0].shape, BF16)] * count,
        keep.size,
        8 * keep.size,
    )


def hot_final_kernel(keep_ref, mate_ref, *rest):
    down_ref, up_ref = rest[-2:]
    height, width = down_ref.shape
    total = keep_ref[0:height, :] + mate_ref[0:height, :].astype(F32)
    for ref in rest[:-2]:
        total += ref[...].astype(F32)
    down_ref[...] = total[:, 0:width]
    up_ref[...] = total[:, width:]


def hot_final(keep, mate, fars, width, height, after):
    return call(
        hot_final_kernel,
        "hot_final",
        after,
        (keep, mate, *fars),
        vmem(2 + len(fars)),
        [sds((height, width), F32), sds((height, keep.shape[1] - width), F32)],
        keep.size,
        4 * keep.size,
    )


def cold_delta_kernel(cap, rank, first, count, ids_ref, down_ref, got_ref, *rest):
    out_refs = rest[:count]
    wide_ref = rest[count]
    flat, width = down_ref.shape
    lo, hi = first * cap, (first + count) * cap
    total = cold_out_of(got_ref, rank, ids_ref.shape[1])[:, lo:hi]
    id_col = column(ids_ref[:, lo:hi]).astype(I32)
    wide_ref[...] = spread_columns(total, id_col, flat // rank)
    step = divide(width, 4)
    for j in range(width // step):
        at = slice(j * step, (j + 1) * step)
        delta = mm(wide_ref[...], down_ref[:, at]).astype(BF16)
        for k in range(count):
            out_refs[k][:, at] = delta[k * cap : (k + 1) * cap, :]


def cold_delta(ids, cold_down, got, cap, rank, first, count, after):
    flat, width = cold_down.shape
    return call(
        functools.partial(cold_delta_kernel, cap, rank, first, count),
        "cold_delta",
        after,
        (ids, cold_down, got),
        vmem(3),
        [sds((cap, width), BF16)] * count,
        2 * flat * count * cap * width,
        2 * flat * width + 2 * count * cap * width,
        scratch=[pltpu.VMEM((count * cap, flat), BF16)],
    )


def cold_in_kernel(peers, cap, rank, ids_ref, down_ref, *rest):
    rx_refs = rest[:peers]
    out_ref, xs_ref = rest[peers:]
    adapters = down_ref.shape[0] // rank
    join(rx_refs, xs_ref, cap)
    id_row = ids_ref[0:1, :]
    group = divide(adapters, 2)
    total = jnp.zeros(out_ref.shape[1:], F32)
    for c in range(adapters // group):
        part = mm(down_ref[c * group * rank : (c + 1) * group * rank, :], xs_ref[...], NT)
        total += fold(part, id_row, float(c * group), group, rank)
    for q in range(out_ref.shape[0]):
        out_ref[q] = total


def cold_in(ids, cold_down, rx, cap, rank, parts, after):
    peers = len(rx)
    flat, width = cold_down.shape
    slots = ids.shape[1]
    return call(
        functools.partial(cold_in_kernel, peers, cap, rank),
        "cold_in",
        after,
        (ids, cold_down, *rx),
        vmem(2 + peers),
        [sds((parts, rank, slots), F32), sds((slots, width), BF16)],
        2 * flat * slots * width,
        2 * (flat + slots) * width,
    )


def cold_down_grad_kernel(rank, ids_ref, xs_ref, got_ref, out_ref, so_ref, wide_ref):
    i = pl.program_id(0)
    group = out_ref.shape[0] // rank

    @pl.when(i == 0)
    def _():
        so_ref[...] = cold_out_of(got_ref, rank, ids_ref.shape[1])

    shifted = ids_ref[0:1, :].astype(I32) - i * group
    spread_rows(wide_ref, so_ref[...], shifted, 0, group)
    out_ref[...] = mm(wide_ref[...], xs_ref[...])


def cold_down_gradient(ids, got, xs, rank, adapters, after):
    slots, width = xs.shape
    flat = adapters * rank
    group = divide(adapters, 4) * rank
    return call(
        functools.partial(cold_down_grad_kernel, rank),
        "cold_down_grad",
        after,
        (ids, xs, got),
        [whole((8, slots)), whole((slots, width)), whole(got.shape)],
        [sds((flat, width), F32)],
        2 * flat * slots * width,
        4 * flat * width + 2 * slots * width,
        out_specs=[pl.BlockSpec((group, width), lambda i: (i, 0))],
        scratch=[pltpu.VMEM((rank, slots), F32), pltpu.VMEM((group, slots), BF16)],
        grid=(flat // group,),
    )


def cold_up_grad_kernel(rank, ids_ref, dys_ref, *rest):
    in_refs = rest[:-3]
    out_ref, si_ref, wide_ref = rest[-3:]
    i = pl.program_id(0)
    group = out_ref.shape[0] // rank

    @pl.when(i == 0)
    def _():
        si_ref[...] = scaled(sum((r[0] for r in in_refs[1:]), in_refs[0][0]))

    shifted = ids_ref[0:1, :].astype(I32) - i * group
    spread_rows(wide_ref, si_ref[...], shifted, 0, group)
    out_ref[...] = mm(wide_ref[...], dys_ref[...])


def cold_up_gradient(ids, ins, dys, rank, adapters, after):
    slots, kv = dys.shape
    flat = adapters * rank
    group = divide(adapters, 2) * rank

    def body(*refs):
        cold_up_grad_kernel(rank, *refs)

    return call(
        body,
        "cold_up_grad",
        after,
        (ids, dys, *ins),
        [whole((8, slots)), whole((slots, kv))] + [whole(v.shape) for v in ins],
        [sds((flat, kv), F32)],
        2 * flat * slots * kv,
        4 * flat * kv + 2 * slots * kv,
        out_specs=[pl.BlockSpec((group, kv), lambda i: (i, 0))],
        scratch=[pltpu.VMEM((rank, slots), F32), pltpu.VMEM((group, slots), BF16)],
        grid=(flat // group,),
    )


def position_matrix(rows_ref, first, count):
    tokens = rows_ref.shape[1]
    as_float = jnp.broadcast_to(rows_ref[2:3, :], (8, tokens)).astype(F32)
    pos = column(as_float).astype(I32) - first
    return jnp.where(lax.broadcasted_iota(I32, (tokens, count), 1) == pos, 1.0, 0.0).astype(BF16)


def local_terms_kernel(near, cap, rank, rows_ref, hd_ref, got_ref, *rest):
    near_refs = rest[:near]
    out_ref, place_ref, left_ref, right_ref = rest[near:]
    flat, width = hd_ref.shape
    tokens = rows_ref.shape[1]
    total = hot_out_of(got_ref, rank)
    as_float = jnp.broadcast_to(rows_ref[0:1, :], (8, tokens)).astype(F32)
    id_col = column(as_float).astype(I32)
    left_ref[:, 0:flat] = spread_columns(total, id_col, flat // rank)
    left_ref[:, flat : flat + near * cap] = position_matrix(rows_ref, 0, near * cap)
    place_ref[...] = position_matrix(rows_ref, near * cap, place_ref.shape[1])
    step = divide(width, 4)
    for j in range(width // step):
        at = slice(j * step, (j + 1) * step)
        right_ref[0:flat, :] = hd_ref[:, at]
        for k in range(near):
            right_ref[flat + k * cap : flat + (k + 1) * cap, :] = near_refs[k][:, at]
        out_ref[:, at] = mm(left_ref[...], right_ref[...]).astype(BF16)


def local_terms(rows, hot_down, got, nears, far, cap, rank, after):
    flat, width = hot_down.shape
    tokens = rows.shape[1]
    near = len(nears)
    depth = flat + near * cap
    return call(
        functools.partial(local_terms_kernel, near, cap, rank),
        "local_terms",
        after,
        (rows, hot_down, got, *nears),
        vmem(3 + near),
        [sds((tokens, width), BF16), sds((tokens, far * cap), BF16)],
        2 * tokens * width * depth,
        2 * width * (tokens + depth),
        scratch=[
            pltpu.VMEM((tokens, depth), BF16),
            pltpu.VMEM((depth, divide(width, 4)), BF16),
        ],
    )


def base_kernel(groups, t_ref, w_ref, local_ref, part_ref, *rest):
    out_ref, passed_ref, dy_ref = rest[-3:]
    passed_ref[...] = part_ref[...]
    t = t_ref[0]
    first, used = 0, 0
    for count in groups:
        refs = rest[used : used + count]
        used += count
        kv = refs[0].shape[1] // 2
        rows = slice(first, first + refs[0].shape[0])
        first += refs[0].shape[0]
        k = 0
        for ref in refs:
            for c in range(ref.shape[1] // kv):
                lanes = pl.ds(pl.multiple_of((t ^ k) * kv, kv), kv)
                dy_ref[rows, lanes] = ref[:, c * kv : (c + 1) * kv]
                k += 1
    for at in pieces_of(w_ref.shape[0]):
        out_ref[:, at] = mm(dy_ref[...], w_ref[at, :], NT) + local_ref[:, at].astype(F32)


def base(t, weight, local, part, dys, after):
    width, kv_all = weight.shape
    tokens = local.shape[0]
    return call(
        functools.partial(base_kernel, [len(blocks) for blocks in dys]),
        "base",
        after,
        (t, weight, local, part, *sum(dys, [])),
        [smem()] + vmem(3 + sum(len(blocks) for blocks in dys)),
        [sds((tokens, width), F32), sds(part.shape, F32)],
        2 * tokens * width * kv_all,
        2 * width * kv_all + 6 * tokens * width,
        scratch=[pltpu.VMEM((tokens, kv_all), BF16)],
    )


def final_kernel(cap, far, place_ref, base_ref, *rest):
    far_refs = rest[:far]
    out_ref, far_ref, held_ref, sems = rest[far:]
    for k, ref in enumerate(far_refs):
        far_ref[k * cap : (k + 1) * cap, :] = ref[...]
    copies = []
    for i, at in enumerate(pieces_of(base_ref.shape[0])):
        held_ref[at, :] = (base_ref[at, :] + mm(place_ref[at, :], far_ref[...])).astype(BF16)
        copies.append(pltpu.make_async_copy(held_ref.at[at], out_ref.at[at], sems.at[i]))
        copies[-1].start()
    for copy in copies:
        copy.wait()


def final(place, base_sum, fars, cap, after):
    tokens, width = base_sum.shape
    far = len(fars)
    return call(
        functools.partial(final_kernel, cap, far),
        "final",
        after,
        (place, base_sum, *fars),
        vmem(2 + far),
        [sds((tokens, width), BF16)],
        2 * tokens * width * far * cap,
        6 * tokens * width,
        out_specs=anywhere(1),
        scratch=[
            pltpu.VMEM((far * cap, width), BF16),
            pltpu.VMEM((tokens, width), BF16),
            pltpu.SemaphoreType.DMA((4,)),
        ],
    )


def swap(value, axis, k):
    count = lax.axis_size(axis)
    return lax.ppermute(value, axis, [(i, i ^ k) for i in range(count)])


def gather_rest(pair, parts):
    blocks, held = [pair], 2
    while held < parts:
        together = blocks[0] if len(blocks) == 1 else jnp.concatenate(blocks, axis=1)
        blocks.append(swap(together, "tensor", held))
        held *= 2
    return blocks


def over_tensor(part, parts):
    return [part] + [swap(part, "tensor", k) for k in range(1, parts)]


def shards(
    tokens_in,
    grad_out,
    value_weight,
    token_adapter,
    adapter_home,
    cold_down,
    cold_up,
    hot_down,
    hot_up,
):
    peers = lax.axis_size("dp")
    parts = lax.axis_size("tensor")
    tokens, width = tokens_in.shape
    kv = grad_out.shape[1]
    cap = tokens // (2 * peers)
    cold_here, rank, _ = cold_down.shape
    hot = hot_down.shape[0]
    hot_here = hot // peers
    near = 2
    flat_cold_down = cold_down.reshape(cold_here * rank, width)
    flat_cold_up = cold_up.reshape(cold_here * rank, kv)
    flat_hot_down = hot_down.reshape(hot * rank, width)
    flat_hot_up = hot_up.reshape(hot * rank, kv)
    me = lax.axis_index("dp").astype(I32).reshape(1)

    t = lax.axis_index("tensor").astype(I32).reshape(1)
    dy_next = swap(grad_out, "tensor", 1)
    x = tokens_in
    sd, rows, pick, token = route(
        me, token_adapter, adapter_home, grad_out, peers, cap, cold_here, hot_here
    )
    rd = [sd[0]] + [swap(sd[k], "dp", k) for k in range(1, peers)]
    (hot_part,), token = hot_products(
        rows, x, flat_hot_down, grad_out, flat_hot_up, rank, token
    )
    (pay, ids, held_dy), token = cold_out(hot_part, flat_cold_up, dy_next, rd, cap, rank, 1, token)
    far_x, token = pack(pick, x, cap, near, peers - near, token)
    far_x = [swap(far_x[k - near], "dp", k) for k in range(near, peers)]
    early = divide(tokens, 4)
    (got, *pairs), token = sum_pieces(
        over_tensor(pay, parts), grad_out, dy_next, (early, tokens - early), token
    )
    dys = [gather_rest(pair, parts) for pair in pairs]
    near_x, token = pack(pick, x, cap, 0, near, token)
    rx = [near_x[0], swap(near_x[1], "dp", 1)] + far_x
    (in_part, xs), token = cold_in(ids, flat_cold_down, rx, cap, rank, 1, token)
    (keep, *sends), token = hot_grads(
        rows, x, grad_out, got, dys[0][-1], rank, hot, peers, token
    )
    mates = [swap(send, "dp", 1) for send in sends]
    near_delta, token = cold_delta(ids, flat_cold_down, got, cap, rank, 0, near, token)
    near_back = [near_delta[0]] + [swap(near_delta[k], "dp", k) for k in range(1, near)]
    height = hot_here * rank
    aways, token = hot_away(keep, mates[1:], token)
    aways = [swap(aways[c - 1], "dp", 2 * c) for c in range(1, peers // 2)]
    far_delta, token = cold_delta(ids, flat_cold_down, got, cap, rank, near, peers - near, token)
    far_back = [swap(far_delta[k - near], "dp", k) for k in range(near, peers)]
    (cold_down_grad,), token = cold_down_gradient(ids, got, xs, rank, cold_here, token)
    (local, place), token = local_terms(
        rows, flat_hot_down, got, near_back, peers - near, cap, rank, token
    )
    (base_sum, passed), token = base(t, value_weight, local, in_part, dys, token)
    ins = over_tensor(passed, parts)
    (hot_down_grad, hot_up_grad), token = hot_final(keep, mates[0], aways, width, height, token)
    (cold_up_grad,), token = cold_up_gradient(ids, ins, held_dy, rank, cold_here, token)
    (input_gradient,), token = final(place, base_sum, far_back, cap, token)
    return (
        input_gradient,
        cold_down_grad.reshape(cold_here, rank, width),
        cold_up_grad.reshape(cold_here, rank, kv),
        hot_down_grad.reshape(hot_here, rank, width),
        hot_up_grad.reshape(hot_here, rank, kv),
    )


def solution(mesh):
    in_specs = (
        P(("groups", "dp"), "tensor"),
        P(("groups", "dp"), "tensor"),
        P("tensor", None),
        P(("groups", "dp")),
        P("groups"),
        P(("groups", "dp"), None, "tensor"),
        P(("groups", "dp"), None, "tensor"),
        P("groups", None, "tensor"),
        P("groups", None, "tensor"),
    )
    out_specs = (
        P(("groups", "dp"), "tensor"),
        P(("groups", "dp"), None, "tensor"),
        P(("groups", "dp"), None, "tensor"),
        P(("groups", "dp"), None, "tensor"),
        P(("groups", "dp"), None, "tensor"),
    )
    return jax.shard_map(shards, mesh=mesh, in_specs=in_specs, out_specs=out_specs, check_vma=False)
```

```python
import functools

import jax
import jax.numpy as jnp
from jax import lax
from jax.experimental import pallas as pl
from jax.experimental.pallas import tpu as pltpu
from jax.sharding import PartitionSpec as P

ADAPTER_SCALE = 2.0
VMEM_LIMIT = 10 * 1024 * 1024
COST_SCALE = 0.3
ROUTE_MOVED = 400
BF16 = jnp.bfloat16
F32 = jnp.float32
I32 = jnp.int32
NN = (((1,), (0,)), ((), ()))
NT = (((1,), (1,)), ((), ()))


def mm(a, b, dims=NN):
    return lax.dot_general(a, b, dims, preferred_element_type=F32)


def sds(shape, dtype):
    return jax.ShapeDtypeStruct(shape, dtype)


def whole(shape):
    return pl.BlockSpec(shape, lambda *_: (0,) * len(shape))


def vmem(count):
    return [pl.BlockSpec(memory_space=pltpu.VMEM)] * count


def smem():
    return pl.BlockSpec(memory_space=pltpu.SMEM)


def hbm(count):
    return [pl.BlockSpec(memory_space=pltpu.HBM)] * count


def anywhere(count):
    return [pl.BlockSpec(memory_space=pl.ANY)] * count


def params():
    return pltpu.CompilerParams(vmem_limit_bytes=VMEM_LIMIT)


def cost(flops, moved):
    return pl.CostEstimate(
        flops=int(COST_SCALE * flops), bytes_accessed=int(COST_SCALE * moved), transcendentals=0
    )


def join(refs, into, rows):
    for k, ref in enumerate(refs):
        into[k * rows : (k + 1) * rows, :] = ref[0:rows, 0 : into.shape[1]]


def join_last(refs, into, rows):
    for k, ref in enumerate(refs):
        into[k * rows : (k + 1) * rows, :] = ref[0:rows, ref.shape[1] - into.shape[1] :]


TOKEN = (8, 128)


def call(body, name, after, args, in_specs, out_shape, flops, moved, out_specs=None, scratch=(), grid=None):
    taken, given = len(args), len(out_shape)
    chained = [] if after is None else [after]

    def kernel(*refs):
        outs = refs[taken + len(chained) :]
        body(*refs[:taken], *outs[:given], *outs[given + 1 :])
        outs[given][...] = jnp.zeros(TOKEN, F32)

    more = {} if grid is None else {"grid": grid}
    results = pl.pallas_call(
        kernel,
        in_specs=list(in_specs) + anywhere(len(chained)),
        out_specs=list(out_specs or vmem(given)) + (vmem(1) if grid is None else [whole(TOKEN)]),
        out_shape=list(out_shape) + [sds(TOKEN, F32)],
        scratch_shapes=list(scratch),
        compiler_params=params(),
        cost_estimate=cost(flops, moved),
        name=name,
        **more,
    )(*args, *chained)
    return results[:given], results[given]


def divide(total, parts):
    return total // parts if total % parts == 0 else total


def pieces_of(total, parts=4):
    step = divide(total, parts)
    return [slice(k * step, (k + 1) * step) for k in range(total // step)]


def column(row_8):
    return jnp.transpose(row_8)[:, 0:1]


def spread_columns(scaled_t, id_col, adapters):
    rank = scaled_t.shape[0]
    count = scaled_t.shape[1]
    scaled = jnp.transpose(scaled_t).astype(BF16)
    width = adapters * rank
    lane = lax.broadcasted_iota(I32, (rank, width), 1)
    sub = lax.broadcasted_iota(I32, (rank, width), 0)
    tile = jnp.where(lax.rem(lane, rank) == sub, 1.0, 0.0).astype(BF16)
    tiled = mm(scaled, tile)
    own = lax.div(lax.broadcasted_iota(I32, (count, width), 1), rank)
    return jnp.where(own == id_col, tiled, 0.0).astype(BF16)


def spread_rows(out_ref, scaled_t, id_row, first, adapters):
    rank = scaled_t.shape[0]
    for a in range(adapters):
        out_ref[a * rank : (a + 1) * rank, :] = jnp.where(
            id_row == first + a, scaled_t, 0.0
        ).astype(BF16)


def fold(product, id_row, first, adapters, rank):
    total = jnp.zeros((rank, product.shape[1]), F32)
    for a in range(adapters):
        total += jnp.where(id_row == first + a, product[a * rank : (a + 1) * rank, :], 0.0)
    return total


def scaled(total):
    return (ADAPTER_SCALE * total).astype(BF16).astype(F32)


def route_kernel(peers, cap, cold_here, hot_here, me_ref, adapter_in, home_in, dy_in, *rest):
    sd_refs = rest[:peers]
    rows_ref, pick_ref, adapter_ref, home_ref, dy_ref, sems = rest[peers:]
    pairs = ((adapter_in, adapter_ref), (home_in, home_ref), (dy_in, dy_ref))
    loads = [pltpu.make_async_copy(a, b, sems.at[n]) for n, (a, b) in enumerate(pairs)]
    for load in loads:
        load.start()
    adapters = home_ref.shape[1]
    tokens = adapter_ref.shape[1]
    slots = peers * cap
    loads[0].wait()
    loads[1].wait()
    me = me_ref[0]
    adapter = adapter_ref[...]
    home = home_ref[...]
    sub8 = lax.broadcasted_iota(I32, (8, adapters), 0)
    digits = jnp.where(
        sub8 == 0, lax.shift_right_logical(home, 5), jnp.where(sub8 == 1, home & 31, 0)
    ).astype(F32).astype(BF16)
    onehot = jnp.where(
        lax.broadcasted_iota(I32, (adapters, tokens), 0) == adapter, 1.0, 0.0
    ).astype(BF16)
    found = mm(digits, onehot).astype(I32)
    row = found[0:1, :] * 32 + found[1:2, :]
    has = adapter < adapters
    cold_total = cold_here * peers
    cold = has & (row < cold_total)
    hot = has & (row >= cold_total)
    dest = jnp.zeros_like(row)
    hot_row = row - cold_total
    hot_dest = jnp.zeros_like(row)
    for p in range(1, peers):
        dest += jnp.where(row >= p * cold_here, 1, 0)
        hot_dest += jnp.where(hot_row >= p * hot_here, 1, 0)
    dest = jnp.minimum(dest, peers - 1)
    local = row - dest * cold_here
    turn = dest ^ me
    height = max(8, peers)
    hits = jnp.where((lax.broadcasted_iota(I32, (height, tokens), 0) == turn) & cold, 1, 0)
    running = hits
    lane = lax.broadcasted_iota(I32, (height, tokens), 1)
    step = 1
    while step < tokens:
        running += jnp.where(lane >= step, pltpu.roll(running, step, 1), 0)
        step *= 2
    within = jnp.sum(hits * (running - 1), axis=0, keepdims=True)
    position = jnp.where(cold, turn * cap + within, slots)
    hot_nat = jnp.where(hot, hot_row, hot_here * peers)
    hot_turn = jnp.where(
        hot,
        (hot_dest ^ me) * hot_here + hot_row - hot_dest * hot_here,
        hot_here * peers,
    )
    sub = lax.broadcasted_iota(I32, (8, tokens), 0)
    rows_ref[...] = jnp.where(
        sub == 0, hot_nat, jnp.where(sub == 1, hot_turn, jnp.where(sub == 2, position, 0))
    )
    pick_ref[...] = jnp.where(
        lax.broadcasted_iota(I32, (slots, tokens), 0) == position, 1.0, 0.0
    ).astype(BF16)
    loads[2].wait()
    packed = mm(pick_ref[...], dy_ref[...]).astype(BF16)
    ids = mm(jnp.broadcast_to(local.astype(F32), (16, tokens)).astype(BF16), pick_ref[...], NT)
    for k in range(peers):
        sd_refs[k][0:cap, :] = packed[k * cap : (k + 1) * cap, :]
        sd_refs[k][cap : cap + 16, :] = jnp.zeros((16, sd_refs[k].shape[1]), BF16)
        sd_refs[k][cap : cap + 16, 0:cap] = ids[:, k * cap : (k + 1) * cap].astype(BF16)


def route(me, token_adapter, adapter_home, dy, peers, cap, cold_here, hot_here):
    tokens, kv = dy.shape
    slots = peers * cap
    outs, token = call(
        functools.partial(route_kernel, peers, cap, cold_here, hot_here),
        "route",
        None,
        (me, token_adapter.reshape(1, -1), adapter_home.reshape(1, -1), dy),
        [smem()] + hbm(3),
        [sds((cap + 16, kv), BF16)] * peers
        + [sds((8, tokens), I32), sds((slots, tokens), BF16)],
        2 * slots * tokens * kv,
        ROUTE_MOVED * tokens * kv,
        scratch=[
            pltpu.VMEM((1, tokens), I32),
            pltpu.VMEM((1, adapter_home.shape[0]), I32),
            pltpu.VMEM((tokens, kv), BF16),
            pltpu.SemaphoreType.DMA((3,)),
        ],
    )
    return outs[:peers], *outs[peers:], token


def pack_kernel(first, cap, pick_ref, x_ref, *out_refs):
    rows = slice(first * cap, (first + len(out_refs)) * cap)
    for at in pieces_of(x_ref.shape[1]):
        packed = mm(pick_ref[rows, :], x_ref[:, at]).astype(BF16)
        for k, ref in enumerate(out_refs):
            ref[:, at] = packed[k * cap : (k + 1) * cap, :]


def pack(pick, x, cap, first, count, after):
    tokens, width = x.shape
    return call(
        functools.partial(pack_kernel, first, cap),
        "pack",
        after,
        (pick, x),
        vmem(2),
        [sds((cap, width), BF16)] * count,
        2 * count * cap * tokens * width,
        2 * (tokens + count * cap) * width,
    )


def hot_products_kernel(rank, rows_ref, x_ref, hd_ref, dy_ref, hu_ref, out_ref):
    hot = hd_ref.shape[0] // rank
    tokens = x_ref.shape[0]
    half = divide(tokens, 2)
    for c in range(tokens // half):
        at = slice(c * half, (c + 1) * half)
        row = rows_ref[0:1, at]
        out_ref[0:rank, at] = fold(mm(hu_ref[...], dy_ref[at, :], NT), row, 0, hot, rank)
        out_ref[rank : 2 * rank, at] = fold(mm(hd_ref[...], x_ref[at, :], NT), row, 0, hot, rank)


def hot_products(rows, x, hot_down, dy, hot_up, rank, after):
    tokens, width = x.shape
    flat = hot_down.shape[0]
    kv = dy.shape[1]
    return call(
        functools.partial(hot_products_kernel, rank),
        "hot_products",
        after,
        (rows, x, hot_down, dy, hot_up),
        vmem(5),
        [sds((2 * rank, tokens), F32)],
        2 * flat * tokens * (width + kv),
        2 * (tokens + flat) * width,
    )


def cold_out_kernel(peers, cap, rank, hot_ref, up_ref, _, *rest):
    rd_refs = rest[:peers]
    pay_ref, ids_ref, dys_ref = rest[peers:]
    adapters = up_ref.shape[0] // rank
    slots = peers * cap
    join_last(rd_refs, dys_ref, cap)
    kv = up_ref.shape[1]
    ids = [
        r[cap : cap + 16, r.shape[1] - kv : r.shape[1] - kv + cap].astype(F32)[0:8]
        for r in rd_refs
    ]
    ids_8 = jnp.concatenate(ids, axis=1)
    ids_ref[...] = ids_8
    id_row = ids_8[0:1, :]
    group = divide(adapters, 8)
    total = jnp.zeros((rank, slots), F32)
    for c in range(adapters // group):
        part = mm(up_ref[c * group * rank : (c + 1) * group * rank, :], dys_ref[...], NT)
        total += fold(part, id_row, float(c * group), group, rank)
    half = rank // 2
    folded = jnp.concatenate([total[0:half], total[half:rank]], axis=1)
    piece = pay_ref.shape[2]
    for q in range(pay_ref.shape[0]):
        at = slice(q * piece, (q + 1) * piece)
        pay_ref[q, 0 : 2 * rank, :] = hot_ref[:, at]
        pay_ref[q, 2 * rank : 2 * rank + half, :] = folded[:, at]


def cold_out(hot_part, cold_up, before, rd, cap, rank, parts, after):
    peers = len(rd)
    flat, kv = cold_up.shape
    slots = peers * cap
    tokens = hot_part.shape[1]
    return call(
        functools.partial(cold_out_kernel, peers, cap, rank),
        "cold_out",
        after,
        (hot_part, cold_up, before, *rd),
        vmem(2) + anywhere(1) + vmem(peers),
        [sds((parts, 2 * rank + rank // 2, tokens // parts), F32), sds((8, slots), F32), sds((slots, kv), BF16)],
        2 * flat * slots * kv,
        2 * (flat + slots) * kv,
    )


def sum_pieces_kernel(parts, dy_ref, next_ref, *refs):
    pay_refs = refs[:parts]
    out_ref, *pair_refs = refs[parts:]
    total = pay_refs[0][0]
    for ref in pay_refs[1:]:
        total += ref[0]
    filled, width = out_ref.shape[1:]
    total = (ADAPTER_SCALE * total).astype(BF16).astype(F32)
    rest = jnp.zeros((filled - total.shape[0], width), F32)
    out_ref[0] = jnp.concatenate([total, rest], axis=0).astype(BF16)
    kv = dy_ref.shape[1]
    first = 0
    for ref in pair_refs:
        at = slice(first, first + ref.shape[0])
        first += ref.shape[0]
        ref[:, 0:kv] = dy_ref[at, :]
        ref[:, kv:] = next_ref[at, :]


def sum_pieces(pays, dy, dy_next, cuts, after):
    _, height, width = pays[0].shape
    filled = -(-height // 16) * 16
    return call(
        functools.partial(sum_pieces_kernel, len(pays)),
        "sum_pieces",
        after,
        (dy, dy_next, *pays),
        vmem(2 + len(pays)),
        [sds((1, filled, width), BF16)] + [sds((rows, 2 * dy.shape[1]), BF16) for rows in cuts],
        len(pays) * pays[0].size,
        4 * len(pays) * pays[0].size,
    )


def gathered(got_ref, first, last):
    return jnp.concatenate(
        [got_ref[q, first:last, :].astype(F32) for q in range(got_ref.shape[0])], axis=1
    )


def hot_out_of(got_ref, rank):
    return gathered(got_ref, 0, rank)


def hot_in_of(got_ref, rank):
    return gathered(got_ref, rank, 2 * rank)


def cold_out_of(got_ref, rank, slots):
    half = rank // 2
    folded = gathered(got_ref, 2 * rank, got_ref.shape[1])[0:half]
    return jnp.concatenate([folded[:, 0:slots], folded[:, slots : 2 * slots]], axis=0)


def hot_grads_kernel(peers, rank, hot, rows_ref, x_ref, dy_ref, got_ref, _, keep_ref, *rest):
    send_refs, wide_ref = rest[:-1], rest[-1]
    width = x_ref.shape[1]
    kv = dy_ref.shape[1]
    block = hot // peers * rank

    def put(product, column):
        for k in range(peers):
            piece = product[k * block : (k + 1) * block, :]
            at = slice((k // 2) * block, (k // 2 + 1) * block)
            if k % 2 == 0:
                keep_ref[at, column] = piece
            else:
                send_refs[k // 2][:, column] = piece.astype(BF16)

    turn = rows_ref[1:2, :]
    spread_rows(wide_ref, hot_in_of(got_ref, rank), turn, 0, hot)
    put(mm(wide_ref[...], dy_ref[...]), slice(width, width + kv))
    spread_rows(wide_ref, hot_out_of(got_ref, rank), turn, 0, hot)
    step = divide(width, 4)
    for j in range(width // step):
        at = slice(j * step, (j + 1) * step)
        put(mm(wide_ref[...], x_ref[:, at]), at)


def hot_grads(rows, x, dy, got, before, rank, hot, peers, after):
    tokens, width = x.shape
    kv = dy.shape[1]
    flat = hot * rank
    half = flat // 2
    return call(
        functools.partial(hot_grads_kernel, peers, rank, hot),
        "hot_grads",
        after,
        (rows, x, dy, got, before),
        vmem(4) + anywhere(1),
        [sds((half, width + kv), F32)]
        + [sds((flat // peers, width + kv), BF16)] * (peers // 2),
        2 * flat * tokens * (width + kv),
        2 * tokens * width + 6 * half * width,
        scratch=[pltpu.VMEM((flat, tokens), BF16)],
    )


def hot_away_kernel(count, keep_ref, *rest):
    for c in range(count):
        mate_ref, out_ref = rest[c], rest[count + c]
        height = out_ref.shape[0]
        at = slice((c + 1) * height, (c + 2) * height)
        out_ref[...] = (keep_ref[at, :] + mate_ref[...].astype(F32)).astype(BF16)


def hot_away(keep, mates, after):
    count = len(mates)
    return call(
        functools.partial(hot_away_kernel, count),
        "hot_away",
        after,
        (keep, *mates),
        vmem(1 + count),
        [sds(mates[0].shape, BF16)] * count,
        keep.size,
        8 * keep.size,
    )


def hot_final_kernel(keep_ref, mate_ref, *rest):
    down_ref, up_ref = rest[-2:]
    height, width = down_ref.shape
    total = keep_ref[0:height, :] + mate_ref[0:height, :].astype(F32)
    for ref in rest[:-2]:
        total += ref[...].astype(F32)
    down_ref[...] = total[:, 0:width]
    up_ref[...] = total[:, width:]


def hot_final(keep, mate, fars, width, height, after):
    return call(
        hot_final_kernel,
        "hot_final",
        after,
        (keep, mate, *fars),
        vmem(2 + len(fars)),
        [sds((height, width), F32), sds((height, keep.shape[1] - width), F32)],
        keep.size,
        4 * keep.size,
    )


def cold_delta_kernel(cap, rank, first, count, ids_ref, down_ref, got_ref, *rest):
    out_refs = rest[:count]
    wide_ref = rest[count]
    flat, width = down_ref.shape
    lo, hi = first * cap, (first + count) * cap
    total = cold_out_of(got_ref, rank, ids_ref.shape[1])[:, lo:hi]
    id_col = column(ids_ref[:, lo:hi]).astype(I32)
    wide_ref[...] = spread_columns(total, id_col, flat // rank)
    step = divide(width, 4)
    for j in range(width // step):
        at = slice(j * step, (j + 1) * step)
        delta = mm(wide_ref[...], down_ref[:, at]).astype(BF16)
        for k in range(count):
            out_refs[k][:, at] = delta[k * cap : (k + 1) * cap, :]


def cold_delta(ids, cold_down, got, cap, rank, first, count, after):
    flat, width = cold_down.shape
    return call(
        functools.partial(cold_delta_kernel, cap, rank, first, count),
        "cold_delta",
        after,
        (ids, cold_down, got),
        vmem(3),
        [sds((cap, width), BF16)] * count,
        2 * flat * count * cap * width,
        2 * flat * width + 2 * count * cap * width,
        scratch=[pltpu.VMEM((count * cap, flat), BF16)],
    )


def cold_in_kernel(peers, cap, rank, ids_ref, down_ref, *rest):
    rx_refs = rest[:peers]
    out_ref, xs_ref = rest[peers:]
    adapters = down_ref.shape[0] // rank
    join(rx_refs, xs_ref, cap)
    id_row = ids_ref[0:1, :]
    group = divide(adapters, 2)
    total = jnp.zeros(out_ref.shape[1:], F32)
    for c in range(adapters // group):
        part = mm(down_ref[c * group * rank : (c + 1) * group * rank, :], xs_ref[...], NT)
        total += fold(part, id_row, float(c * group), group, rank)
    for q in range(out_ref.shape[0]):
        out_ref[q] = total


def cold_in(ids, cold_down, rx, cap, rank, parts, after):
    peers = len(rx)
    flat, width = cold_down.shape
    slots = ids.shape[1]
    return call(
        functools.partial(cold_in_kernel, peers, cap, rank),
        "cold_in",
        after,
        (ids, cold_down, *rx),
        vmem(2 + peers),
        [sds((parts, rank, slots), F32), sds((slots, width), BF16)],
        2 * flat * slots * width,
        2 * (flat + slots) * width,
    )


def cold_down_grad_kernel(rank, ids_ref, xs_ref, got_ref, out_ref, so_ref, wide_ref):
    i = pl.program_id(0)
    group = out_ref.shape[0] // rank

    @pl.when(i == 0)
    def _():
        so_ref[...] = cold_out_of(got_ref, rank, ids_ref.shape[1])

    shifted = ids_ref[0:1, :].astype(I32) - i * group
    spread_rows(wide_ref, so_ref[...], shifted, 0, group)
    out_ref[...] = mm(wide_ref[...], xs_ref[...])


def cold_down_gradient(ids, got, xs, rank, adapters, after):
    slots, width = xs.shape
    flat = adapters * rank
    group = divide(adapters, 8) * rank
    return call(
        functools.partial(cold_down_grad_kernel, rank),
        "cold_down_grad",
        after,
        (ids, xs, got),
        [whole((8, slots)), whole((slots, width)), whole(got.shape)],
        [sds((flat, width), F32)],
        2 * flat * slots * width,
        4 * flat * width + 2 * slots * width,
        out_specs=[pl.BlockSpec((group, width), lambda i: (i, 0))],
        scratch=[pltpu.VMEM((rank, slots), F32), pltpu.VMEM((group, slots), BF16)],
        grid=(flat // group,),
    )


def cold_up_grad_kernel(rank, ids_ref, dys_ref, *rest):
    in_refs = rest[:-3]
    out_ref, si_ref, wide_ref = rest[-3:]
    i = pl.program_id(0)
    group = out_ref.shape[0] // rank

    @pl.when(i == 0)
    def _():
        si_ref[...] = scaled(sum((r[0] for r in in_refs[1:]), in_refs[0][0]))

    shifted = ids_ref[0:1, :].astype(I32) - i * group
    spread_rows(wide_ref, si_ref[...], shifted, 0, group)
    out_ref[...] = mm(wide_ref[...], dys_ref[...])


def cold_up_gradient(ids, ins, dys, rank, adapters, after):
    slots, kv = dys.shape
    flat = adapters * rank
    group = divide(adapters, 2) * rank

    def body(*refs):
        cold_up_grad_kernel(rank, *refs)

    return call(
        body,
        "cold_up_grad",
        after,
        (ids, dys, *ins),
        [whole((8, slots)), whole((slots, kv))] + [whole(v.shape) for v in ins],
        [sds((flat, kv), F32)],
        2 * flat * slots * kv,
        4 * flat * kv + 2 * slots * kv,
        out_specs=[pl.BlockSpec((group, kv), lambda i: (i, 0))],
        scratch=[pltpu.VMEM((rank, slots), F32), pltpu.VMEM((group, slots), BF16)],
        grid=(flat // group,),
    )


def position_matrix(rows_ref, first, count):
    tokens = rows_ref.shape[1]
    as_float = jnp.broadcast_to(rows_ref[2:3, :], (8, tokens)).astype(F32)
    pos = column(as_float).astype(I32) - first
    return jnp.where(lax.broadcasted_iota(I32, (tokens, count), 1) == pos, 1.0, 0.0).astype(BF16)


def local_terms_kernel(near, cap, rank, rows_ref, hd_ref, got_ref, *rest):
    near_refs = rest[:near]
    out_ref, place_ref, left_ref, right_ref = rest[near:]
    flat, width = hd_ref.shape
    tokens = rows_ref.shape[1]
    total = hot_out_of(got_ref, rank)
    as_float = jnp.broadcast_to(rows_ref[0:1, :], (8, tokens)).astype(F32)
    id_col = column(as_float).astype(I32)
    left_ref[:, 0:flat] = spread_columns(total, id_col, flat // rank)
    left_ref[:, flat : flat + near * cap] = position_matrix(rows_ref, 0, near * cap)
    place_ref[...] = position_matrix(rows_ref, near * cap, place_ref.shape[1])
    step = divide(width, 4)
    for j in range(width // step):
        at = slice(j * step, (j + 1) * step)
        right_ref[0:flat, :] = hd_ref[:, at]
        for k in range(near):
            right_ref[flat + k * cap : flat + (k + 1) * cap, :] = near_refs[k][:, at]
        out_ref[:, at] = mm(left_ref[...], right_ref[...]).astype(BF16)


def local_terms(rows, hot_down, got, nears, far, cap, rank, after):
    flat, width = hot_down.shape
    tokens = rows.shape[1]
    near = len(nears)
    depth = flat + near * cap
    return call(
        functools.partial(local_terms_kernel, near, cap, rank),
        "local_terms",
        after,
        (rows, hot_down, got, *nears),
        vmem(3 + near),
        [sds((tokens, width), BF16), sds((tokens, far * cap), BF16)],
        2 * tokens * width * depth,
        2 * width * (tokens + depth),
        scratch=[
            pltpu.VMEM((tokens, depth), BF16),
            pltpu.VMEM((depth, divide(width, 4)), BF16),
        ],
    )


def base_kernel(first, count, t_ref, w_ref, local_ref, *rest):
    block_refs = rest[:count]
    part_refs = rest[count:-3]
    out_ref, passed_ref, dy_ref = rest[-3:]
    passed_ref[...] = sum((r[...] for r in part_refs[1:]), part_refs[0][...])
    t = t_ref[0]
    kv = block_refs[0].shape[1] // 2
    rows = slice(first, first + out_ref.shape[0])
    k = 0
    for ref in block_refs:
        for c in range(ref.shape[1] // kv):
            lanes = pl.ds(pl.multiple_of((t ^ k) * kv, kv), kv)
            dy_ref[:, lanes] = ref[:, c * kv : (c + 1) * kv]
            k += 1
    for at in pieces_of(w_ref.shape[0]):
        out_ref[:, at] = mm(dy_ref[...], w_ref[at, :], NT) + local_ref[rows, at].astype(F32)


def base(t, weight, local, blocks, first, sums, after):
    width, kv_all = weight.shape
    rows = blocks[0].shape[0]
    return call(
        functools.partial(base_kernel, first, len(blocks)),
        "base",
        after,
        (t, weight, local, *blocks, *sums),
        [smem()] + vmem(2 + len(blocks) + len(sums)),
        [sds((rows, width), F32), sds(sums[0].shape, F32)],
        2 * rows * width * kv_all,
        2 * width * kv_all + 6 * rows * width,
        scratch=[pltpu.VMEM((rows, kv_all), BF16)],
    )


def final_kernel(cap, far, place_ref, *rest):
    base_refs = rest[: len(rest) - far - 4]
    far_refs = rest[len(base_refs) : len(base_refs) + far]
    out_ref, far_ref, held_ref, sems = rest[len(base_refs) + far :]
    for k, ref in enumerate(far_refs):
        far_ref[k * cap : (k + 1) * cap, :] = ref[...]
    copies = []
    first = 0
    for ref in base_refs:
        for piece in pieces_of(ref.shape[0], 2):
            at = slice(first + piece.start, first + piece.stop)
            held_ref[at, :] = (ref[piece, :] + mm(place_ref[at, :], far_ref[...])).astype(BF16)
            copies.append(
                pltpu.make_async_copy(held_ref.at[at], out_ref.at[at], sems.at[len(copies)])
            )
            copies[-1].start()
        first += ref.shape[0]
    for copy in copies:
        copy.wait()


def final(place, bases, fars, cap, after):
    tokens = place.shape[0]
    width = bases[0].shape[1]
    far = len(fars)
    return call(
        functools.partial(final_kernel, cap, far),
        "final",
        after,
        (place, *bases, *fars),
        vmem(1 + len(bases) + far),
        [sds((tokens, width), BF16)],
        2 * tokens * width * far * cap,
        6 * tokens * width,
        out_specs=anywhere(1),
        scratch=[
            pltpu.VMEM((far * cap, width), BF16),
            pltpu.VMEM((tokens, width), BF16),
            pltpu.SemaphoreType.DMA((2 * len(bases),)),
        ],
    )


def swap(value, axis, k):
    count = lax.axis_size(axis)
    return lax.ppermute(value, axis, [(i, i ^ k) for i in range(count)])


def gather_rest(pair, parts):
    blocks, held = [pair], 2
    while held < parts:
        together = blocks[0] if len(blocks) == 1 else jnp.concatenate(blocks, axis=1)
        blocks.append(swap(together, "tensor", held))
        held *= 2
    return blocks


def over_tensor(part, parts):
    return [part] + [swap(part, "tensor", k) for k in range(1, parts)]


def shards(
    tokens_in,
    grad_out,
    value_weight,
    token_adapter,
    adapter_home,
    cold_down,
    cold_up,
    hot_down,
    hot_up,
):
    peers = lax.axis_size("dp")
    parts = lax.axis_size("tensor")
    tokens, width = tokens_in.shape
    kv = grad_out.shape[1]
    cap = tokens // (2 * peers)
    cold_here, rank, _ = cold_down.shape
    hot = hot_down.shape[0]
    hot_here = hot // peers
    near = 2
    flat_cold_down = cold_down.reshape(cold_here * rank, width)
    flat_cold_up = cold_up.reshape(cold_here * rank, kv)
    flat_hot_down = hot_down.reshape(hot * rank, width)
    flat_hot_up = hot_up.reshape(hot * rank, kv)
    me = lax.axis_index("dp").astype(I32).reshape(1)

    t = lax.axis_index("tensor").astype(I32).reshape(1)
    dy_next = swap(grad_out, "tensor", 1)
    x = tokens_in
    sd, rows, pick, token = route(
        me, token_adapter, adapter_home, grad_out, peers, cap, cold_here, hot_here
    )
    rd = [sd[0]] + [swap(sd[k], "dp", k) for k in range(1, peers)]
    (hot_part,), token = hot_products(
        rows, x, flat_hot_down, grad_out, flat_hot_up, rank, token
    )
    (pay, ids, held_dy), token = cold_out(hot_part, flat_cold_up, dy_next, rd, cap, rank, 1, token)
    far_x, token = pack(pick, x, cap, near, peers - near, token)
    far_x = [swap(far_x[k - near], "dp", k) for k in range(near, peers)]
    early = 3 * divide(tokens, 8)
    (got, *pairs), token = sum_pieces(
        over_tensor(pay, parts), grad_out, dy_next, (early, tokens - early), token
    )
    dys = [gather_rest(pair, parts) for pair in pairs]
    near_x, token = pack(pick, x, cap, 0, near, token)
    rx = [near_x[0], swap(near_x[1], "dp", 1)] + far_x
    (in_part, xs), token = cold_in(ids, flat_cold_down, rx, cap, rank, 1, token)
    in_next = swap(in_part, "tensor", 1)
    (keep, *sends), token = hot_grads(
        rows, x, grad_out, got, dys[0][-1], rank, hot, peers, token
    )
    mates = [swap(send, "dp", 1) for send in sends]
    near_delta, token = cold_delta(ids, flat_cold_down, got, cap, rank, 0, near, token)
    near_back = [near_delta[0]] + [swap(near_delta[k], "dp", k) for k in range(1, near)]
    height = hot_here * rank
    aways, token = hot_away(keep, mates[1:], token)
    aways = [swap(aways[c - 1], "dp", 2 * c) for c in range(1, peers // 2)]
    far_delta, token = cold_delta(ids, flat_cold_down, got, cap, rank, near, peers - near, token)
    far_back = [swap(far_delta[k - near], "dp", k) for k in range(near, peers)]
    (cold_down_grad,), token = cold_down_gradient(ids, got, xs, rank, cold_here, token)
    (local, place), token = local_terms(
        rows, flat_hot_down, got, near_back, peers - near, cap, rank, token
    )
    (hot_down_grad, hot_up_grad), token = hot_final(keep, mates[0], aways, width, height, token)
    (base_first, passed), token = base(
        t, value_weight, local, dys[0], 0, (in_part, in_next), token
    )
    ins = [passed] + [swap(passed, "tensor", k) for k in range(2, parts, 2)]
    (base_last, _), token = base(t, value_weight, local, dys[1], early, (ids,), token)
    (input_gradient,), token = final(place, (base_first, base_last), far_back, cap, token)
    (cold_up_grad,), token = cold_up_gradient(ids, ins, held_dy, rank, cold_here, token)
    return (
        input_gradient,
        cold_down_grad.reshape(cold_here, rank, width),
        cold_up_grad.reshape(cold_here, rank, kv),
        hot_down_grad.reshape(hot_here, rank, width),
        hot_up_grad.reshape(hot_here, rank, kv),
    )


def solution(mesh):
    in_specs = (
        P(("groups", "dp"), "tensor"),
        P(("groups", "dp"), "tensor"),
        P("tensor", None),
        P(("groups", "dp")),
        P("groups"),
        P(("groups", "dp"), None, "tensor"),
        P(("groups", "dp"), None, "tensor"),
        P("groups", None, "tensor"),
        P("groups", None, "tensor"),
    )
    out_specs = (
        P(("groups", "dp"), "tensor"),
        P(("groups", "dp"), None, "tensor"),
        P(("groups", "dp"), None, "tensor"),
        P(("groups", "dp"), None, "tensor"),
        P(("groups", "dp"), None, "tensor"),
    )
    return jax.shard_map(shards, mesh=mesh, in_specs=in_specs, out_specs=out_specs, check_vma=False)
```

```python
import functools

import jax
import jax.numpy as jnp
from jax import lax
from jax.experimental import pallas as pl
from jax.experimental.pallas import tpu as pltpu
from jax.sharding import PartitionSpec as P

ADAPTER_SCALE = 2.0
VMEM_LIMIT = 10 * 1024 * 1024
COST_SCALE = 0.3
ROUTE_MOVED = 400
BF16 = jnp.bfloat16
F32 = jnp.float32
I32 = jnp.int32
NN = (((1,), (0,)), ((), ()))
NT = (((1,), (1,)), ((), ()))


def mm(a, b, dims=NN):
    return lax.dot_general(a, b, dims, preferred_element_type=F32)


def sds(shape, dtype):
    return jax.ShapeDtypeStruct(shape, dtype)


def whole(shape):
    return pl.BlockSpec(shape, lambda *_: (0,) * len(shape))


def vmem(count):
    return [pl.BlockSpec(memory_space=pltpu.VMEM)] * count


def smem():
    return pl.BlockSpec(memory_space=pltpu.SMEM)


def hbm(count):
    return [pl.BlockSpec(memory_space=pltpu.HBM)] * count


def anywhere(count):
    return [pl.BlockSpec(memory_space=pl.ANY)] * count


def params():
    return pltpu.CompilerParams(vmem_limit_bytes=VMEM_LIMIT)


def cost(flops, moved):
    return pl.CostEstimate(
        flops=int(COST_SCALE * flops), bytes_accessed=int(COST_SCALE * moved), transcendentals=0
    )


def join(refs, into, rows):
    for k, ref in enumerate(refs):
        into[k * rows : (k + 1) * rows, :] = ref[0:rows, 0 : into.shape[1]]


def join_last(refs, into, rows):
    for k, ref in enumerate(refs):
        into[k * rows : (k + 1) * rows, :] = ref[0:rows, ref.shape[1] - into.shape[1] :]


TOKEN = (8, 128)


def call(body, name, after, args, in_specs, out_shape, flops, moved, out_specs=None, scratch=(), grid=None):
    taken, given = len(args), len(out_shape)
    chained = [] if after is None else [after]

    def kernel(*refs):
        outs = refs[taken + len(chained) :]
        body(*refs[:taken], *outs[:given], *outs[given + 1 :])
        outs[given][...] = jnp.zeros(TOKEN, F32)

    more = {} if grid is None else {"grid": grid}
    results = pl.pallas_call(
        kernel,
        in_specs=list(in_specs) + anywhere(len(chained)),
        out_specs=list(out_specs or vmem(given)) + (vmem(1) if grid is None else [whole(TOKEN)]),
        out_shape=list(out_shape) + [sds(TOKEN, F32)],
        scratch_shapes=list(scratch),
        compiler_params=params(),
        cost_estimate=cost(flops, moved),
        name=name,
        **more,
    )(*args, *chained)
    return results[:given], results[given]


def divide(total, parts):
    return total // parts if total % parts == 0 else total


def pieces_of(total, parts=4):
    step = divide(total, parts)
    return [slice(k * step, (k + 1) * step) for k in range(total // step)]


def column(row_8):
    return jnp.transpose(row_8)[:, 0:1]


def spread_columns(scaled_t, id_col, adapters):
    rank = scaled_t.shape[0]
    count = scaled_t.shape[1]
    scaled = jnp.transpose(scaled_t).astype(BF16)
    width = adapters * rank
    lane = lax.broadcasted_iota(I32, (rank, width), 1)
    sub = lax.broadcasted_iota(I32, (rank, width), 0)
    tile = jnp.where(lax.rem(lane, rank) == sub, 1.0, 0.0).astype(BF16)
    tiled = mm(scaled, tile)
    own = lax.div(lax.broadcasted_iota(I32, (count, width), 1), rank)
    return jnp.where(own == id_col, tiled, 0.0).astype(BF16)


def spread_rows(out_ref, scaled_t, id_row, first, adapters):
    rank = scaled_t.shape[0]
    for a in range(adapters):
        out_ref[a * rank : (a + 1) * rank, :] = jnp.where(
            id_row == first + a, scaled_t, 0.0
        ).astype(BF16)


def fold(product, id_row, first, adapters, rank):
    total = jnp.zeros((rank, product.shape[1]), F32)
    for a in range(adapters):
        total += jnp.where(id_row == first + a, product[a * rank : (a + 1) * rank, :], 0.0)
    return total


def scaled(total):
    return (ADAPTER_SCALE * total).astype(BF16).astype(F32)


def route_kernel(peers, cap, cold_here, hot_here, me_ref, adapter_in, home_in, dy_in, *rest):
    sd_refs = rest[:peers]
    rows_ref, pick_ref, adapter_ref, home_ref, dy_ref, sems = rest[peers:]
    pairs = ((adapter_in, adapter_ref), (home_in, home_ref), (dy_in, dy_ref))
    loads = [pltpu.make_async_copy(a, b, sems.at[n]) for n, (a, b) in enumerate(pairs)]
    for load in loads:
        load.start()
    adapters = home_ref.shape[1]
    tokens = adapter_ref.shape[1]
    slots = peers * cap
    loads[0].wait()
    loads[1].wait()
    me = me_ref[0]
    adapter = adapter_ref[...]
    home = home_ref[...]
    sub8 = lax.broadcasted_iota(I32, (8, adapters), 0)
    digits = jnp.where(
        sub8 == 0, lax.shift_right_logical(home, 5), jnp.where(sub8 == 1, home & 31, 0)
    ).astype(F32).astype(BF16)
    onehot = jnp.where(
        lax.broadcasted_iota(I32, (adapters, tokens), 0) == adapter, 1.0, 0.0
    ).astype(BF16)
    found = mm(digits, onehot).astype(I32)
    row = found[0:1, :] * 32 + found[1:2, :]
    has = adapter < adapters
    cold_total = cold_here * peers
    cold = has & (row < cold_total)
    hot = has & (row >= cold_total)
    dest = jnp.zeros_like(row)
    hot_row = row - cold_total
    hot_dest = jnp.zeros_like(row)
    for p in range(1, peers):
        dest += jnp.where(row >= p * cold_here, 1, 0)
        hot_dest += jnp.where(hot_row >= p * hot_here, 1, 0)
    dest = jnp.minimum(dest, peers - 1)
    local = row - dest * cold_here
    turn = dest ^ me
    height = max(8, peers)
    hits = jnp.where((lax.broadcasted_iota(I32, (height, tokens), 0) == turn) & cold, 1, 0)
    running = hits
    lane = lax.broadcasted_iota(I32, (height, tokens), 1)
    step = 1
    while step < tokens:
        running += jnp.where(lane >= step, pltpu.roll(running, step, 1), 0)
        step *= 2
    within = jnp.sum(hits * (running - 1), axis=0, keepdims=True)
    position = jnp.where(cold, turn * cap + within, slots)
    hot_nat = jnp.where(hot, hot_row, hot_here * peers)
    hot_turn = jnp.where(
        hot,
        (hot_dest ^ me) * hot_here + hot_row - hot_dest * hot_here,
        hot_here * peers,
    )
    sub = lax.broadcasted_iota(I32, (8, tokens), 0)
    rows_ref[...] = jnp.where(
        sub == 0, hot_nat, jnp.where(sub == 1, hot_turn, jnp.where(sub == 2, position, 0))
    )
    pick_ref[...] = jnp.where(
        lax.broadcasted_iota(I32, (slots, tokens), 0) == position, 1.0, 0.0
    ).astype(BF16)
    loads[2].wait()
    packed = mm(pick_ref[...], dy_ref[...]).astype(BF16)
    ids = mm(jnp.broadcast_to(local.astype(F32), (16, tokens)).astype(BF16), pick_ref[...], NT)
    for k in range(peers):
        sd_refs[k][0:cap, :] = packed[k * cap : (k + 1) * cap, :]
        sd_refs[k][cap : cap + 16, :] = jnp.zeros((16, sd_refs[k].shape[1]), BF16)
        sd_refs[k][cap : cap + 16, 0:cap] = ids[:, k * cap : (k + 1) * cap].astype(BF16)


def route(me, token_adapter, adapter_home, dy, peers, cap, cold_here, hot_here):
    tokens, kv = dy.shape
    slots = peers * cap
    outs, token = call(
        functools.partial(route_kernel, peers, cap, cold_here, hot_here),
        "route",
        None,
        (me, token_adapter.reshape(1, -1), adapter_home.reshape(1, -1), dy),
        [smem()] + hbm(3),
        [sds((cap + 16, kv), BF16)] * peers
        + [sds((8, tokens), I32), sds((slots, tokens), BF16)],
        2 * slots * tokens * kv,
        ROUTE_MOVED * tokens * kv,
        scratch=[
            pltpu.VMEM((1, tokens), I32),
            pltpu.VMEM((1, adapter_home.shape[0]), I32),
            pltpu.VMEM((tokens, kv), BF16),
            pltpu.SemaphoreType.DMA((3,)),
        ],
    )
    return outs[:peers], *outs[peers:], token


def pack_kernel(first, cap, pick_ref, x_ref, *out_refs):
    rows = slice(first * cap, (first + len(out_refs)) * cap)
    for at in pieces_of(x_ref.shape[1]):
        packed = mm(pick_ref[rows, :], x_ref[:, at]).astype(BF16)
        for k, ref in enumerate(out_refs):
            ref[:, at] = packed[k * cap : (k + 1) * cap, :]


def pack(pick, x, cap, first, count, after):
    tokens, width = x.shape
    return call(
        functools.partial(pack_kernel, first, cap),
        "pack",
        after,
        (pick, x),
        vmem(2),
        [sds((cap, width), BF16)] * count,
        2 * count * cap * tokens * width,
        2 * (tokens + count * cap) * width,
    )


def hot_products_kernel(rank, rows_ref, x_ref, hd_ref, dy_ref, hu_ref, out_ref):
    hot = hd_ref.shape[0] // rank
    tokens = x_ref.shape[0]
    half = divide(tokens, 2)
    for c in range(tokens // half):
        at = slice(c * half, (c + 1) * half)
        row = rows_ref[0:1, at]
        out_ref[0:rank, at] = fold(mm(hu_ref[...], dy_ref[at, :], NT), row, 0, hot, rank)
        out_ref[rank : 2 * rank, at] = fold(mm(hd_ref[...], x_ref[at, :], NT), row, 0, hot, rank)


def hot_products(rows, x, hot_down, dy, hot_up, rank, after):
    tokens, width = x.shape
    flat = hot_down.shape[0]
    kv = dy.shape[1]
    return call(
        functools.partial(hot_products_kernel, rank),
        "hot_products",
        after,
        (rows, x, hot_down, dy, hot_up),
        vmem(5),
        [sds((2 * rank, tokens), F32)],
        2 * flat * tokens * (width + kv),
        2 * (tokens + flat) * width,
    )


def cold_out_kernel(peers, cap, rank, hot_ref, up_ref, _, *rest):
    rd_refs = rest[:peers]
    pay_ref, ids_ref, dys_ref = rest[peers:]
    adapters = up_ref.shape[0] // rank
    slots = peers * cap
    join_last(rd_refs, dys_ref, cap)
    kv = up_ref.shape[1]
    ids = [
        r[cap : cap + 16, r.shape[1] - kv : r.shape[1] - kv + cap].astype(F32)[0:8]
        for r in rd_refs
    ]
    ids_8 = jnp.concatenate(ids, axis=1)
    ids_ref[...] = ids_8
    id_row = ids_8[0:1, :]
    group = divide(adapters, 8)
    total = jnp.zeros((rank, slots), F32)
    for c in range(adapters // group):
        part = mm(up_ref[c * group * rank : (c + 1) * group * rank, :], dys_ref[...], NT)
        total += fold(part, id_row, float(c * group), group, rank)
    half = rank // 2
    folded = jnp.concatenate([total[0:half], total[half:rank]], axis=1)
    piece = pay_ref.shape[2]
    for q in range(pay_ref.shape[0]):
        at = slice(q * piece, (q + 1) * piece)
        pay_ref[q, 0 : 2 * rank, :] = hot_ref[:, at]
        pay_ref[q, 2 * rank : 2 * rank + half, :] = folded[:, at]


def cold_out(hot_part, cold_up, before, rd, cap, rank, parts, after):
    peers = len(rd)
    flat, kv = cold_up.shape
    slots = peers * cap
    tokens = hot_part.shape[1]
    return call(
        functools.partial(cold_out_kernel, peers, cap, rank),
        "cold_out",
        after,
        (hot_part, cold_up, before, *rd),
        vmem(2) + anywhere(1) + vmem(peers),
        [sds((parts, 2 * rank + rank // 2, tokens // parts), F32), sds((8, slots), F32), sds((slots, kv), BF16)],
        2 * flat * slots * kv,
        2 * (flat + slots) * kv,
    )


def sum_pieces_kernel(parts, dy_ref, next_ref, *refs):
    pay_refs = refs[:parts]
    out_ref, *pair_refs = refs[parts:]
    total = pay_refs[0][0]
    for ref in pay_refs[1:]:
        total += ref[0]
    filled, width = out_ref.shape[1:]
    total = (ADAPTER_SCALE * total).astype(BF16).astype(F32)
    rest = jnp.zeros((filled - total.shape[0], width), F32)
    out_ref[0] = jnp.concatenate([total, rest], axis=0).astype(BF16)
    kv = dy_ref.shape[1]
    first = 0
    for ref in pair_refs:
        at = slice(first, first + ref.shape[0])
        first += ref.shape[0]
        ref[:, 0:kv] = dy_ref[at, :]
        ref[:, kv:] = next_ref[at, :]


def sum_pieces(pays, dy, dy_next, cuts, after):
    _, height, width = pays[0].shape
    filled = -(-height // 16) * 16
    return call(
        functools.partial(sum_pieces_kernel, len(pays)),
        "sum_pieces",
        after,
        (dy, dy_next, *pays),
        vmem(2 + len(pays)),
        [sds((1, filled, width), BF16)] + [sds((rows, 2 * dy.shape[1]), BF16) for rows in cuts],
        len(pays) * pays[0].size,
        4 * len(pays) * pays[0].size,
    )


def gathered(got_ref, first, last):
    return jnp.concatenate(
        [got_ref[q, first:last, :].astype(F32) for q in range(got_ref.shape[0])], axis=1
    )


def hot_out_of(got_ref, rank):
    return gathered(got_ref, 0, rank)


def hot_in_of(got_ref, rank):
    return gathered(got_ref, rank, 2 * rank)


def cold_out_of(got_ref, rank, slots):
    half = rank // 2
    folded = gathered(got_ref, 2 * rank, got_ref.shape[1])[0:half]
    return jnp.concatenate([folded[:, 0:slots], folded[:, slots : 2 * slots]], axis=0)


def hot_grads_kernel(peers, rank, hot, rows_ref, x_ref, dy_ref, got_ref, _, keep_ref, *rest):
    send_refs, wide_ref = rest[:-1], rest[-1]
    width = x_ref.shape[1]
    kv = dy_ref.shape[1]
    block = hot // peers * rank

    def put(product, column):
        for k in range(peers):
            piece = product[k * block : (k + 1) * block, :]
            at = slice((k // 2) * block, (k // 2 + 1) * block)
            if k % 2 == 0:
                keep_ref[at, column] = piece
            else:
                send_refs[k // 2][:, column] = piece.astype(BF16)

    turn = rows_ref[1:2, :]
    spread_rows(wide_ref, hot_in_of(got_ref, rank), turn, 0, hot)
    put(mm(wide_ref[...], dy_ref[...]), slice(width, width + kv))
    spread_rows(wide_ref, hot_out_of(got_ref, rank), turn, 0, hot)
    step = divide(width, 4)
    for j in range(width // step):
        at = slice(j * step, (j + 1) * step)
        put(mm(wide_ref[...], x_ref[:, at]), at)


def hot_grads(rows, x, dy, got, before, rank, hot, peers, after):
    tokens, width = x.shape
    kv = dy.shape[1]
    flat = hot * rank
    half = flat // 2
    return call(
        functools.partial(hot_grads_kernel, peers, rank, hot),
        "hot_grads",
        after,
        (rows, x, dy, got, before),
        vmem(4) + anywhere(1),
        [sds((half, width + kv), F32)]
        + [sds((flat // peers, width + kv), BF16)] * (peers // 2),
        2 * flat * tokens * (width + kv),
        2 * tokens * width + 6 * half * width,
        scratch=[pltpu.VMEM((flat, tokens), BF16)],
    )


def hot_away_kernel(count, keep_ref, *rest):
    for c in range(count):
        mate_ref, out_ref = rest[c], rest[count + c]
        height = out_ref.shape[0]
        at = slice((c + 1) * height, (c + 2) * height)
        out_ref[...] = (keep_ref[at, :] + mate_ref[...].astype(F32)).astype(BF16)


def hot_away(keep, mates, after):
    count = len(mates)
    return call(
        functools.partial(hot_away_kernel, count),
        "hot_away",
        after,
        (keep, *mates),
        vmem(1 + count),
        [sds(mates[0].shape, BF16)] * count,
        keep.size,
        8 * keep.size,
    )


def hot_final_kernel(keep_ref, mate_ref, *rest):
    down_ref, up_ref = rest[-2:]
    height, width = down_ref.shape
    total = keep_ref[0:height, :] + mate_ref[0:height, :].astype(F32)
    for ref in rest[:-2]:
        total += ref[...].astype(F32)
    down_ref[...] = total[:, 0:width]
    up_ref[...] = total[:, width:]


def hot_final(keep, mate, fars, width, height, after):
    return call(
        hot_final_kernel,
        "hot_final",
        after,
        (keep, mate, *fars),
        vmem(2 + len(fars)),
        [sds((height, width), F32), sds((height, keep.shape[1] - width), F32)],
        keep.size,
        4 * keep.size,
    )


def cold_delta_kernel(cap, rank, first, count, ids_ref, down_ref, got_ref, *rest):
    out_refs = rest[:count]
    wide_ref = rest[count]
    flat, width = down_ref.shape
    lo, hi = first * cap, (first + count) * cap
    total = cold_out_of(got_ref, rank, ids_ref.shape[1])[:, lo:hi]
    id_col = column(ids_ref[:, lo:hi]).astype(I32)
    wide_ref[...] = spread_columns(total, id_col, flat // rank)
    step = divide(width, 4)
    for j in range(width // step):
        at = slice(j * step, (j + 1) * step)
        delta = mm(wide_ref[...], down_ref[:, at]).astype(BF16)
        for k in range(count):
            out_refs[k][:, at] = delta[k * cap : (k + 1) * cap, :]


def cold_delta(ids, cold_down, got, cap, rank, first, count, after):
    flat, width = cold_down.shape
    return call(
        functools.partial(cold_delta_kernel, cap, rank, first, count),
        "cold_delta",
        after,
        (ids, cold_down, got),
        vmem(3),
        [sds((cap, width), BF16)] * count,
        2 * flat * count * cap * width,
        2 * flat * width + 2 * count * cap * width,
        scratch=[pltpu.VMEM((count * cap, flat), BF16)],
    )


def cold_in_kernel(peers, cap, rank, ids_ref, down_ref, *rest):
    rx_refs = rest[:peers]
    out_ref, xs_ref = rest[peers:]
    adapters = down_ref.shape[0] // rank
    join(rx_refs, xs_ref, cap)
    id_row = ids_ref[0:1, :]
    group = divide(adapters, 2)
    total = jnp.zeros(out_ref.shape[1:], F32)
    for c in range(adapters // group):
        part = mm(down_ref[c * group * rank : (c + 1) * group * rank, :], xs_ref[...], NT)
        total += fold(part, id_row, float(c * group), group, rank)
    for q in range(out_ref.shape[0]):
        out_ref[q] = total


def cold_in(ids, cold_down, rx, cap, rank, parts, after):
    peers = len(rx)
    flat, width = cold_down.shape
    slots = ids.shape[1]
    return call(
        functools.partial(cold_in_kernel, peers, cap, rank),
        "cold_in",
        after,
        (ids, cold_down, *rx),
        vmem(2 + peers),
        [sds((parts, rank, slots), F32), sds((slots, width), BF16)],
        2 * flat * slots * width,
        2 * (flat + slots) * width,
    )


def cold_down_grad_kernel(rank, ids_ref, xs_ref, got_ref, out_ref, so_ref, wide_ref):
    i = pl.program_id(0)
    group = out_ref.shape[0] // rank

    @pl.when(i == 0)
    def _():
        so_ref[...] = cold_out_of(got_ref, rank, ids_ref.shape[1])

    shifted = ids_ref[0:1, :].astype(I32) - i * group
    spread_rows(wide_ref, so_ref[...], shifted, 0, group)
    out_ref[...] = mm(wide_ref[...], xs_ref[...])


def cold_down_gradient(ids, got, xs, rank, adapters, after):
    slots, width = xs.shape
    flat = adapters * rank
    group = divide(adapters, 8) * rank
    return call(
        functools.partial(cold_down_grad_kernel, rank),
        "cold_down_grad",
        after,
        (ids, xs, got),
        [whole((8, slots)), whole((slots, width)), whole(got.shape)],
        [sds((flat, width), F32)],
        2 * flat * slots * width,
        4 * flat * width + 2 * slots * width,
        out_specs=[pl.BlockSpec((group, width), lambda i: (i, 0))],
        scratch=[pltpu.VMEM((rank, slots), F32), pltpu.VMEM((group, slots), BF16)],
        grid=(flat // group,),
    )


def cold_up_grad_kernel(rank, ids_ref, dys_ref, *rest):
    in_refs = rest[:-3]
    out_ref, si_ref, wide_ref = rest[-3:]
    i = pl.program_id(0)
    group = out_ref.shape[0] // rank

    @pl.when(i == 0)
    def _():
        si_ref[...] = scaled(sum((r[0] for r in in_refs[1:]), in_refs[0][0]))

    shifted = ids_ref[0:1, :].astype(I32) - i * group
    spread_rows(wide_ref, si_ref[...], shifted, 0, group)
    out_ref[...] = mm(wide_ref[...], dys_ref[...])


def cold_up_gradient(ids, ins, dys, rank, adapters, after):
    slots, kv = dys.shape
    flat = adapters * rank
    group = divide(adapters, 2) * rank

    def body(*refs):
        cold_up_grad_kernel(rank, *refs)

    return call(
        body,
        "cold_up_grad",
        after,
        (ids, dys, *ins),
        [whole((8, slots)), whole((slots, kv))] + [whole(v.shape) for v in ins],
        [sds((flat, kv), F32)],
        2 * flat * slots * kv,
        4 * flat * kv + 2 * slots * kv,
        out_specs=[pl.BlockSpec((group, kv), lambda i: (i, 0))],
        scratch=[pltpu.VMEM((rank, slots), F32), pltpu.VMEM((group, slots), BF16)],
        grid=(flat // group,),
    )


def position_matrix(rows_ref, first, count):
    tokens = rows_ref.shape[1]
    as_float = jnp.broadcast_to(rows_ref[2:3, :], (8, tokens)).astype(F32)
    pos = column(as_float).astype(I32) - first
    return jnp.where(lax.broadcasted_iota(I32, (tokens, count), 1) == pos, 1.0, 0.0).astype(BF16)


def local_terms_kernel(near, cap, rank, rows_ref, hd_ref, got_ref, *rest):
    near_refs = rest[:near]
    out_ref, place_ref, left_ref, right_ref = rest[near:]
    flat, width = hd_ref.shape
    tokens = rows_ref.shape[1]
    total = hot_out_of(got_ref, rank)
    as_float = jnp.broadcast_to(rows_ref[0:1, :], (8, tokens)).astype(F32)
    id_col = column(as_float).astype(I32)
    left_ref[:, 0:flat] = spread_columns(total, id_col, flat // rank)
    left_ref[:, flat : flat + near * cap] = position_matrix(rows_ref, 0, near * cap)
    place_ref[...] = position_matrix(rows_ref, near * cap, place_ref.shape[1])
    step = divide(width, 4)
    for j in range(width // step):
        at = slice(j * step, (j + 1) * step)
        right_ref[0:flat, :] = hd_ref[:, at]
        for k in range(near):
            right_ref[flat + k * cap : flat + (k + 1) * cap, :] = near_refs[k][:, at]
        out_ref[:, at] = mm(left_ref[...], right_ref[...]).astype(BF16)


def local_terms(rows, hot_down, got, nears, far, cap, rank, after):
    flat, width = hot_down.shape
    tokens = rows.shape[1]
    near = len(nears)
    depth = flat + near * cap
    return call(
        functools.partial(local_terms_kernel, near, cap, rank),
        "local_terms",
        after,
        (rows, hot_down, got, *nears),
        vmem(3 + near),
        [sds((tokens, width), BF16), sds((tokens, far * cap), BF16)],
        2 * tokens * width * depth,
        2 * width * (tokens + depth),
        scratch=[
            pltpu.VMEM((tokens, depth), BF16),
            pltpu.VMEM((depth, divide(width, 4)), BF16),
        ],
    )


def base_kernel(first, count, t_ref, w_ref, local_ref, *rest):
    block_refs = rest[:count]
    part_refs = rest[count:-3]
    out_ref, passed_ref, dy_ref = rest[-3:]
    passed_ref[...] = sum((r[...] for r in part_refs[1:]), part_refs[0][...])
    t = t_ref[0]
    kv = block_refs[0].shape[1] // 2
    rows = slice(first, first + out_ref.shape[0])
    k = 0
    for ref in block_refs:
        for c in range(ref.shape[1] // kv):
            lanes = pl.ds(pl.multiple_of((t ^ k) * kv, kv), kv)
            dy_ref[:, lanes] = ref[:, c * kv : (c + 1) * kv]
            k += 1
    for at in pieces_of(w_ref.shape[0]):
        out_ref[:, at] = mm(dy_ref[...], w_ref[at, :], NT) + local_ref[rows, at].astype(F32)


def base(t, weight, local, blocks, first, sums, after):
    width, kv_all = weight.shape
    rows = blocks[0].shape[0]
    return call(
        functools.partial(base_kernel, first, len(blocks)),
        "base",
        after,
        (t, weight, local, *blocks, *sums),
        [smem()] + vmem(2 + len(blocks) + len(sums)),
        [sds((rows, width), F32), sds(sums[0].shape, F32)],
        2 * rows * width * kv_all,
        2 * width * kv_all + 6 * rows * width,
        scratch=[pltpu.VMEM((rows, kv_all), BF16)],
    )


def final_kernel(cap, far, place_ref, *rest):
    base_refs = rest[: len(rest) - far - 4]
    far_refs = rest[len(base_refs) : len(base_refs) + far]
    out_ref, far_ref, held_ref, sems = rest[len(base_refs) + far :]
    for k, ref in enumerate(far_refs):
        far_ref[k * cap : (k + 1) * cap, :] = ref[...]
    copies = []
    first = 0
    for ref in base_refs:
        for piece in pieces_of(ref.shape[0], 2):
            at = slice(first + piece.start, first + piece.stop)
            held_ref[at, :] = (ref[piece, :] + mm(place_ref[at, :], far_ref[...])).astype(BF16)
            copies.append(
                pltpu.make_async_copy(held_ref.at[at], out_ref.at[at], sems.at[len(copies)])
            )
            copies[-1].start()
        first += ref.shape[0]
    for copy in copies:
        copy.wait()


def final(place, bases, fars, cap, after):
    tokens = place.shape[0]
    width = bases[0].shape[1]
    far = len(fars)
    return call(
        functools.partial(final_kernel, cap, far),
        "final",
        after,
        (place, *bases, *fars),
        vmem(1 + len(bases) + far),
        [sds((tokens, width), BF16)],
        2 * tokens * width * far * cap,
        6 * tokens * width,
        out_specs=anywhere(1),
        scratch=[
            pltpu.VMEM((far * cap, width), BF16),
            pltpu.VMEM((tokens, width), BF16),
            pltpu.SemaphoreType.DMA((2 * len(bases),)),
        ],
    )


def swap(value, axis, k):
    count = lax.axis_size(axis)
    return lax.ppermute(value, axis, [(i, i ^ k) for i in range(count)])


def gather_rest(pair, parts):
    blocks, held = [pair], 2
    while held < parts:
        together = blocks[0] if len(blocks) == 1 else jnp.concatenate(blocks, axis=1)
        blocks.append(swap(together, "tensor", held))
        held *= 2
    return blocks


def over_tensor(part, parts):
    return [part] + [swap(part, "tensor", k) for k in range(1, parts)]


def shards(
    tokens_in,
    grad_out,
    value_weight,
    token_adapter,
    adapter_home,
    cold_down,
    cold_up,
    hot_down,
    hot_up,
):
    peers = lax.axis_size("dp")
    parts = lax.axis_size("tensor")
    tokens, width = tokens_in.shape
    kv = grad_out.shape[1]
    cap = tokens // (2 * peers)
    cold_here, rank, _ = cold_down.shape
    hot = hot_down.shape[0]
    hot_here = hot // peers
    near = 2
    flat_cold_down = cold_down.reshape(cold_here * rank, width)
    flat_cold_up = cold_up.reshape(cold_here * rank, kv)
    flat_hot_down = hot_down.reshape(hot * rank, width)
    flat_hot_up = hot_up.reshape(hot * rank, kv)
    me = lax.axis_index("dp").astype(I32).reshape(1)

    t = lax.axis_index("tensor").astype(I32).reshape(1)
    dy_next = swap(grad_out, "tensor", 1)
    x = tokens_in
    sd, rows, pick, token = route(
        me, token_adapter, adapter_home, grad_out, peers, cap, cold_here, hot_here
    )
    rd = [sd[0]] + [swap(sd[k], "dp", k) for k in range(1, peers)]
    (hot_part,), token = hot_products(
        rows, x, flat_hot_down, grad_out, flat_hot_up, rank, token
    )
    (pay, ids, held_dy), token = cold_out(hot_part, flat_cold_up, dy_next, rd, cap, rank, 1, token)
    far_x, token = pack(pick, x, cap, near, peers - near, token)
    far_x = [swap(far_x[k - near], "dp", k) for k in range(near, peers)]
    early = 5 * divide(tokens, 16)
    (got, *pairs), token = sum_pieces(
        over_tensor(pay, parts), grad_out, dy_next, (early, tokens - early), token
    )
    dys = [gather_rest(pair, parts) for pair in pairs]
    near_x, token = pack(pick, x, cap, 0, near, token)
    rx = [near_x[0], swap(near_x[1], "dp", 1)] + far_x
    (in_part, xs), token = cold_in(ids, flat_cold_down, rx, cap, rank, 1, token)
    in_next = swap(in_part, "tensor", 1)
    near_delta, token = cold_delta(ids, flat_cold_down, got, cap, rank, 0, near, token)
    near_back = [near_delta[0]] + [swap(near_delta[k], "dp", k) for k in range(1, near)]
    (keep, *sends), token = hot_grads(
        rows, x, grad_out, got, dys[0][-1], rank, hot, peers, token
    )
    mates = [swap(send, "dp", 1) for send in sends]
    height = hot_here * rank
    aways, token = hot_away(keep, mates[1:], token)
    aways = [swap(aways[c - 1], "dp", 2 * c) for c in range(1, peers // 2)]
    far_delta, token = cold_delta(ids, flat_cold_down, got, cap, rank, near, peers - near, token)
    far_back = [swap(far_delta[k - near], "dp", k) for k in range(near, peers)]
    (cold_down_grad,), token = cold_down_gradient(ids, got, xs, rank, cold_here, token)
    (local, place), token = local_terms(
        rows, flat_hot_down, got, near_back, peers - near, cap, rank, token
    )
    (hot_down_grad, hot_up_grad), token = hot_final(keep, mates[0], aways, width, height, token)
    (base_first, _), token = base(t, value_weight, local, dys[0], 0, (ids,), token)
    (base_last, passed), token = base(
        t, value_weight, local, dys[1], early, (in_part, in_next), token
    )
    ins = [passed] + [swap(passed, "tensor", k) for k in range(2, parts, 2)]
    (input_gradient,), token = final(place, (base_first, base_last), far_back, cap, token)
    (cold_up_grad,), token = cold_up_gradient(ids, ins, held_dy, rank, cold_here, token)
    return (
        input_gradient,
        cold_down_grad.reshape(cold_here, rank, width),
        cold_up_grad.reshape(cold_here, rank, kv),
        hot_down_grad.reshape(hot_here, rank, width),
        hot_up_grad.reshape(hot_here, rank, kv),
    )


def solution(mesh):
    in_specs = (
        P(("groups", "dp"), "tensor"),
        P(("groups", "dp"), "tensor"),
        P("tensor", None),
        P(("groups", "dp")),
        P("groups"),
        P(("groups", "dp"), None, "tensor"),
        P(("groups", "dp"), None, "tensor"),
        P("groups", None, "tensor"),
        P("groups", None, "tensor"),
    )
    out_specs = (
        P(("groups", "dp"), "tensor"),
        P(("groups", "dp"), None, "tensor"),
        P(("groups", "dp"), None, "tensor"),
        P(("groups", "dp"), None, "tensor"),
        P(("groups", "dp"), None, "tensor"),
    )
    return jax.shard_map(shards, mesh=mesh, in_specs=in_specs, out_specs=out_specs, check_vma=False)
```

```python
import functools

import jax
import jax.numpy as jnp
from jax import lax
from jax.experimental import pallas as pl
from jax.experimental.pallas import tpu as pltpu
from jax.sharding import PartitionSpec as P

ADAPTER_SCALE = 2.0
VMEM_LIMIT = 10 * 1024 * 1024
COST_SCALE = 0.3
ROUTE_MOVED = 400
BF16 = jnp.bfloat16
F32 = jnp.float32
I32 = jnp.int32
NN = (((1,), (0,)), ((), ()))
NT = (((1,), (1,)), ((), ()))


def mm(a, b, dims=NN):
    return lax.dot_general(a, b, dims, preferred_element_type=F32)


def sds(shape, dtype):
    return jax.ShapeDtypeStruct(shape, dtype)


def whole(shape):
    return pl.BlockSpec(shape, lambda *_: (0,) * len(shape))


def vmem(count):
    return [pl.BlockSpec(memory_space=pltpu.VMEM)] * count


def smem():
    return pl.BlockSpec(memory_space=pltpu.SMEM)


def anywhere(count):
    return [pl.BlockSpec(memory_space=pl.ANY)] * count


def params():
    return pltpu.CompilerParams(vmem_limit_bytes=VMEM_LIMIT)


def cost(flops, moved):
    return pl.CostEstimate(
        flops=int(COST_SCALE * flops), bytes_accessed=int(COST_SCALE * moved), transcendentals=0
    )


def join(refs, into, rows):
    for k, ref in enumerate(refs):
        into[k * rows : (k + 1) * rows, :] = ref[0:rows, 0 : into.shape[1]]


def join_last(refs, into, rows):
    for k, ref in enumerate(refs):
        into[k * rows : (k + 1) * rows, :] = ref[0:rows, ref.shape[1] - into.shape[1] :]


TOKEN = (8, 128)


def call(body, name, after, args, in_specs, out_shape, flops, moved, out_specs=None, scratch=(), grid=None):
    taken, given = len(args), len(out_shape)
    chained = [] if after is None else [after]

    def kernel(*refs):
        outs = refs[taken + len(chained) :]
        body(*refs[:taken], *outs[:given], *outs[given + 1 :])
        outs[given][...] = jnp.zeros(TOKEN, F32)

    more = {} if grid is None else {"grid": grid}
    results = pl.pallas_call(
        kernel,
        in_specs=list(in_specs) + anywhere(len(chained)),
        out_specs=list(out_specs or vmem(given)) + (vmem(1) if grid is None else [whole(TOKEN)]),
        out_shape=list(out_shape) + [sds(TOKEN, F32)],
        scratch_shapes=list(scratch),
        compiler_params=params(),
        cost_estimate=cost(flops, moved),
        name=name,
        **more,
    )(*args, *chained)
    return results[:given], results[given]


def divide(total, parts):
    return total // parts if total % parts == 0 else total


def pieces_of(total, parts=4):
    step = divide(total, parts)
    return [slice(k * step, (k + 1) * step) for k in range(total // step)]


def column(row_8):
    return jnp.transpose(row_8)[:, 0:1]


def spread_columns(scaled_t, id_col, adapters):
    rank = scaled_t.shape[0]
    count = scaled_t.shape[1]
    scaled = jnp.transpose(scaled_t).astype(BF16)
    width = adapters * rank
    lane = lax.broadcasted_iota(I32, (rank, width), 1)
    sub = lax.broadcasted_iota(I32, (rank, width), 0)
    tile = jnp.where(lax.rem(lane, rank) == sub, 1.0, 0.0).astype(BF16)
    tiled = mm(scaled, tile)
    own = lax.div(lax.broadcasted_iota(I32, (count, width), 1), rank)
    return jnp.where(own == id_col, tiled, 0.0).astype(BF16)


def spread_rows(out_ref, scaled_t, id_row, first, adapters):
    rank = scaled_t.shape[0]
    for a in range(adapters):
        out_ref[a * rank : (a + 1) * rank, :] = jnp.where(
            id_row == first + a, scaled_t, 0.0
        ).astype(BF16)


def fold(product, id_row, first, adapters, rank):
    total = jnp.zeros((rank, product.shape[1]), F32)
    for a in range(adapters):
        total += jnp.where(id_row == first + a, product[a * rank : (a + 1) * rank, :], 0.0)
    return total


def scaled(total):
    return (ADAPTER_SCALE * total).astype(BF16).astype(F32)


def route_kernel(peers, cap, cold_here, hot_here, me_ref, adapter_ref, home_ref, dy_ref, *rest):
    sd_refs = rest[:peers]
    rows_ref, pick_ref, held_ref = rest[peers:]
    held_ref[...] = dy_ref[...]
    adapters = home_ref.shape[1]
    tokens = adapter_ref.shape[1]
    slots = peers * cap
    me = me_ref[0]
    adapter = adapter_ref[...]
    home = home_ref[...]
    sub8 = lax.broadcasted_iota(I32, (8, adapters), 0)
    digits = jnp.where(
        sub8 == 0, lax.shift_right_logical(home, 5), jnp.where(sub8 == 1, home & 31, 0)
    ).astype(F32).astype(BF16)
    onehot = jnp.where(
        lax.broadcasted_iota(I32, (adapters, tokens), 0) == adapter, 1.0, 0.0
    ).astype(BF16)
    found = mm(digits, onehot).astype(I32)
    row = found[0:1, :] * 32 + found[1:2, :]
    has = adapter < adapters
    cold_total = cold_here * peers
    cold = has & (row < cold_total)
    hot = has & (row >= cold_total)
    dest = jnp.zeros_like(row)
    hot_row = row - cold_total
    hot_dest = jnp.zeros_like(row)
    for p in range(1, peers):
        dest += jnp.where(row >= p * cold_here, 1, 0)
        hot_dest += jnp.where(hot_row >= p * hot_here, 1, 0)
    dest = jnp.minimum(dest, peers - 1)
    local = row - dest * cold_here
    turn = dest ^ me
    height = max(8, peers)
    hits = jnp.where((lax.broadcasted_iota(I32, (height, tokens), 0) == turn) & cold, 1, 0)
    running = hits
    lane = lax.broadcasted_iota(I32, (height, tokens), 1)
    step = 1
    while step < tokens:
        running += jnp.where(lane >= step, pltpu.roll(running, step, 1), 0)
        step *= 2
    within = jnp.sum(hits * (running - 1), axis=0, keepdims=True)
    position = jnp.where(cold, turn * cap + within, slots)
    hot_nat = jnp.where(hot, hot_row, hot_here * peers)
    hot_turn = jnp.where(
        hot,
        (hot_dest ^ me) * hot_here + hot_row - hot_dest * hot_here,
        hot_here * peers,
    )
    sub = lax.broadcasted_iota(I32, (8, tokens), 0)
    rows_ref[...] = jnp.where(
        sub == 0, hot_nat, jnp.where(sub == 1, hot_turn, jnp.where(sub == 2, position, 0))
    )
    pick_ref[...] = jnp.where(
        lax.broadcasted_iota(I32, (slots, tokens), 0) == position, 1.0, 0.0
    ).astype(BF16)
    packed = mm(pick_ref[...], dy_ref[...]).astype(BF16)
    ids = mm(jnp.broadcast_to(local.astype(F32), (16, tokens)).astype(BF16), pick_ref[...], NT)
    for k in range(peers):
        sd_refs[k][0:cap, :] = packed[k * cap : (k + 1) * cap, :]
        sd_refs[k][cap : cap + 16, :] = jnp.zeros((16, sd_refs[k].shape[1]), BF16)
        sd_refs[k][cap : cap + 16, 0:cap] = ids[:, k * cap : (k + 1) * cap].astype(BF16)


def route(me, token_adapter, adapter_home, dy, peers, cap, cold_here, hot_here):
    tokens, kv = dy.shape
    slots = peers * cap
    outs, token = call(
        functools.partial(route_kernel, peers, cap, cold_here, hot_here),
        "route",
        None,
        (me, token_adapter.reshape(1, -1), adapter_home.reshape(1, -1), dy),
        [smem()] + vmem(3),
        [sds((cap + 16, kv), BF16)] * peers
        + [sds((8, tokens), I32), sds((slots, tokens), BF16), sds(dy.shape, BF16)],
        2 * slots * tokens * kv,
        ROUTE_MOVED * tokens * kv,
    )
    return outs[:peers], *outs[peers:], token


def pack_kernel(first, cap, pick_ref, x_ref, *out_refs):
    rows = slice(first * cap, (first + len(out_refs)) * cap)
    for at in pieces_of(x_ref.shape[1]):
        packed = mm(pick_ref[rows, :], x_ref[:, at]).astype(BF16)
        for k, ref in enumerate(out_refs):
            ref[:, at] = packed[k * cap : (k + 1) * cap, :]


def pack(pick, x, cap, first, count, after):
    tokens, width = x.shape
    return call(
        functools.partial(pack_kernel, first, cap),
        "pack",
        after,
        (pick, x),
        vmem(2),
        [sds((cap, width), BF16)] * count,
        2 * count * cap * tokens * width,
        2 * (tokens + count * cap) * width,
    )


def hot_products_kernel(rank, rows_ref, x_ref, hd_ref, dy_ref, hu_ref, out_ref):
    hot = hd_ref.shape[0] // rank
    tokens = x_ref.shape[0]
    half = divide(tokens, 2)
    for c in range(tokens // half):
        at = slice(c * half, (c + 1) * half)
        row = rows_ref[0:1, at]
        out_ref[0:rank, at] = fold(mm(hu_ref[...], dy_ref[at, :], NT), row, 0, hot, rank)
        out_ref[rank : 2 * rank, at] = fold(mm(hd_ref[...], x_ref[at, :], NT), row, 0, hot, rank)


def hot_products(rows, x, hot_down, dy, hot_up, rank, after):
    tokens, width = x.shape
    flat = hot_down.shape[0]
    kv = dy.shape[1]
    return call(
        functools.partial(hot_products_kernel, rank),
        "hot_products",
        after,
        (rows, x, hot_down, dy, hot_up),
        vmem(5),
        [sds((2 * rank, tokens), F32)],
        2 * flat * tokens * (width + kv),
        2 * (tokens + flat) * width,
    )


def cold_out_kernel(peers, cap, rank, hot_ref, up_ref, _, *rest):
    rd_refs = rest[:peers]
    pay_ref, ids_ref, dys_ref = rest[peers:]
    adapters = up_ref.shape[0] // rank
    slots = peers * cap
    join_last(rd_refs, dys_ref, cap)
    kv = up_ref.shape[1]
    ids = [
        r[cap : cap + 16, r.shape[1] - kv : r.shape[1] - kv + cap].astype(F32)[0:8]
        for r in rd_refs
    ]
    ids_8 = jnp.concatenate(ids, axis=1)
    ids_ref[...] = ids_8
    id_row = ids_8[0:1, :]
    group = divide(adapters, 8)
    total = jnp.zeros((rank, slots), F32)
    for c in range(adapters // group):
        part = mm(up_ref[c * group * rank : (c + 1) * group * rank, :], dys_ref[...], NT)
        total += fold(part, id_row, float(c * group), group, rank)
    half = rank // 2
    folded = jnp.concatenate([total[0:half], total[half:rank]], axis=1)
    piece = pay_ref.shape[2]
    for q in range(pay_ref.shape[0]):
        at = slice(q * piece, (q + 1) * piece)
        pay_ref[q, 0 : 2 * rank, :] = hot_ref[:, at]
        pay_ref[q, 2 * rank : 2 * rank + half, :] = folded[:, at]


def cold_out(hot_part, cold_up, before, rd, cap, rank, parts, after):
    peers = len(rd)
    flat, kv = cold_up.shape
    slots = peers * cap
    tokens = hot_part.shape[1]
    return call(
        functools.partial(cold_out_kernel, peers, cap, rank),
        "cold_out",
        after,
        (hot_part, cold_up, before, *rd),
        vmem(2) + anywhere(1) + vmem(peers),
        [sds((parts, 2 * rank + rank // 2, tokens // parts), F32), sds((8, slots), F32), sds((slots, kv), BF16)],
        2 * flat * slots * kv,
        2 * (flat + slots) * kv,
    )


def sum_pieces_kernel(parts, dy_ref, next_ref, *refs):
    pay_refs = refs[:parts]
    out_ref, *pair_refs = refs[parts:]
    total = pay_refs[0][0]
    for ref in pay_refs[1:]:
        total += ref[0]
    filled, width = out_ref.shape[1:]
    total = (ADAPTER_SCALE * total).astype(BF16).astype(F32)
    rest = jnp.zeros((filled - total.shape[0], width), F32)
    out_ref[0] = jnp.concatenate([total, rest], axis=0).astype(BF16)
    kv = dy_ref.shape[1]
    first = 0
    for ref in pair_refs:
        at = slice(first, first + ref.shape[0])
        first += ref.shape[0]
        ref[:, 0:kv] = dy_ref[at, :]
        ref[:, kv:] = next_ref[at, :]


def sum_pieces(pays, dy, dy_next, cuts, after):
    _, height, width = pays[0].shape
    filled = -(-height // 16) * 16
    return call(
        functools.partial(sum_pieces_kernel, len(pays)),
        "sum_pieces",
        after,
        (dy, dy_next, *pays),
        vmem(2 + len(pays)),
        [sds((1, filled, width), BF16)] + [sds((rows, 2 * dy.shape[1]), BF16) for rows in cuts],
        len(pays) * pays[0].size,
        4 * len(pays) * pays[0].size,
    )


def gathered(got_ref, first, last):
    return jnp.concatenate(
        [got_ref[q, first:last, :].astype(F32) for q in range(got_ref.shape[0])], axis=1
    )


def hot_out_of(got_ref, rank):
    return gathered(got_ref, 0, rank)


def hot_in_of(got_ref, rank):
    return gathered(got_ref, rank, 2 * rank)


def cold_out_of(got_ref, rank, slots):
    half = rank // 2
    folded = gathered(got_ref, 2 * rank, got_ref.shape[1])[0:half]
    return jnp.concatenate([folded[:, 0:slots], folded[:, slots : 2 * slots]], axis=0)


def hot_grads_kernel(peers, rank, hot, rows_ref, x_ref, dy_ref, got_ref, _, keep_ref, *rest):
    send_refs, wide_ref = rest[:-1], rest[-1]
    width = x_ref.shape[1]
    kv = dy_ref.shape[1]
    block = hot // peers * rank

    def put(product, column):
        for k in range(peers):
            piece = product[k * block : (k + 1) * block, :]
            at = slice((k // 2) * block, (k // 2 + 1) * block)
            if k % 2 == 0:
                keep_ref[at, column] = piece
            else:
                send_refs[k // 2][:, column] = piece.astype(BF16)

    turn = rows_ref[1:2, :]
    spread_rows(wide_ref, hot_in_of(got_ref, rank), turn, 0, hot)
    put(mm(wide_ref[...], dy_ref[...]), slice(width, width + kv))
    spread_rows(wide_ref, hot_out_of(got_ref, rank), turn, 0, hot)
    step = divide(width, 4)
    for j in range(width // step):
        at = slice(j * step, (j + 1) * step)
        put(mm(wide_ref[...], x_ref[:, at]), at)


def hot_grads(rows, x, dy, got, before, rank, hot, peers, after):
    tokens, width = x.shape
    kv = dy.shape[1]
    flat = hot * rank
    half = flat // 2
    return call(
        functools.partial(hot_grads_kernel, peers, rank, hot),
        "hot_grads",
        after,
        (rows, x, dy, got, before),
        vmem(4) + anywhere(1),
        [sds((half, width + kv), F32)]
        + [sds((flat // peers, width + kv), BF16)] * (peers // 2),
        2 * flat * tokens * (width + kv),
        2 * tokens * width + 6 * half * width,
        scratch=[pltpu.VMEM((flat, tokens), BF16)],
    )


def hot_away_kernel(count, keep_ref, *rest):
    for c in range(count):
        mate_ref, out_ref = rest[c], rest[count + c]
        height = out_ref.shape[0]
        at = slice((c + 1) * height, (c + 2) * height)
        out_ref[...] = (keep_ref[at, :] + mate_ref[...].astype(F32)).astype(BF16)


def hot_away(keep, mates, after):
    count = len(mates)
    return call(
        functools.partial(hot_away_kernel, count),
        "hot_away",
        after,
        (keep, *mates),
        vmem(1 + count),
        [sds(mates[0].shape, BF16)] * count,
        keep.size,
        8 * keep.size,
    )


def hot_final_kernel(keep_ref, mate_ref, *rest):
    down_ref, up_ref = rest[-2:]
    height, width = down_ref.shape
    total = keep_ref[0:height, :] + mate_ref[0:height, :].astype(F32)
    for ref in rest[:-2]:
        total += ref[...].astype(F32)
    down_ref[...] = total[:, 0:width]
    up_ref[...] = total[:, width:]


def hot_final(keep, mate, fars, width, height, after):
    return call(
        hot_final_kernel,
        "hot_final",
        after,
        (keep, mate, *fars),
        vmem(2 + len(fars)),
        [sds((height, width), F32), sds((height, keep.shape[1] - width), F32)],
        keep.size,
        4 * keep.size,
    )


def cold_delta_kernel(cap, rank, first, count, ids_ref, down_ref, got_ref, *rest):
    out_refs = rest[:count]
    wide_ref = rest[count]
    flat, width = down_ref.shape
    lo, hi = first * cap, (first + count) * cap
    total = cold_out_of(got_ref, rank, ids_ref.shape[1])[:, lo:hi]
    id_col = column(ids_ref[:, lo:hi]).astype(I32)
    wide_ref[...] = spread_columns(total, id_col, flat // rank)
    step = divide(width, 4)
    for j in range(width // step):
        at = slice(j * step, (j + 1) * step)
        delta = mm(wide_ref[...], down_ref[:, at]).astype(BF16)
        for k in range(count):
            out_refs[k][:, at] = delta[k * cap : (k + 1) * cap, :]


def cold_delta(ids, cold_down, got, cap, rank, first, count, after):
    flat, width = cold_down.shape
    return call(
        functools.partial(cold_delta_kernel, cap, rank, first, count),
        "cold_delta",
        after,
        (ids, cold_down, got),
        vmem(3),
        [sds((cap, width), BF16)] * count,
        2 * flat * count * cap * width,
        2 * flat * width + 2 * count * cap * width,
        scratch=[pltpu.VMEM((count * cap, flat), BF16)],
    )


def cold_in_kernel(peers, cap, rank, ids_ref, down_ref, *rest):
    rx_refs = rest[:peers]
    out_ref, xs_ref = rest[peers:]
    adapters = down_ref.shape[0] // rank
    join(rx_refs, xs_ref, cap)
    id_row = ids_ref[0:1, :]
    group = divide(adapters, 2)
    total = jnp.zeros(out_ref.shape[1:], F32)
    for c in range(adapters // group):
        part = mm(down_ref[c * group * rank : (c + 1) * group * rank, :], xs_ref[...], NT)
        total += fold(part, id_row, float(c * group), group, rank)
    for q in range(out_ref.shape[0]):
        out_ref[q] = total


def cold_in(ids, cold_down, rx, cap, rank, parts, after):
    peers = len(rx)
    flat, width = cold_down.shape
    slots = ids.shape[1]
    return call(
        functools.partial(cold_in_kernel, peers, cap, rank),
        "cold_in",
        after,
        (ids, cold_down, *rx),
        vmem(2 + peers),
        [sds((parts, rank, slots), F32), sds((slots, width), BF16)],
        2 * flat * slots * width,
        2 * (flat + slots) * width,
    )


def cold_down_grad_kernel(rank, ids_ref, xs_ref, got_ref, out_ref, so_ref, wide_ref):
    i = pl.program_id(0)
    group = out_ref.shape[0] // rank

    @pl.when(i == 0)
    def _():
        so_ref[...] = cold_out_of(got_ref, rank, ids_ref.shape[1])

    shifted = ids_ref[0:1, :].astype(I32) - i * group
    spread_rows(wide_ref, so_ref[...], shifted, 0, group)
    out_ref[...] = mm(wide_ref[...], xs_ref[...])


def cold_down_gradient(ids, got, xs, rank, adapters, after):
    slots, width = xs.shape
    flat = adapters * rank
    group = divide(adapters, 8) * rank
    return call(
        functools.partial(cold_down_grad_kernel, rank),
        "cold_down_grad",
        after,
        (ids, xs, got),
        [whole((8, slots)), whole((slots, width)), whole(got.shape)],
        [sds((flat, width), F32)],
        2 * flat * slots * width,
        4 * flat * width + 2 * slots * width,
        out_specs=[pl.BlockSpec((group, width), lambda i: (i, 0))],
        scratch=[pltpu.VMEM((rank, slots), F32), pltpu.VMEM((group, slots), BF16)],
        grid=(flat // group,),
    )


def cold_up_grad_kernel(rank, ids_ref, dys_ref, *rest):
    in_refs = rest[:-3]
    out_ref, si_ref, wide_ref = rest[-3:]
    i = pl.program_id(0)
    group = out_ref.shape[0] // rank

    @pl.when(i == 0)
    def _():
        si_ref[...] = scaled(sum((r[0] for r in in_refs[1:]), in_refs[0][0]))

    shifted = ids_ref[0:1, :].astype(I32) - i * group
    spread_rows(wide_ref, si_ref[...], shifted, 0, group)
    out_ref[...] = mm(wide_ref[...], dys_ref[...])


def cold_up_gradient(ids, ins, dys, rank, adapters, after):
    slots, kv = dys.shape
    flat = adapters * rank
    group = divide(adapters, 2) * rank

    def body(*refs):
        cold_up_grad_kernel(rank, *refs)

    return call(
        body,
        "cold_up_grad",
        after,
        (ids, dys, *ins),
        [whole((8, slots)), whole((slots, kv))] + [whole(v.shape) for v in ins],
        [sds((flat, kv), F32)],
        2 * flat * slots * kv,
        4 * flat * kv + 2 * slots * kv,
        out_specs=[pl.BlockSpec((group, kv), lambda i: (i, 0))],
        scratch=[pltpu.VMEM((rank, slots), F32), pltpu.VMEM((group, slots), BF16)],
        grid=(flat // group,),
    )


def position_matrix(rows_ref, first, count):
    tokens = rows_ref.shape[1]
    as_float = jnp.broadcast_to(rows_ref[2:3, :], (8, tokens)).astype(F32)
    pos = column(as_float).astype(I32) - first
    return jnp.where(lax.broadcasted_iota(I32, (tokens, count), 1) == pos, 1.0, 0.0).astype(BF16)


def local_terms_kernel(near, cap, rank, rows_ref, hd_ref, got_ref, *rest):
    near_refs = rest[:near]
    out_ref, place_ref, left_ref, right_ref = rest[near:]
    flat, width = hd_ref.shape
    tokens = rows_ref.shape[1]
    total = hot_out_of(got_ref, rank)
    as_float = jnp.broadcast_to(rows_ref[0:1, :], (8, tokens)).astype(F32)
    id_col = column(as_float).astype(I32)
    left_ref[:, 0:flat] = spread_columns(total, id_col, flat // rank)
    left_ref[:, flat : flat + near * cap] = position_matrix(rows_ref, 0, near * cap)
    place_ref[...] = position_matrix(rows_ref, near * cap, place_ref.shape[1])
    step = divide(width, 4)
    for j in range(width // step):
        at = slice(j * step, (j + 1) * step)
        right_ref[0:flat, :] = hd_ref[:, at]
        for k in range(near):
            right_ref[flat + k * cap : flat + (k + 1) * cap, :] = near_refs[k][:, at]
        out_ref[:, at] = mm(left_ref[...], right_ref[...]).astype(BF16)


def local_terms(rows, hot_down, got, nears, far, cap, rank, after):
    flat, width = hot_down.shape
    tokens = rows.shape[1]
    near = len(nears)
    depth = flat + near * cap
    return call(
        functools.partial(local_terms_kernel, near, cap, rank),
        "local_terms",
        after,
        (rows, hot_down, got, *nears),
        vmem(3 + near),
        [sds((tokens, width), BF16), sds((tokens, far * cap), BF16)],
        2 * tokens * width * depth,
        2 * width * (tokens + depth),
        scratch=[
            pltpu.VMEM((tokens, depth), BF16),
            pltpu.VMEM((depth, divide(width, 4)), BF16),
        ],
    )


def base_kernel(first, count, t_ref, w_ref, local_ref, *rest):
    block_refs = rest[:count]
    part_refs = rest[count:-3]
    out_ref, passed_ref, dy_ref = rest[-3:]
    passed_ref[...] = sum((r[...] for r in part_refs[1:]), part_refs[0][...])
    t = t_ref[0]
    kv = block_refs[0].shape[1] // 2
    rows = slice(first, first + out_ref.shape[0])
    k = 0
    for ref in block_refs:
        for c in range(ref.shape[1] // kv):
            lanes = pl.ds(pl.multiple_of((t ^ k) * kv, kv), kv)
            dy_ref[:, lanes] = ref[:, c * kv : (c + 1) * kv]
            k += 1
    for at in pieces_of(w_ref.shape[0]):
        out_ref[:, at] = mm(dy_ref[...], w_ref[at, :], NT) + local_ref[rows, at].astype(F32)


def base(t, weight, local, blocks, first, sums, after):
    width, kv_all = weight.shape
    rows = blocks[0].shape[0]
    return call(
        functools.partial(base_kernel, first, len(blocks)),
        "base",
        after,
        (t, weight, local, *blocks, *sums),
        [smem()] + vmem(2 + len(blocks) + len(sums)),
        [sds((rows, width), F32), sds(sums[0].shape, F32)],
        2 * rows * width * kv_all,
        2 * width * kv_all + 6 * rows * width,
        scratch=[pltpu.VMEM((rows, kv_all), BF16)],
    )


def final_kernel(cap, far, place_ref, *rest):
    base_refs = rest[: len(rest) - far - 4]
    far_refs = rest[len(base_refs) : len(base_refs) + far]
    out_ref, far_ref, held_ref, sems = rest[len(base_refs) + far :]
    for k, ref in enumerate(far_refs):
        far_ref[k * cap : (k + 1) * cap, :] = ref[...]
    copies = []
    first = 0
    for ref in base_refs:
        for piece in pieces_of(ref.shape[0], 2):
            at = slice(first + piece.start, first + piece.stop)
            held_ref[at, :] = (ref[piece, :] + mm(place_ref[at, :], far_ref[...])).astype(BF16)
            copies.append(
                pltpu.make_async_copy(held_ref.at[at], out_ref.at[at], sems.at[len(copies)])
            )
            copies[-1].start()
        first += ref.shape[0]
    for copy in copies:
        copy.wait()


def final(place, bases, fars, cap, after):
    tokens = place.shape[0]
    width = bases[0].shape[1]
    far = len(fars)
    return call(
        functools.partial(final_kernel, cap, far),
        "final",
        after,
        (place, *bases, *fars),
        vmem(1 + len(bases) + far),
        [sds((tokens, width), BF16)],
        2 * tokens * width * far * cap,
        6 * tokens * width,
        out_specs=anywhere(1),
        scratch=[
            pltpu.VMEM((far * cap, width), BF16),
            pltpu.VMEM((tokens, width), BF16),
            pltpu.SemaphoreType.DMA((2 * len(bases),)),
        ],
    )


def swap(value, axis, k):
    count = lax.axis_size(axis)
    return lax.ppermute(value, axis, [(i, i ^ k) for i in range(count)])


def gather_rest(pair, parts):
    blocks, held = [pair], 2
    while held < parts:
        together = blocks[0] if len(blocks) == 1 else jnp.concatenate(blocks, axis=1)
        blocks.append(swap(together, "tensor", held))
        held *= 2
    return blocks


def over_tensor(part, parts):
    return [part] + [swap(part, "tensor", k) for k in range(1, parts)]


def shards(
    tokens_in,
    grad_out,
    value_weight,
    token_adapter,
    adapter_home,
    cold_down,
    cold_up,
    hot_down,
    hot_up,
):
    peers = lax.axis_size("dp")
    parts = lax.axis_size("tensor")
    tokens, width = tokens_in.shape
    kv = grad_out.shape[1]
    cap = tokens // (2 * peers)
    cold_here, rank, _ = cold_down.shape
    hot = hot_down.shape[0]
    hot_here = hot // peers
    near = 2
    flat_cold_down = cold_down.reshape(cold_here * rank, width)
    flat_cold_up = cold_up.reshape(cold_here * rank, kv)
    flat_hot_down = hot_down.reshape(hot * rank, width)
    flat_hot_up = hot_up.reshape(hot * rank, kv)
    me = lax.axis_index("dp").astype(I32).reshape(1)

    t = lax.axis_index("tensor").astype(I32).reshape(1)
    dy_next = swap(grad_out, "tensor", 1)
    x = tokens_in
    sd, rows, pick, dy, token = route(
        me, token_adapter, adapter_home, grad_out, peers, cap, cold_here, hot_here
    )
    rd = [sd[0]] + [swap(sd[k], "dp", k) for k in range(1, peers)]
    (hot_part,), token = hot_products(
        rows, x, flat_hot_down, grad_out, flat_hot_up, rank, token
    )
    (pay, ids, held_dy), token = cold_out(hot_part, flat_cold_up, dy_next, rd, cap, rank, 1, token)
    far_x, token = pack(pick, x, cap, near, peers - near, token)
    far_x = [swap(far_x[k - near], "dp", k) for k in range(near, peers)]
    early = 5 * divide(tokens, 16)
    (got, *pairs), token = sum_pieces(
        over_tensor(pay, parts), dy, dy_next, (early, tokens - early), token
    )
    dys = [gather_rest(pair, parts) for pair in pairs]
    near_x, token = pack(pick, x, cap, 0, near, token)
    rx = [near_x[0], swap(near_x[1], "dp", 1)] + far_x
    (in_part, xs), token = cold_in(ids, flat_cold_down, rx, cap, rank, 1, token)
    in_next = swap(in_part, "tensor", 1)
    near_delta, token = cold_delta(ids, flat_cold_down, got, cap, rank, 0, near, token)
    near_back = [near_delta[0]] + [swap(near_delta[k], "dp", k) for k in range(1, near)]
    (keep, *sends), token = hot_grads(
        rows, x, dy, got, dys[0][-1], rank, hot, peers, token
    )
    mates = [swap(send, "dp", 1) for send in sends]
    height = hot_here * rank
    aways, token = hot_away(keep, mates[1:], token)
    aways = [swap(aways[c - 1], "dp", 2 * c) for c in range(1, peers // 2)]
    far_delta, token = cold_delta(ids, flat_cold_down, got, cap, rank, near, peers - near, token)
    far_back = [swap(far_delta[k - near], "dp", k) for k in range(near, peers)]
    (cold_down_grad,), token = cold_down_gradient(ids, got, xs, rank, cold_here, token)
    (local, place), token = local_terms(
        rows, flat_hot_down, got, near_back, peers - near, cap, rank, token
    )
    (hot_down_grad, hot_up_grad), token = hot_final(keep, mates[0], aways, width, height, token)
    (base_first, _), token = base(t, value_weight, local, dys[0], 0, (ids,), token)
    (base_last, passed), token = base(
        t, value_weight, local, dys[1], early, (in_part, in_next), token
    )
    ins = [passed] + [swap(passed, "tensor", k) for k in range(2, parts, 2)]
    (input_gradient,), token = final(place, (base_first, base_last), far_back, cap, token)
    (cold_up_grad,), token = cold_up_gradient(ids, ins, held_dy, rank, cold_here, token)
    return (
        input_gradient,
        cold_down_grad.reshape(cold_here, rank, width),
        cold_up_grad.reshape(cold_here, rank, kv),
        hot_down_grad.reshape(hot_here, rank, width),
        hot_up_grad.reshape(hot_here, rank, kv),
    )


def solution(mesh):
    in_specs = (
        P(("groups", "dp"), "tensor"),
        P(("groups", "dp"), "tensor"),
        P("tensor", None),
        P(("groups", "dp")),
        P("groups"),
        P(("groups", "dp"), None, "tensor"),
        P(("groups", "dp"), None, "tensor"),
        P("groups", None, "tensor"),
        P("groups", None, "tensor"),
    )
    out_specs = (
        P(("groups", "dp"), "tensor"),
        P(("groups", "dp"), None, "tensor"),
        P(("groups", "dp"), None, "tensor"),
        P(("groups", "dp"), None, "tensor"),
        P(("groups", "dp"), None, "tensor"),
    )
    return jax.shard_map(shards, mesh=mesh, in_specs=in_specs, out_specs=out_specs, check_vma=False)
```

```python
import functools

import jax
import jax.numpy as jnp
from jax import lax
from jax.experimental import pallas as pl
from jax.experimental.pallas import tpu as pltpu
from jax.sharding import PartitionSpec as P

ADAPTER_SCALE = 2.0
VMEM_LIMIT = 10 * 1024 * 1024
COST_SCALE = 0.3
ROUTE_MOVED = 400
BF16 = jnp.bfloat16
F32 = jnp.float32
I32 = jnp.int32
NN = (((1,), (0,)), ((), ()))
NT = (((1,), (1,)), ((), ()))


def mm(a, b, dims=NN):
    return lax.dot_general(a, b, dims, preferred_element_type=F32)


def sds(shape, dtype):
    return jax.ShapeDtypeStruct(shape, dtype)


def whole(shape):
    return pl.BlockSpec(shape, lambda *_: (0,) * len(shape))


def vmem(count):
    return [pl.BlockSpec(memory_space=pltpu.VMEM)] * count


def smem():
    return pl.BlockSpec(memory_space=pltpu.SMEM)


def anywhere(count):
    return [pl.BlockSpec(memory_space=pl.ANY)] * count


def params():
    return pltpu.CompilerParams(vmem_limit_bytes=VMEM_LIMIT)


def cost(flops, moved):
    return pl.CostEstimate(
        flops=int(COST_SCALE * flops), bytes_accessed=int(COST_SCALE * moved), transcendentals=0
    )


def join(refs, into, rows):
    for k, ref in enumerate(refs):
        into[k * rows : (k + 1) * rows, :] = ref[0:rows, 0 : into.shape[1]]


def join_last(refs, into, rows):
    for k, ref in enumerate(refs):
        into[k * rows : (k + 1) * rows, :] = ref[0:rows, ref.shape[1] - into.shape[1] :]


TOKEN = (8, 128)


def call(body, name, after, args, in_specs, out_shape, flops, moved, out_specs=None, scratch=(), grid=None):
    taken, given = len(args), len(out_shape)
    chained = [] if after is None else [after]

    def kernel(*refs):
        outs = refs[taken + len(chained) :]
        body(*refs[:taken], *outs[:given], *outs[given + 1 :])
        outs[given][...] = jnp.zeros(TOKEN, F32)

    more = {} if grid is None else {"grid": grid}
    results = pl.pallas_call(
        kernel,
        in_specs=list(in_specs) + anywhere(len(chained)),
        out_specs=list(out_specs or vmem(given)) + (vmem(1) if grid is None else [whole(TOKEN)]),
        out_shape=list(out_shape) + [sds(TOKEN, F32)],
        scratch_shapes=list(scratch),
        compiler_params=params(),
        cost_estimate=cost(flops, moved),
        name=name,
        **more,
    )(*args, *chained)
    return results[:given], results[given]


def divide(total, parts):
    return total // parts if total % parts == 0 else total


def pieces_of(total, parts=4):
    step = divide(total, parts)
    return [slice(k * step, (k + 1) * step) for k in range(total // step)]


def column(row_8):
    return jnp.transpose(row_8)[:, 0:1]


def spread_columns(scaled_t, id_col, adapters):
    rank = scaled_t.shape[0]
    count = scaled_t.shape[1]
    scaled = jnp.transpose(scaled_t).astype(BF16)
    width = adapters * rank
    lane = lax.broadcasted_iota(I32, (rank, width), 1)
    sub = lax.broadcasted_iota(I32, (rank, width), 0)
    tile = jnp.where(lax.rem(lane, rank) == sub, 1.0, 0.0).astype(BF16)
    tiled = mm(scaled, tile)
    own = lax.div(lax.broadcasted_iota(I32, (count, width), 1), rank)
    return jnp.where(own == id_col, tiled, 0.0).astype(BF16)


def spread_rows(out_ref, scaled_t, id_row, first, adapters):
    rank = scaled_t.shape[0]
    for a in range(adapters):
        out_ref[a * rank : (a + 1) * rank, :] = jnp.where(
            id_row == first + a, scaled_t, 0.0
        ).astype(BF16)


def fold(product, id_row, first, adapters, rank):
    total = jnp.zeros((rank, product.shape[1]), F32)
    for a in range(adapters):
        total += jnp.where(id_row == first + a, product[a * rank : (a + 1) * rank, :], 0.0)
    return total


def scaled(total):
    return (ADAPTER_SCALE * total).astype(BF16).astype(F32)


def route_kernel(peers, cap, cold_here, hot_here, me_ref, adapter_ref, home_ref, dy_ref, *rest):
    sd_refs = rest[:peers]
    rows_ref, pick_ref, held_ref = rest[peers:]
    held_ref[...] = dy_ref[...]
    adapters = home_ref.shape[1]
    tokens = adapter_ref.shape[1]
    slots = peers * cap
    me = me_ref[0]
    adapter = adapter_ref[...]
    home = home_ref[...]
    sub8 = lax.broadcasted_iota(I32, (8, adapters), 0)
    digits = jnp.where(
        sub8 == 0, lax.shift_right_logical(home, 5), jnp.where(sub8 == 1, home & 31, 0)
    ).astype(F32).astype(BF16)
    onehot = jnp.where(
        lax.broadcasted_iota(I32, (adapters, tokens), 0) == adapter, 1.0, 0.0
    ).astype(BF16)
    found = mm(digits, onehot).astype(I32)
    row = found[0:1, :] * 32 + found[1:2, :]
    has = adapter < adapters
    cold_total = cold_here * peers
    cold = has & (row < cold_total)
    hot = has & (row >= cold_total)
    dest = jnp.zeros_like(row)
    hot_row = row - cold_total
    hot_dest = jnp.zeros_like(row)
    for p in range(1, peers):
        dest += jnp.where(row >= p * cold_here, 1, 0)
        hot_dest += jnp.where(hot_row >= p * hot_here, 1, 0)
    dest = jnp.minimum(dest, peers - 1)
    local = row - dest * cold_here
    turn = dest ^ me
    height = max(8, peers)
    hits = jnp.where((lax.broadcasted_iota(I32, (height, tokens), 0) == turn) & cold, 1, 0)
    running = hits
    lane = lax.broadcasted_iota(I32, (height, tokens), 1)
    step = 1
    while step < tokens:
        running += jnp.where(lane >= step, pltpu.roll(running, step, 1), 0)
        step *= 2
    within = jnp.sum(hits * (running - 1), axis=0, keepdims=True)
    position = jnp.where(cold, turn * cap + within, slots)
    hot_nat = jnp.where(hot, hot_row, hot_here * peers)
    hot_turn = jnp.where(
        hot,
        (hot_dest ^ me) * hot_here + hot_row - hot_dest * hot_here,
        hot_here * peers,
    )
    sub = lax.broadcasted_iota(I32, (8, tokens), 0)
    rows_ref[...] = jnp.where(
        sub == 0, hot_nat, jnp.where(sub == 1, hot_turn, jnp.where(sub == 2, position, 0))
    )
    pick_ref[...] = jnp.where(
        lax.broadcasted_iota(I32, (slots, tokens), 0) == position, 1.0, 0.0
    ).astype(BF16)
    packed = mm(pick_ref[...], dy_ref[...]).astype(BF16)
    ids = mm(jnp.broadcast_to(local.astype(F32), (16, tokens)).astype(BF16), pick_ref[...], NT)
    for k in range(peers):
        sd_refs[k][0:cap, :] = packed[k * cap : (k + 1) * cap, :]
        sd_refs[k][cap : cap + 16, :] = jnp.zeros((16, sd_refs[k].shape[1]), BF16)
        sd_refs[k][cap : cap + 16, 0:cap] = ids[:, k * cap : (k + 1) * cap].astype(BF16)


def route(me, token_adapter, adapter_home, dy, peers, cap, cold_here, hot_here):
    tokens, kv = dy.shape
    slots = peers * cap
    outs, token = call(
        functools.partial(route_kernel, peers, cap, cold_here, hot_here),
        "route",
        None,
        (me, token_adapter.reshape(1, -1), adapter_home.reshape(1, -1), dy),
        [smem()] + vmem(3),
        [sds((cap + 16, kv), BF16)] * peers
        + [sds((8, tokens), I32), sds((slots, tokens), BF16), sds(dy.shape, BF16)],
        2 * slots * tokens * kv,
        ROUTE_MOVED * tokens * kv,
    )
    return outs[:peers], *outs[peers:], token


def pack_kernel(first, cap, pick_ref, x_ref, *out_refs):
    rows = slice(first * cap, (first + len(out_refs)) * cap)
    for at in pieces_of(x_ref.shape[1]):
        packed = mm(pick_ref[rows, :], x_ref[:, at]).astype(BF16)
        for k, ref in enumerate(out_refs):
            ref[:, at] = packed[k * cap : (k + 1) * cap, :]


def pack(pick, x, cap, first, count, after):
    tokens, width = x.shape
    return call(
        functools.partial(pack_kernel, first, cap),
        "pack",
        after,
        (pick, x),
        vmem(2),
        [sds((cap, width), BF16)] * count,
        2 * count * cap * tokens * width,
        2 * (tokens + count * cap) * width,
    )


def hot_products_kernel(rank, rows_ref, x_ref, hd_ref, dy_ref, hu_ref, out_ref):
    hot = hd_ref.shape[0] // rank
    tokens = x_ref.shape[0]
    half = divide(tokens, 2)
    for c in range(tokens // half):
        at = slice(c * half, (c + 1) * half)
        row = rows_ref[0:1, at]
        out_ref[0:rank, at] = fold(mm(hu_ref[...], dy_ref[at, :], NT), row, 0, hot, rank)
        out_ref[rank : 2 * rank, at] = fold(mm(hd_ref[...], x_ref[at, :], NT), row, 0, hot, rank)


def hot_products(rows, x, hot_down, dy, hot_up, rank, after):
    tokens, width = x.shape
    flat = hot_down.shape[0]
    kv = dy.shape[1]
    return call(
        functools.partial(hot_products_kernel, rank),
        "hot_products",
        after,
        (rows, x, hot_down, dy, hot_up),
        vmem(5),
        [sds((2 * rank, tokens), F32)],
        2 * flat * tokens * (width + kv),
        2 * (tokens + flat) * width,
    )


def cold_out_kernel(peers, cap, rank, hot_ref, up_ref, _, *rest):
    rd_refs = rest[:peers]
    pay_ref, ids_ref, dys_ref = rest[peers:]
    adapters = up_ref.shape[0] // rank
    slots = peers * cap
    join_last(rd_refs, dys_ref, cap)
    kv = up_ref.shape[1]
    ids = [
        r[cap : cap + 16, r.shape[1] - kv : r.shape[1] - kv + cap].astype(F32)[0:8]
        for r in rd_refs
    ]
    ids_8 = jnp.concatenate(ids, axis=1)
    ids_ref[...] = ids_8
    id_row = ids_8[0:1, :]
    group = divide(adapters, 8)
    total = jnp.zeros((rank, slots), F32)
    for c in range(adapters // group):
        part = mm(up_ref[c * group * rank : (c + 1) * group * rank, :], dys_ref[...], NT)
        total += fold(part, id_row, float(c * group), group, rank)
    half = rank // 2
    folded = jnp.concatenate([total[0:half], total[half:rank]], axis=1)
    piece = pay_ref.shape[2]
    for q in range(pay_ref.shape[0]):
        at = slice(q * piece, (q + 1) * piece)
        pay_ref[q, 0 : 2 * rank, :] = hot_ref[:, at]
        pay_ref[q, 2 * rank : 2 * rank + half, :] = folded[:, at]


def cold_out(hot_part, cold_up, before, rd, cap, rank, parts, after):
    peers = len(rd)
    flat, kv = cold_up.shape
    slots = peers * cap
    tokens = hot_part.shape[1]
    return call(
        functools.partial(cold_out_kernel, peers, cap, rank),
        "cold_out",
        after,
        (hot_part, cold_up, before, *rd),
        vmem(2) + anywhere(1) + vmem(peers),
        [sds((parts, 2 * rank + rank // 2, tokens // parts), F32), sds((8, slots), F32), sds((slots, kv), BF16)],
        2 * flat * slots * kv,
        2 * (flat + slots) * kv,
    )


def sum_pieces_kernel(parts, dy_ref, next_ref, *refs):
    pay_refs = refs[:parts]
    out_ref, *pair_refs = refs[parts:]
    total = pay_refs[0][0]
    for ref in pay_refs[1:]:
        total += ref[0]
    filled, width = out_ref.shape[1:]
    total = (ADAPTER_SCALE * total).astype(BF16).astype(F32)
    rest = jnp.zeros((filled - total.shape[0], width), F32)
    out_ref[0] = jnp.concatenate([total, rest], axis=0).astype(BF16)
    kv = dy_ref.shape[1]
    first = 0
    for ref in pair_refs:
        at = slice(first, first + ref.shape[0])
        first += ref.shape[0]
        ref[:, 0:kv] = dy_ref[at, :]
        ref[:, kv:] = next_ref[at, :]


def sum_pieces(pays, dy, dy_next, cuts, after):
    _, height, width = pays[0].shape
    filled = -(-height // 16) * 16
    return call(
        functools.partial(sum_pieces_kernel, len(pays)),
        "sum_pieces",
        after,
        (dy, dy_next, *pays),
        vmem(2 + len(pays)),
        [sds((1, filled, width), BF16)] + [sds((rows, 2 * dy.shape[1]), BF16) for rows in cuts],
        len(pays) * pays[0].size,
        4 * len(pays) * pays[0].size,
    )


def gathered(got_ref, first, last):
    return jnp.concatenate(
        [got_ref[q, first:last, :].astype(F32) for q in range(got_ref.shape[0])], axis=1
    )


def hot_out_of(got_ref, rank):
    return gathered(got_ref, 0, rank)


def hot_in_of(got_ref, rank):
    return gathered(got_ref, rank, 2 * rank)


def cold_out_of(got_ref, rank, slots):
    half = rank // 2
    folded = gathered(got_ref, 2 * rank, got_ref.shape[1])[0:half]
    return jnp.concatenate([folded[:, 0:slots], folded[:, slots : 2 * slots]], axis=0)


def hot_grads_kernel(peers, rank, hot, rows_ref, x_ref, dy_ref, got_ref, _, keep_ref, *rest):
    send_refs, wide_ref = rest[:-1], rest[-1]
    width = x_ref.shape[1]
    kv = dy_ref.shape[1]
    block = hot // peers * rank

    def put(product, column):
        for k in range(peers):
            piece = product[k * block : (k + 1) * block, :]
            at = slice((k // 2) * block, (k // 2 + 1) * block)
            if k % 2 == 0:
                keep_ref[at, column] = piece
            else:
                send_refs[k // 2][:, column] = piece.astype(BF16)

    turn = rows_ref[1:2, :]
    spread_rows(wide_ref, hot_in_of(got_ref, rank), turn, 0, hot)
    put(mm(wide_ref[...], dy_ref[...]), slice(width, width + kv))
    spread_rows(wide_ref, hot_out_of(got_ref, rank), turn, 0, hot)
    step = divide(width, 4)
    for j in range(width // step):
        at = slice(j * step, (j + 1) * step)
        put(mm(wide_ref[...], x_ref[:, at]), at)


def hot_grads(rows, x, dy, got, before, rank, hot, peers, after):
    tokens, width = x.shape
    kv = dy.shape[1]
    flat = hot * rank
    half = flat // 2
    return call(
        functools.partial(hot_grads_kernel, peers, rank, hot),
        "hot_grads",
        after,
        (rows, x, dy, got, before),
        vmem(4) + anywhere(1),
        [sds((half, width + kv), F32)]
        + [sds((flat // peers, width + kv), BF16)] * (peers // 2),
        2 * flat * tokens * (width + kv),
        2 * tokens * width + 6 * half * width,
        scratch=[pltpu.VMEM((flat, tokens), BF16)],
    )


def hot_away_kernel(count, keep_ref, *rest):
    for c in range(count):
        mate_ref, out_ref = rest[c], rest[count + c]
        height = out_ref.shape[0]
        at = slice((c + 1) * height, (c + 2) * height)
        out_ref[...] = (keep_ref[at, :] + mate_ref[...].astype(F32)).astype(BF16)


def hot_away(keep, mates, after):
    count = len(mates)
    return call(
        functools.partial(hot_away_kernel, count),
        "hot_away",
        after,
        (keep, *mates),
        vmem(1 + count),
        [sds(mates[0].shape, BF16)] * count,
        keep.size,
        8 * keep.size,
    )


def hot_final_kernel(keep_ref, mate_ref, *rest):
    down_ref, up_ref = rest[-2:]
    height, width = down_ref.shape
    total = keep_ref[0:height, :] + mate_ref[0:height, :].astype(F32)
    for ref in rest[:-2]:
        total += ref[...].astype(F32)
    down_ref[...] = total[:, 0:width]
    up_ref[...] = total[:, width:]


def hot_final(keep, mate, fars, width, height, after):
    return call(
        hot_final_kernel,
        "hot_final",
        after,
        (keep, mate, *fars),
        vmem(2 + len(fars)),
        [sds((height, width), F32), sds((height, keep.shape[1] - width), F32)],
        keep.size,
        4 * keep.size,
    )


def cold_delta_kernel(cap, rank, first, count, ids_ref, down_ref, got_ref, *rest):
    out_refs = rest[:count]
    wide_ref = rest[count]
    flat, width = down_ref.shape
    lo, hi = first * cap, (first + count) * cap
    total = cold_out_of(got_ref, rank, ids_ref.shape[1])[:, lo:hi]
    id_col = column(ids_ref[:, lo:hi]).astype(I32)
    wide_ref[...] = spread_columns(total, id_col, flat // rank)
    step = divide(width, 4)
    for j in range(width // step):
        at = slice(j * step, (j + 1) * step)
        delta = mm(wide_ref[...], down_ref[:, at]).astype(BF16)
        for k in range(count):
            out_refs[k][:, at] = delta[k * cap : (k + 1) * cap, :]


def cold_delta(ids, cold_down, got, cap, rank, first, count, after):
    flat, width = cold_down.shape
    return call(
        functools.partial(cold_delta_kernel, cap, rank, first, count),
        "cold_delta",
        after,
        (ids, cold_down, got),
        vmem(3),
        [sds((cap, width), BF16)] * count,
        2 * flat * count * cap * width,
        2 * flat * width + 2 * count * cap * width,
        scratch=[pltpu.VMEM((count * cap, flat), BF16)],
    )


def cold_in_kernel(peers, cap, rank, ids_ref, down_ref, *rest):
    rx_refs = rest[:peers]
    out_ref, xs_ref = rest[peers:]
    adapters = down_ref.shape[0] // rank
    join(rx_refs, xs_ref, cap)
    id_row = ids_ref[0:1, :]
    group = divide(adapters, 2)
    total = jnp.zeros(out_ref.shape[1:], F32)
    for c in range(adapters // group):
        part = mm(down_ref[c * group * rank : (c + 1) * group * rank, :], xs_ref[...], NT)
        total += fold(part, id_row, float(c * group), group, rank)
    for q in range(out_ref.shape[0]):
        out_ref[q] = total


def cold_in(ids, cold_down, rx, cap, rank, parts, after):
    peers = len(rx)
    flat, width = cold_down.shape
    slots = ids.shape[1]
    return call(
        functools.partial(cold_in_kernel, peers, cap, rank),
        "cold_in",
        after,
        (ids, cold_down, *rx),
        vmem(2 + peers),
        [sds((parts, rank, slots), F32), sds((slots, width), BF16)],
        2 * flat * slots * width,
        2 * (flat + slots) * width,
    )


def cold_down_grad_kernel(rank, ids_ref, xs_ref, got_ref, out_ref, so_ref, wide_ref):
    i = pl.program_id(0)
    group = out_ref.shape[0] // rank

    @pl.when(i == 0)
    def _():
        so_ref[...] = cold_out_of(got_ref, rank, ids_ref.shape[1])

    shifted = ids_ref[0:1, :].astype(I32) - i * group
    spread_rows(wide_ref, so_ref[...], shifted, 0, group)
    out_ref[...] = mm(wide_ref[...], xs_ref[...])


def cold_down_gradient(ids, got, xs, rank, adapters, after):
    slots, width = xs.shape
    flat = adapters * rank
    group = divide(adapters, 8) * rank
    return call(
        functools.partial(cold_down_grad_kernel, rank),
        "cold_down_grad",
        after,
        (ids, xs, got),
        [whole((8, slots)), whole((slots, width)), whole(got.shape)],
        [sds((flat, width), F32)],
        2 * flat * slots * width,
        4 * flat * width + 2 * slots * width,
        out_specs=[pl.BlockSpec((group, width), lambda i: (i, 0))],
        scratch=[pltpu.VMEM((rank, slots), F32), pltpu.VMEM((group, slots), BF16)],
        grid=(flat // group,),
    )


def cold_up_grad_kernel(rank, ids_ref, dys_ref, *rest):
    in_refs = rest[:-3]
    out_ref, si_ref, wide_ref = rest[-3:]
    i = pl.program_id(0)
    group = out_ref.shape[0] // rank

    @pl.when(i == 0)
    def _():
        si_ref[...] = scaled(sum((r[0] for r in in_refs[1:]), in_refs[0][0]))

    shifted = ids_ref[0:1, :].astype(I32) - i * group
    spread_rows(wide_ref, si_ref[...], shifted, 0, group)
    out_ref[...] = mm(wide_ref[...], dys_ref[...])


def cold_up_gradient(ids, ins, dys, rank, adapters, after):
    slots, kv = dys.shape
    flat = adapters * rank
    group = divide(adapters, 4) * rank

    def body(*refs):
        cold_up_grad_kernel(rank, *refs)

    return call(
        body,
        "cold_up_grad",
        after,
        (ids, dys, *ins),
        [whole((8, slots)), whole((slots, kv))] + [whole(v.shape) for v in ins],
        [sds((flat, kv), F32)],
        2 * flat * slots * kv,
        4 * flat * kv + 2 * slots * kv,
        out_specs=[pl.BlockSpec((group, kv), lambda i: (i, 0))],
        scratch=[pltpu.VMEM((rank, slots), F32), pltpu.VMEM((group, slots), BF16)],
        grid=(flat // group,),
    )


def position_matrix(rows_ref, first, count):
    tokens = rows_ref.shape[1]
    as_float = jnp.broadcast_to(rows_ref[2:3, :], (8, tokens)).astype(F32)
    pos = column(as_float).astype(I32) - first
    return jnp.where(lax.broadcasted_iota(I32, (tokens, count), 1) == pos, 1.0, 0.0).astype(BF16)


def local_terms_kernel(near, cap, rank, rows_ref, hd_ref, got_ref, *rest):
    near_refs = rest[:near]
    out_ref, place_ref, left_ref, right_ref = rest[near:]
    flat, width = hd_ref.shape
    tokens = rows_ref.shape[1]
    total = hot_out_of(got_ref, rank)
    as_float = jnp.broadcast_to(rows_ref[0:1, :], (8, tokens)).astype(F32)
    id_col = column(as_float).astype(I32)
    left_ref[:, 0:flat] = spread_columns(total, id_col, flat // rank)
    left_ref[:, flat : flat + near * cap] = position_matrix(rows_ref, 0, near * cap)
    place_ref[...] = position_matrix(rows_ref, near * cap, place_ref.shape[1])
    step = divide(width, 4)
    for j in range(width // step):
        at = slice(j * step, (j + 1) * step)
        right_ref[0:flat, :] = hd_ref[:, at]
        for k in range(near):
            right_ref[flat + k * cap : flat + (k + 1) * cap, :] = near_refs[k][:, at]
        out_ref[:, at] = mm(left_ref[...], right_ref[...]).astype(BF16)


def local_terms(rows, hot_down, got, nears, far, cap, rank, after):
    flat, width = hot_down.shape
    tokens = rows.shape[1]
    near = len(nears)
    depth = flat + near * cap
    return call(
        functools.partial(local_terms_kernel, near, cap, rank),
        "local_terms",
        after,
        (rows, hot_down, got, *nears),
        vmem(3 + near),
        [sds((tokens, width), BF16), sds((tokens, far * cap), BF16)],
        2 * tokens * width * depth,
        2 * width * (tokens + depth),
        scratch=[
            pltpu.VMEM((tokens, depth), BF16),
            pltpu.VMEM((depth, divide(width, 4)), BF16),
        ],
    )


def base_kernel(first, count, t_ref, w_ref, local_ref, *rest):
    block_refs = rest[:count]
    part_refs = rest[count:-3]
    out_ref, passed_ref, dy_ref = rest[-3:]
    passed_ref[...] = sum((r[...] for r in part_refs[1:]), part_refs[0][...])
    t = t_ref[0]
    kv = block_refs[0].shape[1] // 2
    rows = slice(first, first + out_ref.shape[0])
    k = 0
    for ref in block_refs:
        for c in range(ref.shape[1] // kv):
            lanes = pl.ds(pl.multiple_of((t ^ k) * kv, kv), kv)
            dy_ref[:, lanes] = ref[:, c * kv : (c + 1) * kv]
            k += 1
    for at in pieces_of(w_ref.shape[0]):
        out_ref[:, at] = mm(dy_ref[...], w_ref[at, :], NT) + local_ref[rows, at].astype(F32)


def base(t, weight, local, blocks, first, sums, after):
    width, kv_all = weight.shape
    rows = blocks[0].shape[0]
    return call(
        functools.partial(base_kernel, first, len(blocks)),
        "base",
        after,
        (t, weight, local, *blocks, *sums),
        [smem()] + vmem(2 + len(blocks) + len(sums)),
        [sds((rows, width), F32), sds(sums[0].shape, F32)],
        2 * rows * width * kv_all,
        2 * width * kv_all + 6 * rows * width,
        scratch=[pltpu.VMEM((rows, kv_all), BF16)],
    )


def final_kernel(cap, far, place_ref, *rest):
    base_refs = rest[: len(rest) - far - 4]
    far_refs = rest[len(base_refs) : len(base_refs) + far]
    out_ref, far_ref, held_ref, sems = rest[len(base_refs) + far :]
    for k, ref in enumerate(far_refs):
        far_ref[k * cap : (k + 1) * cap, :] = ref[...]
    copies = []
    first = 0
    for ref in base_refs:
        for piece in pieces_of(ref.shape[0], 2):
            at = slice(first + piece.start, first + piece.stop)
            held_ref[at, :] = (ref[piece, :] + mm(place_ref[at, :], far_ref[...])).astype(BF16)
            copies.append(
                pltpu.make_async_copy(held_ref.at[at], out_ref.at[at], sems.at[len(copies)])
            )
            copies[-1].start()
        first += ref.shape[0]
    for copy in copies:
        copy.wait()


def final(place, bases, fars, cap, after):
    tokens = place.shape[0]
    width = bases[0].shape[1]
    far = len(fars)
    return call(
        functools.partial(final_kernel, cap, far),
        "final",
        after,
        (place, *bases, *fars),
        vmem(1 + len(bases) + far),
        [sds((tokens, width), BF16)],
        2 * tokens * width * far * cap,
        6 * tokens * width,
        out_specs=anywhere(1),
        scratch=[
            pltpu.VMEM((far * cap, width), BF16),
            pltpu.VMEM((tokens, width), BF16),
            pltpu.SemaphoreType.DMA((2 * len(bases),)),
        ],
    )


def swap(value, axis, k):
    count = lax.axis_size(axis)
    return lax.ppermute(value, axis, [(i, i ^ k) for i in range(count)])


def gather_rest(pair, parts):
    blocks, held = [pair], 2
    while held < parts:
        together = blocks[0] if len(blocks) == 1 else jnp.concatenate(blocks, axis=1)
        blocks.append(swap(together, "tensor", held))
        held *= 2
    return blocks


def over_tensor(part, parts):
    return [part] + [swap(part, "tensor", k) for k in range(1, parts)]


def shards(
    tokens_in,
    grad_out,
    value_weight,
    token_adapter,
    adapter_home,
    cold_down,
    cold_up,
    hot_down,
    hot_up,
):
    peers = lax.axis_size("dp")
    parts = lax.axis_size("tensor")
    tokens, width = tokens_in.shape
    kv = grad_out.shape[1]
    cap = tokens // (2 * peers)
    cold_here, rank, _ = cold_down.shape
    hot = hot_down.shape[0]
    hot_here = hot // peers
    near = 2
    flat_cold_down = cold_down.reshape(cold_here * rank, width)
    flat_cold_up = cold_up.reshape(cold_here * rank, kv)
    flat_hot_down = hot_down.reshape(hot * rank, width)
    flat_hot_up = hot_up.reshape(hot * rank, kv)
    me = lax.axis_index("dp").astype(I32).reshape(1)

    t = lax.axis_index("tensor").astype(I32).reshape(1)
    dy_next = swap(grad_out, "tensor", 1)
    x = tokens_in
    sd, rows, pick, dy, token = route(
        me, token_adapter, adapter_home, grad_out, peers, cap, cold_here, hot_here
    )
    rd = [sd[0]] + [swap(sd[k], "dp", k) for k in range(1, peers)]
    (hot_part,), token = hot_products(
        rows, x, flat_hot_down, grad_out, flat_hot_up, rank, token
    )
    (pay, ids, held_dy), token = cold_out(hot_part, flat_cold_up, dy_next, rd, cap, rank, 1, token)
    far_x, token = pack(pick, x, cap, near, peers - near, token)
    far_x = [swap(far_x[k - near], "dp", k) for k in range(near, peers)]
    early = 5 * divide(tokens, 16)
    (got, *pairs), token = sum_pieces(
        over_tensor(pay, parts), dy, dy_next, (early, tokens - early), token
    )
    dys = [gather_rest(pair, parts) for pair in pairs]
    near_x, token = pack(pick, x, cap, 0, near, token)
    rx = [near_x[0], swap(near_x[1], "dp", 1)] + far_x
    (in_part, xs), token = cold_in(ids, flat_cold_down, rx, cap, rank, 1, token)
    in_next = swap(in_part, "tensor", 1)
    near_delta, token = cold_delta(ids, flat_cold_down, got, cap, rank, 0, near, token)
    near_back = [near_delta[0]] + [swap(near_delta[k], "dp", k) for k in range(1, near)]
    (keep, *sends), token = hot_grads(
        rows, x, dy, got, dys[0][-1], rank, hot, peers, token
    )
    mates = [swap(send, "dp", 1) for send in sends]
    height = hot_here * rank
    aways, token = hot_away(keep, mates[1:], token)
    aways = [swap(aways[c - 1], "dp", 2 * c) for c in range(1, peers // 2)]
    far_delta, token = cold_delta(ids, flat_cold_down, got, cap, rank, near, peers - near, token)
    far_back = [swap(far_delta[k - near], "dp", k) for k in range(near, peers)]
    (cold_down_grad,), token = cold_down_gradient(ids, got, xs, rank, cold_here, token)
    (local, place), token = local_terms(
        rows, flat_hot_down, got, near_back, peers - near, cap, rank, token
    )
    (hot_down_grad, hot_up_grad), token = hot_final(keep, mates[0], aways, width, height, token)
    (base_first, _), token = base(t, value_weight, local, dys[0], 0, (ids,), token)
    (base_last, passed), token = base(
        t, value_weight, local, dys[1], early, (in_part, in_next), token
    )
    ins = [passed] + [swap(passed, "tensor", k) for k in range(2, parts, 2)]
    (input_gradient,), token = final(place, (base_first, base_last), far_back, cap, token)
    (cold_up_grad,), token = cold_up_gradient(ids, ins, held_dy, rank, cold_here, token)
    return (
        input_gradient,
        cold_down_grad.reshape(cold_here, rank, width),
        cold_up_grad.reshape(cold_here, rank, kv),
        hot_down_grad.reshape(hot_here, rank, width),
        hot_up_grad.reshape(hot_here, rank, kv),
    )


def solution(mesh):
    in_specs = (
        P(("groups", "dp"), "tensor"),
        P(("groups", "dp"), "tensor"),
        P("tensor", None),
        P(("groups", "dp")),
        P("groups"),
        P(("groups", "dp"), None, "tensor"),
        P(("groups", "dp"), None, "tensor"),
        P("groups", None, "tensor"),
        P("groups", None, "tensor"),
    )
    out_specs = (
        P(("groups", "dp"), "tensor"),
        P(("groups", "dp"), None, "tensor"),
        P(("groups", "dp"), None, "tensor"),
        P(("groups", "dp"), None, "tensor"),
        P(("groups", "dp"), None, "tensor"),
    )
    return jax.shard_map(shards, mesh=mesh, in_specs=in_specs, out_specs=out_specs, check_vma=False)
```
